32 devices in a mesh: groups: 2 (over y), shard: 4 (over z), sub: 4 (over x, core).
Axes of the slice: x: 2, y: 2, z: 4, core: 2. Of those that a mesh axis runs over, the one named last changes fastest.
Arguments:
- points: bfloat16 [49152, 1024], P(('groups', 'shard', 'sub')), parts along dimension 0, may hold values from -6 to 6
- block_ids: int32 [384], P(('groups', 'shard', 'sub')), parts along dimension 0, may hold values from 0 to 3
- slot_ids: int32 [49152], P(('groups', 'shard', 'sub')), parts along dimension 0, may hold values from 0 to 127
- live_blocks: int32 [32], P(('groups', 'shard', 'sub')), parts along dimension 0, may hold values from 6 to 12, as said below
- old_centroids: bfloat16 [1024, 1024], P(('groups', 'shard'), 'sub'), parts along dimension 0, may hold values from -6 to 6
Outputs:
- new_centroids: bfloat16 [1024, 1024], P(('groups', 'shard'), 'sub'), parts along dimension 0
- margin: float32 [49152], P(('groups', 'shard', 'sub')), parts along dimension 0
The draws below stay inside these ranges and needn't reach their ends.
There are 2 independent parts, one for each index of `groups`. The reference program is written for one: setup_inputs(seed, part) draws one part's arguments, and reference() takes and returns one part's arrays. A program takes and returns all parts, laid end to end along the dimension named above; each array names one. Nothing has to cross between parts.
Inputs may be any that keep to these rules, and one draw needn't show every extreme that they name: `live_blocks`: some device holds 12 live blocks in every draw.
All inputs are finite; a program needn't handle non-finite values.
Results may differ from the reference program's by a relative error of at most 0.0026.
Values may be sent and summed in bfloat16 or wider, within the bound.
No kernel may reach another device: no remote copies, remote signals or barrier semaphores. Data moves between devices by JAX's collectives and lax.ppermute only.
A program may use at most 128 MiB of HBM per device.

```python
import math
import jax
import jax.numpy as jnp
import numpy as np
from jax import lax

D = 1024
SLOT = 128
BLK_DEV = 12
CENTROIDS = 512
ROWS_DEV = 1536
BLOCKS = 192
POINTS = 24576
N_SHARD = 4
N_SUB = 4


def draw_live_blocks(key, part):
    key = jax.random.fold_in(key, 7)
    first_key, second_key = jax.random.split(key)
    device_total = N_SHARD * N_SUB
    counts = jax.random.randint(first_key, (device_total,), max(BLK_DEV // 2, 1), BLK_DEV + 1)
    fullest = jax.random.randint(second_key, (), 0, device_total)
    return jnp.where(jnp.arange(device_total) == fullest, BLK_DEV, counts).astype(jnp.int32)


def plant(values, own_key, least, high):
    shape = values.shape
    index_at = [jax.random.randint(jax.random.fold_in(own_key, axis), (), 0, shape[axis]) for axis in range(len(shape))]
    values = values.at[tuple(index_at)].set(least)
    longest = shape.index(max(shape))
    index_at[longest] = (index_at[longest] + 1) % shape[longest]
    return values.at[tuple(index_at)].set(high)


def levels(stream_key, shape, cuts, least, top_value):
    level = 1.0
    for dim, parts in cuts:
        draws = jax.random.uniform(jax.random.fold_in(jax.random.fold_in(stream_key, 6), dim), (parts,), jnp.float32, least / len(cuts), top_value / len(cuts))
        level = level * jnp.repeat(jnp.exp(draws), shape[dim] // parts).reshape((-1,) + (1,) * (len(shape) - 1 - dim))
    return level


def cumulative_ranks(count, lean):
    portions = [(1 << 20) // math.isqrt(standing ** lean) + 1 for standing in range(1, count + 1)]
    scale = 1 + sum(portions) // (1 << 30)
    return np.cumsum(np.array([max(1, weight // scale) for weight in portions]))


def skewed_ids(rng, shape, count, skew):
    listing = cumulative_ranks(count, skew)
    lot = jax.random.randint(jax.random.fold_in(rng, 1), shape, 0, int(listing[count - 1]))
    standing = jnp.searchsorted(jnp.asarray(listing, jnp.int32), lot, side="right")
    return jax.random.permutation(jax.random.fold_in(rng, 2), count)[standing].astype(jnp.int32)


def normal_values(own_key, dims, scale, limit, cuts=(), kind=jnp.bfloat16):
    values = scale * jax.random.normal(own_key, dims, jnp.float32)
    if cuts:
        values = values * levels(own_key, dims, cuts, -0.22, 0.18)
    return jnp.clip(values, -limit, limit).astype(kind)


def setup_inputs(seed: int = 0, part: int = 0) -> dict:
    streams_of = jax.random.split(jax.random.key(seed), 6)
    part_splits = jax.random.split(jax.random.fold_in(streams_of[5], part), 6)
    points = normal_values(part_splits[0], (POINTS, D), 1.0, 6.0, ((0, 16),))
    block_ids = plant(skewed_ids(part_splits[1], (BLOCKS,), CENTROIDS // SLOT, 2), jax.random.fold_in(part_splits[1], 3), 0, (CENTROIDS // SLOT) - 1).astype(jnp.int32)
    slot_ids = plant(jax.random.randint(part_splits[2], (POINTS,), 0, SLOT), jax.random.fold_in(part_splits[2], 1), 0, SLOT - 1).astype(jnp.int32)
    live_blocks = draw_live_blocks(jax.random.fold_in(jax.random.fold_in(streams_of[5], part), 71), part)
    old_centroids = normal_values(part_splits[4], (CENTROIDS, D), 1.0, 6.0, ((0, 4), (1, 4)))
    return {"points": points, "block_ids": block_ids, "slot_ids": slot_ids, "live_blocks": live_blocks, "old_centroids": old_centroids}


prior_weight = 4.0
norm_eps = 1e-06

def reference(points, block_ids, slot_ids, live_blocks, old_centroids):
    block_count = points.shape[0] // SLOT
    point_blocks = points.reshape(block_count, SLOT, D)
    slot_table = slot_ids.reshape(block_count, SLOT)
    block_index = jnp.arange(block_count, dtype=jnp.int32)
    live_mask = block_index % BLK_DEV < live_blocks[block_index // BLK_DEV]
    cent_range = jnp.arange(SLOT, dtype=jnp.int32)

    def add_block(sums_acc, entries):
        point_rows, slot_row, block_id, alive = entries
        onehot_rows = ((slot_row[:, None] == cent_range[None, :]) & alive).astype(jnp.bfloat16)
        block_sum = jnp.dot(onehot_rows.T, point_rows, preferred_element_type=jnp.float32)
        first_row = (block_id * SLOT).astype(jnp.int32)
        current = lax.dynamic_slice_in_dim(sums_acc, first_row, SLOT, 0)
        return (lax.dynamic_update_slice_in_dim(sums_acc, current + block_sum, first_row, 0), None)
    sums, _ = lax.scan(add_block, jnp.zeros((CENTROIDS, D), jnp.float32), (point_blocks, slot_table, block_ids, live_mask))
    combined = sums + prior_weight * old_centroids.astype(jnp.float32)
    squares = lax.optimization_barrier(jnp.sum(combined * combined, axis=1, keepdims=True))
    new_centroids = (combined * lax.rsqrt(squares + norm_eps)).astype(jnp.bfloat16)
    own_ids = (block_ids[:, None] * SLOT + slot_table).reshape(-1).astype(jnp.int32)
    cent_index = jnp.arange(CENTROIDS, dtype=jnp.int32)

    def score_rows(entries):
        point_rows, own_row = entries
        score_block = jnp.dot(point_rows, new_centroids.T, preferred_element_type=jnp.float32)
        own_hit = own_row[:, None] == cent_index[None, :]
        own_score = lax.optimization_barrier(jnp.sum(jnp.where(own_hit, score_block, 0.0), axis=1))
        rival = lax.optimization_barrier(jnp.max(jnp.where(own_hit, -jnp.inf, score_block), axis=1))
        return own_score - rival
    margin = lax.map(score_rows, (points.reshape(-1, ROWS_DEV, D), own_ids.reshape(-1, ROWS_DEV)))
    return (new_centroids, margin.reshape(-1))
```

```python
import functools
import math

import jax
import jax.numpy as jnp
from jax import lax
from jax.experimental import pallas as pl
from jax.experimental.pallas import tpu as pltpu
from jax.sharding import PartitionSpec as P

SLOT = 128
POINT_LIMIT = 6.0

prior_weight = 4.0
norm_eps = 1e-06

LOW_EXP = -32
MIB = 1 << 20


def code_rate(top_exp):
    return 32767.0 / (top_exp - LOW_EXP)


def encode(value, rate):
    size = jnp.maximum(jnp.abs(value), 2.0**LOW_EXP)
    level = jnp.floor((jnp.log2(size) - LOW_EXP) * rate + 0.5)
    return jnp.where(value < 0.0, -level, level).astype(jnp.int32).astype(jnp.int16)


def decode(code, rate):
    level = code.astype(jnp.int32).astype(jnp.float32)
    size = jnp.exp2(jnp.abs(level) * (1.0 / rate) + LOW_EXP)
    return jnp.where(level == 0.0, 0.0, jnp.where(level < 0.0, -size, size))


def sums_kernel(place, bids, slots, points, send, keep, held, acc, arrived, *, blocks, shards, halves, rows, width):
    sub, shard, live = place[0], place[1], place[2]
    copies = []
    for block in range(blocks):
        span = pl.ds(block * SLOT, SLOT)
        copies.append(pltpu.make_async_copy(points.at[span], held.at[span], arrived.at[block]))
        copies[-1].start()
    acc[...] = jnp.zeros_like(acc)
    for block in range(blocks):
        copies[block].wait()

        @pl.when(block < live)
        def _(block=block):
            hot = slots[block : block + 1, :] == lax.broadcasted_iota(jnp.int32, (SLOT, SLOT), 0)
            part = jnp.dot(
                hot.astype(jnp.bfloat16),
                held[block * SLOT : (block + 1) * SLOT, :],
                preferred_element_type=jnp.float32,
            )
            first = pl.multiple_of(bids[block] * SLOT, SLOT)
            acc[pl.ds(first, SLOT), :] += part

    for half in range(halves):
        for step in range(shards):
            row = pl.ds(pl.multiple_of((shard ^ step) * rows, rows), rows)
            near = pl.multiple_of((sub ^ (2 * half)) * width, width)
            far = pl.multiple_of((sub ^ 1 ^ (2 * half)) * width, width)
            keep[half, step] = acc[row, pl.ds(near, width)]
            send[half, step] = acc[row, pl.ds(far, width)]


def score_kernel(
    place, bids, slots, own, points, *refs, blocks, shards, subs, rows, width, rate, group
):
    codes, (fresh, margin, cents) = refs[:subs], refs[subs:]
    sub, shard = place[0], place[1]
    def normalise(step, _):
        pieces = [decode(code[step], rate) for code in codes]
        squares = sum(jnp.sum(piece * piece, axis=1, keepdims=True) for piece in pieces)
        scale = lax.rsqrt(squares + norm_eps)
        row = pl.ds(pl.multiple_of(step * rows, rows), rows)
        for index, piece in enumerate(pieces):
            column = pl.ds(pl.multiple_of((sub ^ index) * width, width), width)
            cents[row, column] = (piece * scale).astype(jnp.bfloat16)

        @pl.when(step == 0)
        def _():
            fresh[...] = (own[...] * scale).astype(jnp.bfloat16)

        return 0

    lax.fori_loop(0, shards, normalise, 0)
    for block in range(blocks // group):
        score = lax.dot_general(
            cents[...],
            points[block * group * SLOT : (block + 1) * group * SLOT, :],
            (((1,), (1,)), ((), ())),
            preferred_element_type=jnp.float32,
        )
        for inner in range(group):
            at = block * group + inner
            part = score[:, inner * SLOT : (inner + 1) * SLOT]
            row = (bids[at] ^ shard) * SLOT + slots[at : at + 1, :]
            hit = lax.broadcasted_iota(jnp.int32, part.shape, 0) == row
            mine = jnp.sum(jnp.where(hit, part, 0.0), axis=0, keepdims=True)
            rival = jnp.max(jnp.where(hit, -jnp.inf, part), axis=0, keepdims=True)
            margin[at : at + 1, :] = mine - rival


def local(points, block_ids, slot_ids, live_blocks, old_centroids):
    row_count, feat_width = points.shape
    blocks = row_count // SLOT
    shards = lax.axis_size("shard")
    subs = lax.axis_size("sub")
    rows, width = old_centroids.shape
    total = rows * shards
    halves = subs // 2
    top = POINT_LIMIT * (row_count * shards * subs + prior_weight)
    rate = code_rate(math.ceil(math.log2(top)))
    place = jnp.stack([lax.axis_index("sub"), lax.axis_index("shard"), live_blocks[0]]).astype(jnp.int32)
    slots = slot_ids.reshape(blocks, SLOT)
    smem = pl.BlockSpec(memory_space=pltpu.SMEM)
    vmem = pl.BlockSpec(memory_space=pltpu.VMEM)
    hbm = pl.BlockSpec(memory_space=pltpu.HBM)

    def swap(value, axis, count, bits):
        return lax.ppermute(value, axis, [(i, i ^ bits) for i in range(count)])

    piece = jax.ShapeDtypeStruct((halves, shards, rows, width), jnp.float32)
    send, keep = pl.pallas_call(
        functools.partial(
            sums_kernel, blocks=blocks, shards=shards, halves=halves, rows=rows, width=width
        ),
        out_shape=(piece, piece),
        in_specs=[smem, smem, vmem, hbm],
        out_specs=(vmem, vmem),
        scratch_shapes=[
            pltpu.VMEM((row_count, feat_width), jnp.bfloat16),
            pltpu.VMEM((total, feat_width), jnp.float32),
            pltpu.SemaphoreType.DMA((blocks,)),
        ],
        compiler_params=pltpu.CompilerParams(vmem_limit_bytes=8 * MIB + 8 * total * feat_width),
        name="sums",
    )(place, block_ids, slots, points)

    mine = keep + swap(send, "sub", subs, 1)
    span = halves
    bits = 2
    while span > 1:
        split = mine.reshape((span // 2, 2) + mine.shape[1:])
        there = swap(encode(split[:, 1], rate), "sub", subs, bits)
        mine = split[:, 0] + decode(there, rate)
        span //= 2
        bits *= 2
    mine = mine[0]
    combined = mine[0] + prior_weight * old_centroids.astype(jnp.float32)
    for step in range(1, shards):
        there = swap(encode(mine[step], rate), "shard", shards, step)
        combined = combined + decode(there, rate)

    code = encode(combined, rate)
    gathered = [jnp.stack([code] + [swap(code, "shard", shards, step) for step in range(1, shards)])]
    bits = subs // 2
    held = {0: gathered[0]}
    while bits >= 1:
        for index in list(held):
            held[index ^ bits] = swap(held[index], "sub", subs, bits)
        bits //= 2

    group = 2 if blocks % 2 == 0 else 1
    fresh, margin = pl.pallas_call(
        functools.partial(
            score_kernel,
            blocks=blocks,
            shards=shards,
            subs=subs,
            rows=rows,
            width=width,
            rate=rate,
            group=group,
        ),
        out_shape=(
            jax.ShapeDtypeStruct((rows, width), jnp.bfloat16),
            jax.ShapeDtypeStruct((blocks, SLOT), jnp.float32),
        ),
        in_specs=[smem, smem, vmem, vmem, vmem] + [vmem] * subs,
        out_specs=(vmem, vmem),
        scratch_shapes=[
            pltpu.VMEM((total, feat_width), jnp.bfloat16),
        ],
        compiler_params=pltpu.CompilerParams(vmem_limit_bytes=12 * MIB + 6 * total * feat_width),
        name="scores",
    )(place, block_ids, slots, combined, points, *[held[index] for index in range(subs)])
    return fresh, margin.reshape(row_count)


def solution(mesh):
    return jax.shard_map(
        local,
        mesh=mesh,
        in_specs=(
            P(("groups", "shard", "sub"), None),
            P(("groups", "shard", "sub")),
            P(("groups", "shard", "sub")),
            P(("groups", "shard", "sub")),
            P(("groups", "shard"), "sub"),
        ),
        out_specs=(P(("groups", "shard"), "sub"), P(("groups", "shard", "sub"))),
        check_vma=False,
    )
```

```python
import functools
import math

import jax
import jax.numpy as jnp
from jax import lax
from jax.experimental import pallas as pl
from jax.experimental.pallas import tpu as pltpu
from jax.sharding import PartitionSpec as P

SLOT = 128
POINT_LIMIT = 6.0

prior_weight = 4.0
norm_eps = 1e-06

LOW_EXP = -32
MIB = 1 << 20


def code_rate(top_exp):
    return 32767.0 / (top_exp - LOW_EXP)


def encode(value, rate):
    size = jnp.maximum(jnp.abs(value), 2.0**LOW_EXP)
    level = jnp.floor((jnp.log2(size) - LOW_EXP) * rate + 0.5)
    return jnp.where(value < 0.0, -level, level).astype(jnp.int32).astype(jnp.int16)


def decode(code, rate):
    level = code.astype(jnp.int32).astype(jnp.float32)
    size = jnp.exp2(jnp.abs(level) * (1.0 / rate) + LOW_EXP)
    return jnp.where(level == 0.0, 0.0, jnp.where(level < 0.0, -size, size))


def sums_kernel(
    live, bids_in, slots_in, points, send, keep, bids, slots, held, acc, small, arrived,
    *, blocks, shards, halves, rows, width
):
    sub = lax.axis_index("sub")
    firsts = [
        pltpu.make_async_copy(bids_in, bids, small.at[0]),
        pltpu.make_async_copy(slots_in, slots, small.at[1]),
    ]
    for copy in firsts:
        copy.start()
    copies = []
    for block in range(blocks):
        span = pl.ds(block * SLOT, SLOT)
        copies.append(pltpu.make_async_copy(points.at[span], held.at[span], arrived.at[block]))
        copies[-1].start()
    acc[...] = jnp.zeros_like(acc)
    for copy in firsts:
        copy.wait()
    for block in range(blocks):
        copies[block].wait()

        @pl.when(block < live[0])
        def _(block=block):
            hot = slots[block : block + 1, :] == lax.broadcasted_iota(jnp.int32, (SLOT, SLOT), 0)
            part = jnp.dot(
                hot.astype(jnp.bfloat16),
                held[block * SLOT : (block + 1) * SLOT, :],
                preferred_element_type=jnp.float32,
            )
            first = pl.multiple_of(bids[block] * SLOT, SLOT)
            acc[pl.ds(first, SLOT), :] += part

    for half in range(halves):
        near = pl.multiple_of((sub ^ (2 * half)) * width, width)
        far = pl.multiple_of((sub ^ 1 ^ (2 * half)) * width, width)
        for step in range(shards):
            row = slice(step * rows, (step + 1) * rows)
            keep[half, step] = acc[row, pl.ds(near, width)]
            send[half, step] = acc[row, pl.ds(far, width)]


def score_kernel(
    bids, slots, own, points, *refs, blocks, shards, subs, rows, width, rate, group
):
    codes, (fresh, margin, cents) = refs[:subs], refs[subs:]
    sub, shard = lax.axis_index("sub"), lax.axis_index("shard")
    def normalise(step, _):
        pieces = [decode(code[step], rate) for code in codes]
        squares = sum(jnp.sum(piece * piece, axis=1, keepdims=True) for piece in pieces)
        scale = lax.rsqrt(squares + norm_eps)
        row = pl.ds(pl.multiple_of(step * rows, rows), rows)
        for index, piece in enumerate(pieces):
            column = pl.ds(pl.multiple_of((sub ^ index) * width, width), width)
            cents[row, column] = (piece * scale).astype(jnp.bfloat16)

        @pl.when(step == shard)
        def _():
            fresh[...] = (own[...] * scale).astype(jnp.bfloat16)

        return 0

    lax.fori_loop(0, shards, normalise, 0)
    for block in range(blocks // group):
        score = lax.dot_general(
            cents[...],
            points[block * group * SLOT : (block + 1) * group * SLOT, :],
            (((1,), (1,)), ((), ())),
            preferred_element_type=jnp.float32,
        )
        for inner in range(group):
            at = block * group + inner
            part = score[:, inner * SLOT : (inner + 1) * SLOT]
            row = bids[at] * SLOT + slots[at : at + 1, :]
            hit = lax.broadcasted_iota(jnp.int32, part.shape, 0) == row
            mine = jnp.sum(jnp.where(hit, part, 0.0), axis=0, keepdims=True)
            rival = jnp.max(jnp.where(hit, -jnp.inf, part), axis=0, keepdims=True)
            margin[at : at + 1, :] = mine - rival


def local(points, block_ids, slot_ids, live_blocks, old_centroids):
    row_count, feat_width = points.shape
    blocks = row_count // SLOT
    shards = lax.axis_size("shard")
    subs = lax.axis_size("sub")
    rows, width = old_centroids.shape
    total = rows * shards
    halves = subs // 2
    top = POINT_LIMIT * (row_count * shards * subs + prior_weight)
    rate = code_rate(math.ceil(math.log2(top)))
    slots = slot_ids.reshape(blocks, SLOT)
    smem = pl.BlockSpec(memory_space=pltpu.SMEM)
    vmem = pl.BlockSpec(memory_space=pltpu.VMEM)
    hbm = pl.BlockSpec(memory_space=pltpu.HBM)

    def swap(value, axis, count, bits):
        return lax.ppermute(value, axis, [(i, i ^ bits) for i in range(count)])

    piece = jax.ShapeDtypeStruct((halves, shards, rows, width), jnp.float32)
    send, keep = pl.pallas_call(
        functools.partial(
            sums_kernel, blocks=blocks, shards=shards, halves=halves, rows=rows, width=width
        ),
        out_shape=(piece, piece),
        in_specs=[smem, hbm, hbm, hbm],
        out_specs=(vmem, vmem),
        scratch_shapes=[
            pltpu.SMEM((blocks,), jnp.int32),
            pltpu.VMEM((blocks, SLOT), jnp.int32),
            pltpu.VMEM((row_count, feat_width), jnp.bfloat16),
            pltpu.VMEM((total, feat_width), jnp.float32),
            pltpu.SemaphoreType.DMA((2,)),
            pltpu.SemaphoreType.DMA((blocks,)),
        ],
        compiler_params=pltpu.CompilerParams(vmem_limit_bytes=8 * MIB + 8 * total * feat_width),
        name="sums",
    )(live_blocks, *[pltpu.with_memory_space_constraint(x, pltpu.HBM) for x in (block_ids, slots, points)])

    mine = keep + swap(send, "sub", subs, 1)
    span = halves
    bits = 2
    while span > 1:
        split = mine.reshape((span // 2, 2) + mine.shape[1:])
        there = swap(encode(split[:, 1], rate), "sub", subs, bits)
        mine = split[:, 0] + decode(there, rate)
        span //= 2
        bits *= 2
    there = lax.all_to_all(encode(mine[0], rate), "shard", split_axis=0, concat_axis=0, tiled=True)
    combined = jnp.sum(decode(there, rate), axis=0) + prior_weight * old_centroids.astype(jnp.float32)

    gathered = lax.all_gather(encode(combined, rate), "shard", axis=0)
    bits = subs // 2
    held = {0: gathered}
    while bits >= 1:
        for index in list(held):
            held[index ^ bits] = swap(held[index], "sub", subs, bits)
        bits //= 2

    group = 2 if blocks % 2 == 0 else 1
    fresh, margin = pl.pallas_call(
        functools.partial(
            score_kernel,
            blocks=blocks,
            shards=shards,
            subs=subs,
            rows=rows,
            width=width,
            rate=rate,
            group=group,
        ),
        out_shape=(
            jax.ShapeDtypeStruct((rows, width), jnp.bfloat16),
            jax.ShapeDtypeStruct((blocks, SLOT), jnp.float32),
        ),
        in_specs=[smem, vmem, vmem, vmem] + [vmem] * subs,
        out_specs=(vmem, vmem),
        scratch_shapes=[
            pltpu.VMEM((total, feat_width), jnp.bfloat16),
        ],
        compiler_params=pltpu.CompilerParams(vmem_limit_bytes=12 * MIB + 6 * total * feat_width),
        name="scores",
    )(block_ids, slots, combined, points, *[held[index] for index in range(subs)])
    return fresh, margin.reshape(row_count)


def solution(mesh):
    return jax.shard_map(
        local,
        mesh=mesh,
        in_specs=(
            P(("groups", "shard", "sub"), None),
            P(("groups", "shard", "sub")),
            P(("groups", "shard", "sub")),
            P(("groups", "shard", "sub")),
            P(("groups", "shard"), "sub"),
        ),
        out_specs=(P(("groups", "shard"), "sub"), P(("groups", "shard", "sub"))),
        check_vma=False,
    )
```

```python
import functools
import math

import jax
import jax.numpy as jnp
from jax import lax
from jax.experimental import pallas as pl
from jax.experimental.pallas import tpu as pltpu
from jax.sharding import PartitionSpec as P

SLOT = 128
POINT_LIMIT = 6.0

prior_weight = 4.0
norm_eps = 1e-06

LOW_EXP = -32
MIB = 1 << 20


def code_rate(top_exp):
    return 32767.0 / (top_exp - LOW_EXP)


def encode(value, rate):
    size = jnp.maximum(jnp.abs(value), 2.0**LOW_EXP)
    level = jnp.floor((jnp.log2(size) - LOW_EXP) * rate + 0.5)
    return jnp.where(value < 0.0, -level, level).astype(jnp.int32).astype(jnp.int16)


def decode(code, rate):
    level = code.astype(jnp.int32).astype(jnp.float32)
    size = jnp.exp2(jnp.abs(level) * (1.0 / rate) + LOW_EXP)
    return jnp.where(level == 0.0, 0.0, jnp.where(level < 0.0, -size, size))


def bits_of(count):
    return [1 << bit for bit in range(count.bit_length() - 1)]


def steps_of(subs, shards, half):
    subs_first = [("sub", bit) for bit in bits_of(subs)[1:]]
    shards_all = [("shard", bit) for bit in bits_of(shards)]
    if half == 0:
        return subs_first + shards_all
    return shards_all[:1] + subs_first + shards_all[1:]


def pieces_of(steps):
    pieces = [(0, 0)]
    for axis, bit in reversed(steps):
        far = [(sub ^ bit, shard) if axis == "sub" else (sub, shard ^ bit) for sub, shard in pieces]
        pieces = pieces + far
    return pieces


def sums_kernel(
    live, bids_in, slots_in, points, *refs, blocks, shards, subs, rows, width
):
    outs, (bids, slots, held, acc, small, arrived) = refs[:4], refs[4:]
    sub, shard = lax.axis_index("sub"), lax.axis_index("shard")
    firsts = [
        pltpu.make_async_copy(bids_in, bids, small.at[0]),
        pltpu.make_async_copy(slots_in, slots, small.at[1]),
    ]
    for copy in firsts:
        copy.start()
    copies = []
    for block in range(blocks):
        span = pl.ds(block * SLOT, SLOT)
        copies.append(pltpu.make_async_copy(points.at[span], held.at[span], arrived.at[block]))
        copies[-1].start()
    acc[...] = jnp.zeros_like(acc)
    for copy in firsts:
        copy.wait()
    for block in range(blocks):
        copies[block].wait()

        @pl.when(block < live[0])
        def _(block=block):
            hot = slots[block : block + 1, :] == lax.broadcasted_iota(jnp.int32, (SLOT, SLOT), 0)
            part = jnp.dot(
                hot.astype(jnp.bfloat16),
                held[block * SLOT : (block + 1) * SLOT, :],
                preferred_element_type=jnp.float32,
            )
            first = pl.multiple_of(bids[block] * SLOT, SLOT)
            acc[pl.ds(first, SLOT), :] += part

    half_rows = rows // 2
    for half in range(2):
        send, keep = outs[2 * half : 2 * half + 2]
        for index, (over_sub, over_shard) in enumerate(pieces_of(steps_of(subs, shards, half))):
            row = pl.ds(pl.multiple_of((shard ^ over_shard) * rows + half * half_rows, half_rows), half_rows)
            near = pl.multiple_of((sub ^ over_sub) * width, width)
            far = pl.multiple_of((sub ^ 1 ^ over_sub) * width, width)
            keep[index] = acc[row, pl.ds(near, width)]
            send[index] = acc[row, pl.ds(far, width)]


def score_kernel(
    bids, slots, own, points, near, far, *refs, half, blocks, shards, subs, rows, width, rate, group
):
    if half:
        (mine_in, rival_in, fresh_in), (fresh, margin, cents) = refs[:3], refs[3:]
    else:
        fresh, mine_out, rival_out, cents = refs
    sub, shard = lax.axis_index("sub"), lax.axis_index("shard")
    half_rows = rows // 2
    pieces = pieces_of(steps_of(subs, shards, half))
    for over_shard in range(shards):
        parts = []
        for index, (over_sub, piece_shard) in enumerate(pieces):
            if piece_shard == over_shard:
                parts.append((sub ^ over_sub, decode(near[index], rate)))
                parts.append((sub ^ 1 ^ over_sub, decode(far[index], rate)))
        squares = sum(jnp.sum(part * part, axis=1, keepdims=True) for _, part in parts)
        scale = lax.rsqrt(squares + norm_eps)
        row = pl.ds(pl.multiple_of((shard ^ over_shard) * half_rows, half_rows), half_rows)
        for place, part in parts:
            cents[row, pl.ds(pl.multiple_of(place * width, width), width)] = (part * scale).astype(jnp.bfloat16)
        if over_shard == 0:
            updated = (own[...] * scale).astype(jnp.bfloat16)
            if half:
                fresh[:half_rows] = fresh_in[...]
                fresh[half_rows:] = updated
            else:
                fresh[...] = updated

    for block in range(blocks // group):
        score = lax.dot_general(
            cents[...],
            points[block * group * SLOT : (block + 1) * group * SLOT, :],
            (((1,), (1,)), ((), ())),
            preferred_element_type=jnp.float32,
        )
        for inner in range(group):
            at = block * group + inner
            line = slice(at, at + 1)
            part = score[:, inner * SLOT : (inner + 1) * SLOT]
            slot = slots[line, :] - half * half_rows
            row = jnp.where((slot >= 0) & (slot < half_rows), bids[at] * half_rows + slot, -1)
            hit = lax.broadcasted_iota(jnp.int32, part.shape, 0) == row
            mine = jnp.sum(jnp.where(hit, part, 0.0), axis=0, keepdims=True)
            rival = jnp.max(jnp.where(hit, -jnp.inf, part), axis=0, keepdims=True)
            if half:
                margin[line, :] = (mine_in[line, :] + mine) - jnp.maximum(rival_in[line, :], rival)
            else:
                mine_out[line, :] = mine
                rival_out[line, :] = rival


def local(points, block_ids, slot_ids, live_blocks, old_centroids):
    row_count, feat_width = points.shape
    blocks = row_count // SLOT
    shards = lax.axis_size("shard")
    subs = lax.axis_size("sub")
    counts = {"sub": subs, "shard": shards}
    rows, width = old_centroids.shape
    half_rows = rows // 2
    total = rows * shards
    top = POINT_LIMIT * (row_count * shards * subs + prior_weight)
    rate = code_rate(math.ceil(math.log2(top)))
    slots = slot_ids.reshape(blocks, SLOT)
    smem = pl.BlockSpec(memory_space=pltpu.SMEM)
    vmem = pl.BlockSpec(memory_space=pltpu.VMEM)
    hbm = pl.BlockSpec(memory_space=pltpu.HBM)

    def swap(value, axis, bit):
        return lax.ppermute(value, axis, [(i, i ^ bit) for i in range(counts[axis])])

    piece = jax.ShapeDtypeStruct((shards * subs // 2, half_rows, width), jnp.float32)
    sums = pl.pallas_call(
        functools.partial(sums_kernel, blocks=blocks, shards=shards, subs=subs, rows=rows, width=width),
        out_shape=(piece,) * 4,
        in_specs=[smem, hbm, hbm, hbm],
        out_specs=(vmem,) * 4,
        scratch_shapes=[
            pltpu.SMEM((blocks,), jnp.int32),
            pltpu.VMEM((blocks, SLOT), jnp.int32),
            pltpu.VMEM((row_count, feat_width), jnp.bfloat16),
            pltpu.VMEM((total, feat_width), jnp.float32),
            pltpu.SemaphoreType.DMA((2,)),
            pltpu.SemaphoreType.DMA((blocks,)),
        ],
        compiler_params=pltpu.CompilerParams(vmem_limit_bytes=8 * MIB + 8 * total * feat_width),
        name="sums",
    )(live_blocks, *[pltpu.with_memory_space_constraint(x, pltpu.HBM) for x in (block_ids, slots, points)])

    steps = [steps_of(subs, shards, half) for half in range(2)]
    prior = prior_weight * old_centroids.astype(jnp.float32)
    crossed = [swap(sums[2 * half], "sub", 1) for half in range(2)]
    mine = [sums[2 * half + 1] + crossed[half] for half in range(2)]
    for turn in range(len(steps[0]) - 1):
        for half in range(2):
            axis, bit = steps[half][turn]
            count = mine[half].shape[0] // 2
            there = swap(encode(mine[half][count:], rate), axis, bit)
            mine[half] = mine[half][:count] + decode(there, rate)
    codes = []
    owned = []
    for half in range(2):
        axis, bit = steps[half][-1]
        with_prior = mine[half][0] + prior[half * half_rows : (half + 1) * half_rows]
        pair = jnp.stack([with_prior, mine[half][1]])
        there = decode(swap(encode(pair, rate), axis, bit), rate)
        owned.append(with_prior + there[1])
        codes.append(encode(jnp.stack([owned[half], mine[half][1] + there[0]]), rate))
    for turn in reversed(range(len(steps[0]) - 1)):
        for half in range(2):
            axis, bit = steps[half][turn]
            codes[half] = jnp.concatenate([codes[half], swap(codes[half], axis, bit)])
    others = [swap(codes[half], "sub", 1) for half in range(2)]

    group = 2 if blocks % 2 == 0 else 1

    def scores(half, earlier):
        line = jax.ShapeDtypeStruct((blocks, SLOT), jnp.float32)
        fresh = jax.ShapeDtypeStruct((rows if half else half_rows, width), jnp.bfloat16)
        return pl.pallas_call(
            functools.partial(
                score_kernel,
                half=half,
                blocks=blocks,
                shards=shards,
                subs=subs,
                rows=rows,
                width=width,
                rate=rate,
                group=group,
            ),
            out_shape=(fresh, line) if half else (fresh, line, line),
            in_specs=[smem] + [vmem] * (5 + len(earlier)),
            out_specs=(vmem,) * (2 if half else 3),
            scratch_shapes=[pltpu.VMEM((total // 2, feat_width), jnp.bfloat16)],
            compiler_params=pltpu.CompilerParams(vmem_limit_bytes=12 * MIB + 6 * total * feat_width),
            cost_estimate=pl.CostEstimate(
                flops=row_count * total * feat_width,
                bytes_accessed=2 * row_count * feat_width,
                transcendentals=total * feat_width // 2,
            ),
            name=f"scores{half}",
        )(block_ids, slots, owned[half], points, codes[half], others[half], *earlier)

    fresh, own_score, rival = scores(0, ())
    fresh, margin = scores(1, (own_score, rival, fresh))
    return fresh, margin.reshape(row_count)


def solution(mesh):
    return jax.shard_map(
        local,
        mesh=mesh,
        in_specs=(
            P(("groups", "shard", "sub"), None),
            P(("groups", "shard", "sub")),
            P(("groups", "shard", "sub")),
            P(("groups", "shard", "sub")),
            P(("groups", "shard"), "sub"),
        ),
        out_specs=(P(("groups", "shard"), "sub"), P(("groups", "shard", "sub"))),
        check_vma=False,
    )
```

```python
import functools
import math

import jax
import jax.numpy as jnp
from jax import lax
from jax.experimental import pallas as pl
from jax.experimental.pallas import tpu as pltpu
from jax.sharding import PartitionSpec as P

SLOT = 128
POINT_LIMIT = 6.0

prior_weight = 4.0
norm_eps = 1e-06

LOW_EXP = -32
MIB = 1 << 20


def code_rate(top_exp):
    return 32767.0 / (top_exp - LOW_EXP)


def encode(value, rate):
    size = jnp.maximum(jnp.abs(value), 2.0**LOW_EXP)
    level = jnp.floor((jnp.log2(size) - LOW_EXP) * rate + 0.5)
    return jnp.where(value < 0.0, -level, level).astype(jnp.int32).astype(jnp.int16)


def decode(code, rate):
    level = code.astype(jnp.int32).astype(jnp.float32)
    size = jnp.exp2(jnp.abs(level) * (1.0 / rate) + LOW_EXP)
    return jnp.where(level == 0.0, 0.0, jnp.where(level < 0.0, -size, size))


def bits_of(count):
    return [1 << bit for bit in range(count.bit_length() - 1)]


def steps_of(subs, shards, side):
    subs_rest = [("sub", bit) for bit in bits_of(subs)[1:]]
    shards_all = [("shard", bit) for bit in bits_of(shards)]
    if side == 0:
        return subs_rest + shards_all
    return shards_all[:1] + subs_rest + shards_all[1:]


def piece_at(steps, over_sub, over_shard):
    place = 0
    for axis, bit in steps:
        over = over_sub if axis == "sub" else over_shard
        place = place * 2 + (over // bit) % 2
    return place


def sided(side, subs, shards, over_sub, over_shard):
    places = [piece_at(steps_of(subs, shards, s), over_sub, over_shard) for s in range(2)]
    return jnp.where(side == 0, places[0], places[1])


def sums_kernel(
    live_in, bids_in, slots_in, old_in, points, keep, send, live, bids, slots, old, held, small, arrived,
    *, blocks, shards, subs, width
):
    sub, shard = lax.axis_index("sub"), lax.axis_index("shard")
    side = sub % 2
    firsts = [
        pltpu.make_async_copy(here, there, small.at[index])
        for index, (here, there) in enumerate(
            [(live_in, live), (bids_in, bids), (slots_in, slots), (old_in, old)]
        )
    ]
    for copy in firsts:
        copy.start()
    copies = []
    for block in range(blocks):
        span = pl.ds(block * SLOT, SLOT)
        copies.append(pltpu.make_async_copy(points.at[span], held.at[span], arrived.at[block]))
        copies[-1].start()
    keep[...] = jnp.zeros_like(keep)
    send[...] = jnp.zeros_like(send)
    for copy in firsts:
        copy.wait()
    keep[0] = prior_weight * old[...].astype(jnp.float32)
    for block in range(blocks):
        copies[block].wait()

        @pl.when(block < live[0])
        def _(block=block):
            hot = slots[block : block + 1, :] == lax.broadcasted_iota(jnp.int32, (SLOT, SLOT), 0)
            hot = hot.astype(jnp.bfloat16)
            over_shard = bids[block] ^ shard
            for over_sub in range(0, subs, 2):
                for sums, flip in ((keep, 0), (send, 1)):
                    place = sided(side ^ flip, subs, shards, over_sub, over_shard)
                    column = pl.multiple_of((sub ^ over_sub ^ flip) * width, width)
                    sums[place] += jnp.dot(
                        hot,
                        held[block * SLOT : (block + 1) * SLOT, pl.ds(column, width)],
                        preferred_element_type=jnp.float32,
                    )


def pair_kernel(*refs, rate):
    terms, (mine, code) = refs[:-2], refs[-2:]
    total = terms[0][...] + terms[1][...]
    for term in terms[2:]:
        total = total + decode(term[...], rate)
    mine[...] = total
    code[...] = encode(total, rate)


def finish_kernel(mine, there, own, code, *, rate):
    own[...] = mine[0] + decode(there[1], rate)
    code[0] = encode(own[...], rate)
    code[1] = encode(mine[1] + decode(there[0], rate), rate)


def score_kernel(
    bids, slots, own, points, near, far, fresh, margin, cents, *, blocks, shards, subs, rows, width, rate, group
):
    sub, shard = lax.axis_index("sub"), lax.axis_index("shard")
    side = sub % 2
    for over_shard in range(shards):
        parts = []
        for over_sub in range(0, subs, 2):
            parts.append((sub ^ over_sub, decode(near[sided(side, subs, shards, over_sub, over_shard)], rate)))
            parts.append((sub ^ 1 ^ over_sub, decode(far[sided(1 - side, subs, shards, over_sub, over_shard)], rate)))
        squares = sum(jnp.sum(part * part, axis=1, keepdims=True) for _, part in parts)
        scale = lax.rsqrt(squares + norm_eps)
        row = pl.ds(pl.multiple_of((shard ^ over_shard) * rows, rows), rows)
        for place, part in parts:
            cents[row, pl.ds(pl.multiple_of(place * width, width), width)] = (part * scale).astype(jnp.bfloat16)
        if over_shard == 0:
            fresh[...] = (own[...] * scale).astype(jnp.bfloat16)

    for block in range(blocks // group):
        score = lax.dot_general(
            cents[...],
            points[block * group * SLOT : (block + 1) * group * SLOT, :],
            (((1,), (1,)), ((), ())),
            preferred_element_type=jnp.float32,
        )
        for inner in range(group):
            at = block * group + inner
            line = slice(at, at + 1)
            part = score[:, inner * SLOT : (inner + 1) * SLOT]
            hit = lax.broadcasted_iota(jnp.int32, part.shape, 0) == bids[at] * SLOT + slots[line, :]
            mine = jnp.sum(jnp.where(hit, part, 0.0), axis=0, keepdims=True)
            rival = jnp.max(jnp.where(hit, -jnp.inf, part), axis=0, keepdims=True)
            margin[line, :] = mine - rival


def local(points, block_ids, slot_ids, live_blocks, old_centroids):
    row_count, feat_width = points.shape
    blocks = row_count // SLOT
    shards = lax.axis_size("shard")
    subs = lax.axis_size("sub")
    rows, width = old_centroids.shape
    total = rows * shards
    top = POINT_LIMIT * (row_count * shards * subs + prior_weight)
    rate = code_rate(math.ceil(math.log2(top)))
    slots = slot_ids.reshape(blocks, SLOT)
    steps = [steps_of(subs, shards, side) for side in range(2)]
    pieces = 1 << len(steps[0])
    smem = pl.BlockSpec(memory_space=pltpu.SMEM)
    vmem = pl.BlockSpec(memory_space=pltpu.VMEM)
    hbm = pl.BlockSpec(memory_space=pltpu.HBM)

    def swap(value, turn):
        pairs = []
        for shard in range(shards):
            for sub in range(subs):
                axis, bit = steps[sub % 2][turn] if turn >= 0 else ("sub", 1)
                there = (shard ^ bit, sub) if axis == "shard" else (shard, sub ^ bit)
                pairs.append((shard * subs + sub, there[0] * subs + there[1]))
        return lax.ppermute(value, ("shard", "sub"), pairs)

    def in_hbm(value):
        return pltpu.with_memory_space_constraint(value, pltpu.HBM)

    piece = jax.ShapeDtypeStruct((pieces, rows, width), jnp.float32)
    keep, send = pl.pallas_call(
        functools.partial(sums_kernel, blocks=blocks, shards=shards, subs=subs, width=width),
        out_shape=(piece, piece),
        in_specs=[hbm] * 5,
        out_specs=(vmem, vmem),
        scratch_shapes=[
            pltpu.SMEM((1,), jnp.int32),
            pltpu.SMEM((blocks,), jnp.int32),
            pltpu.VMEM((blocks, SLOT), jnp.int32),
            pltpu.VMEM((rows, width), jnp.bfloat16),
            pltpu.VMEM((row_count, feat_width), jnp.bfloat16),
            pltpu.SemaphoreType.DMA((4,)),
            pltpu.SemaphoreType.DMA((blocks,)),
        ],
        compiler_params=pltpu.CompilerParams(vmem_limit_bytes=8 * MIB + 4 * total * feat_width),
        name="sums",
    )(live_blocks, in_hbm(block_ids), in_hbm(slots), in_hbm(old_centroids), in_hbm(points))

    terms = [keep, swap(send, -1)]

    def so_far(first, end):
        value = terms[0][first:end] + terms[1][first:end]
        for term in terms[2:]:
            value = value + decode(term[first:end], rate)
        return value

    count = pieces
    for turn in range(len(steps[0]) - 1):
        count //= 2
        terms.append(swap(encode(so_far(count, 2 * count), rate), turn))

    two = (2, rows, width)
    first_two = pl.BlockSpec(two, lambda step: (0, 0, 0))
    mine, code = pl.pallas_call(
        functools.partial(pair_kernel, rate=rate),
        grid=(1,),
        out_shape=(jax.ShapeDtypeStruct(two, jnp.float32), jax.ShapeDtypeStruct(two, jnp.int16)),
        in_specs=[first_two] * len(terms),
        out_specs=(first_two, first_two),
        name="pair",
    )(*terms)
    own, code = pl.pallas_call(
        functools.partial(finish_kernel, rate=rate),
        out_shape=(jax.ShapeDtypeStruct((rows, width), jnp.float32), jax.ShapeDtypeStruct(two, jnp.int16)),
        name="finish",
    )(mine, swap(code, len(steps[0]) - 1))

    near = code
    for turn in reversed(range(1, len(steps[0]) - 1)):
        near = jnp.concatenate([near, swap(near, turn)])
    last = swap(near, 0)
    far = jnp.concatenate([swap(near, -1), swap(last, -1)])
    near = jnp.concatenate([near, last])

    group = 2 if blocks % 2 == 0 else 1
    fresh, margin = pl.pallas_call(
        functools.partial(
            score_kernel, blocks=blocks, shards=shards, subs=subs, rows=rows, width=width, rate=rate, group=group
        ),
        out_shape=(
            jax.ShapeDtypeStruct((rows, width), jnp.bfloat16),
            jax.ShapeDtypeStruct((blocks, SLOT), jnp.float32),
        ),
        in_specs=[smem] + [vmem] * 5,
        out_specs=(vmem, vmem),
        scratch_shapes=[pltpu.VMEM((total, feat_width), jnp.bfloat16)],
        compiler_params=pltpu.CompilerParams(vmem_limit_bytes=12 * MIB + 6 * total * feat_width),
        name="scores",
    )(block_ids, slots, own, points, near, far)
    return fresh, margin.reshape(row_count)


def solution(mesh):
    return jax.shard_map(
        local,
        mesh=mesh,
        in_specs=(
            P(("groups", "shard", "sub"), None),
            P(("groups", "shard", "sub")),
            P(("groups", "shard", "sub")),
            P(("groups", "shard", "sub")),
            P(("groups", "shard"), "sub"),
        ),
        out_specs=(P(("groups", "shard"), "sub"), P(("groups", "shard", "sub"))),
        check_vma=False,
    )
```

```python
import functools
import math

import jax
import jax.numpy as jnp
from jax import lax
from jax.experimental import pallas as pl
from jax.experimental.pallas import tpu as pltpu
from jax.sharding import PartitionSpec as P

SLOT = 128
POINT_LIMIT = 6.0

prior_weight = 4.0
norm_eps = 1e-06

LOW_EXP = -32
MIB = 1 << 20


def code_rate(top_exp):
    return 32767.0 / (top_exp - LOW_EXP)


def encode(value, rate):
    size = jnp.maximum(jnp.abs(value), 2.0**LOW_EXP)
    level = jnp.floor((jnp.log2(size) - LOW_EXP) * rate + 0.5)
    return jnp.where(value < 0.0, -level, level).astype(jnp.int32).astype(jnp.int16)


def decode(code, rate):
    level = code.astype(jnp.int32).astype(jnp.float32)
    size = jnp.exp2(jnp.abs(level) * (1.0 / rate) + LOW_EXP)
    return jnp.where(level == 0.0, 0.0, jnp.where(level < 0.0, -size, size))


def bits_of(count):
    return [1 << bit for bit in range(count.bit_length() - 1)]


def near_group(subs, shards):
    group = [(0, 0)]
    for bit in bits_of(subs)[1:]:
        group = group + [(sub ^ bit, shard) for sub, shard in group]
    group = group + [(sub, shard ^ 1) for sub, shard in group]
    return group[:1] + group[:0:-1]


def late_bits(shards):
    return bits_of(shards)[1:]


def late_place(bits, over_shard):
    place = 0
    for bit in bits:
        place = place * 2 + (over_shard // bit) % 2
    return place


def sums_kernel(
    live_in, bids_in, slots_in, points, *refs, blocks, shards, subs, width, flip, owned
):
    if owned:
        old_in, sums, live, bids, slots, held, small, arrived, old = refs
    else:
        sums, live, bids, slots, held, small, arrived = refs
    sub, shard = lax.axis_index("sub"), lax.axis_index("shard")
    width_all = (subs // 2) * width
    firsts = [
        pltpu.make_async_copy(live_in, live, small.at[0]),
        pltpu.make_async_copy(bids_in, bids, small.at[1]),
        pltpu.make_async_copy(slots_in, slots, small.at[2]),
    ]
    if owned:
        firsts.append(pltpu.make_async_copy(old_in, old, small.at[3]))
    for copy in firsts:
        copy.start()
    copies = []
    for block in range(blocks):
        span = pl.ds(block * SLOT, SLOT)
        for index, over_sub in enumerate(range(0, subs, 2)):
            column = pl.multiple_of((sub ^ over_sub ^ flip) * width, width)
            copies.append(
                pltpu.make_async_copy(
                    points.at[span, pl.ds(column, width)],
                    held.at[span, pl.ds(index * width, width)],
                    arrived.at[block * (subs // 2) + index],
                )
            )
            copies[-1].start()
    sums[...] = jnp.zeros_like(sums)
    for copy in firsts:
        copy.wait()
    if owned:
        sums[0, 0] = prior_weight * old[...].astype(jnp.float32)
    group = near_group(subs, shards)
    bits = late_bits(shards)
    for block in range(blocks):
        slot = jnp.where(block < live[0], slots[block : block + 1, :], -1)
        hot = (slot == lax.broadcasted_iota(jnp.int32, (SLOT, SLOT), 0)).astype(jnp.bfloat16)
        over_shard = bids[block] ^ shard
        late = late_place(bits, over_shard)
        for index, over_sub in enumerate(range(0, subs, 2)):
            copies[block * (subs // 2) + index].wait()
            part = jnp.dot(
                hot,
                held[block * SLOT : (block + 1) * SLOT, index * width : (index + 1) * width],
                preferred_element_type=jnp.float32,
            )
            at = jnp.where(over_shard % 2 == 0, group.index((over_sub, 0)), group.index((over_sub, 1)))
            sums[at, late] += part


def mix_kernel(keep, crossed, *refs, rate):
    terms, (mine, code) = refs[:-2], refs[-2:]
    total = keep[0] + crossed[0]
    for term in terms:
        total = total + decode(term[...], rate)
    mine[...] = total
    code[...] = encode(total, rate)


def finish_kernel(mine, there, own, code, *, rate):
    own[...] = mine[0] + decode(there[1], rate)
    code[0] = encode(own[...], rate)
    code[1] = encode(mine[1] + decode(there[0], rate), rate)


def score_kernel(
    bids, slots, own, points, *refs, blocks, shards, subs, rows, width, rate, group
):
    chips = near_group(subs, shards)
    near, far, (fresh, margin, cents) = refs[: len(chips)], refs[len(chips) : 2 * len(chips)], refs[2 * len(chips) :]
    sub, shard = lax.axis_index("sub"), lax.axis_index("shard")
    bits = late_bits(shards)
    for over_shard in range(shards):
        late = late_place(bits, over_shard)
        parts = []
        for over_sub in range(0, subs, 2):
            chip = chips.index((over_sub, over_shard % 2))
            parts.append((sub ^ over_sub, decode(near[chip][late], rate)))
            parts.append((sub ^ 1 ^ over_sub, decode(far[chip][late], rate)))
        squares = sum(jnp.sum(part * part, axis=1, keepdims=True) for _, part in parts)
        scale = lax.rsqrt(squares + norm_eps)
        row = pl.ds(pl.multiple_of((shard ^ over_shard) * rows, rows), rows)
        for place, part in parts:
            cents[row, pl.ds(pl.multiple_of(place * width, width), width)] = (part * scale).astype(jnp.bfloat16)
        if over_shard == 0:
            fresh[...] = (own[...] * scale).astype(jnp.bfloat16)

    for block in range(blocks // group):
        score = lax.dot_general(
            cents[...],
            points[block * group * SLOT : (block + 1) * group * SLOT, :],
            (((1,), (1,)), ((), ())),
            preferred_element_type=jnp.float32,
        )
        for inner in range(group):
            at = block * group + inner
            line = slice(at, at + 1)
            part = score[:, inner * SLOT : (inner + 1) * SLOT]
            hit = lax.broadcasted_iota(jnp.int32, part.shape, 0) == bids[at] * SLOT + slots[line, :]
            mine = jnp.sum(jnp.where(hit, part, 0.0), axis=0, keepdims=True)
            rival = jnp.max(jnp.where(hit, -jnp.inf, part), axis=0, keepdims=True)
            margin[line, :] = mine - rival


def local(points, block_ids, slot_ids, live_blocks, old_centroids):
    row_count, feat_width = points.shape
    blocks = row_count // SLOT
    shards = lax.axis_size("shard")
    subs = lax.axis_size("sub")
    rows, width = old_centroids.shape
    total = rows * shards
    top = POINT_LIMIT * (row_count * shards * subs + prior_weight)
    rate = code_rate(math.ceil(math.log2(top)))
    slots = slot_ids.reshape(blocks, SLOT)
    chips = near_group(subs, shards)
    bits = late_bits(shards)
    late = 1 << len(bits)
    small_limit = 4 * MIB + 8 * total * feat_width
    smem = pl.BlockSpec(memory_space=pltpu.SMEM)
    vmem = pl.BlockSpec(memory_space=pltpu.VMEM)
    hbm = pl.BlockSpec(memory_space=pltpu.HBM)

    def swap(value, over_sub, over_shard):
        pairs = []
        for shard in range(shards):
            for sub in range(subs):
                pairs.append((shard * subs + sub, (shard ^ over_shard) * subs + (sub ^ over_sub)))
        return lax.ppermute(value, ("shard", "sub"), pairs)

    def in_hbm(value):
        return pltpu.with_memory_space_constraint(value, pltpu.HBM)

    def sums(flip, *owned):
        return pl.pallas_call(
            functools.partial(
                sums_kernel, blocks=blocks, shards=shards, subs=subs, width=width, flip=flip, owned=bool(owned)
            ),
            out_shape=jax.ShapeDtypeStruct((len(chips), late, rows, width), jnp.float32),
            in_specs=[hbm] * (4 + len(owned)),
            out_specs=vmem,
            scratch_shapes=[
                pltpu.SMEM((1,), jnp.int32),
                pltpu.SMEM((blocks,), jnp.int32),
                pltpu.VMEM((blocks, SLOT), jnp.int32),
                pltpu.VMEM((row_count, feat_width // 2), jnp.bfloat16),
                pltpu.SemaphoreType.DMA((4,)),
                pltpu.SemaphoreType.DMA((blocks * subs // 2,)),
            ]
            + [pltpu.VMEM((rows, width), jnp.bfloat16)] * len(owned),
            compiler_params=pltpu.CompilerParams(vmem_limit_bytes=8 * MIB + 2 * total * feat_width),
            cost_estimate=pl.CostEstimate(
                flops=row_count * SLOT * feat_width,
                bytes_accessed=row_count * feat_width,
                transcendentals=0,
            ),
            name="sums_keep" if owned else "sums_send",
        )(live_blocks, in_hbm(block_ids), in_hbm(slots), in_hbm(points), *[in_hbm(x) for x in owned])

    crossed = swap(sums(1), 1, 0)
    keep = sums(0, old_centroids)
    terms = []
    for index, (over_sub, over_shard) in list(enumerate(chips))[1:]:
        terms.append(swap(encode(keep[index] + crossed[index], rate), over_sub, over_shard))

    piece = (late, rows, width)
    mine, code = pl.pallas_call(
        functools.partial(mix_kernel, rate=rate),
        out_shape=(jax.ShapeDtypeStruct(piece, jnp.float32), jax.ShapeDtypeStruct(piece, jnp.int16)),
        compiler_params=pltpu.CompilerParams(vmem_limit_bytes=small_limit),
        name="mix",
    )(keep, crossed, *terms)
    for bit in bits[:-1]:
        half = mine.shape[0] // 2
        mine = mine[:half] + decode(swap(encode(mine[half:], rate), 0, bit), rate)
        code = encode(mine, rate)
    two = (2, rows, width)
    own, code = pl.pallas_call(
        functools.partial(finish_kernel, rate=rate),
        out_shape=(jax.ShapeDtypeStruct((rows, width), jnp.float32), jax.ShapeDtypeStruct(two, jnp.int16)),
        compiler_params=pltpu.CompilerParams(vmem_limit_bytes=small_limit),
        name="finish",
    )(mine, swap(code, 0, bits[-1]))
    for bit in reversed(bits[:-1]):
        code = jnp.concatenate([code, swap(code, 0, bit)])
    near = [code] + [swap(code, over_sub, over_shard) for over_sub, over_shard in chips[1:]]
    far = [swap(block, 1, 0) for block in near]

    group = 2 if blocks % 2 == 0 else 1
    fresh, margin = pl.pallas_call(
        functools.partial(
            score_kernel, blocks=blocks, shards=shards, subs=subs, rows=rows, width=width, rate=rate, group=group
        ),
        out_shape=(
            jax.ShapeDtypeStruct((rows, width), jnp.bfloat16),
            jax.ShapeDtypeStruct((blocks, SLOT), jnp.float32),
        ),
        in_specs=[smem] + [vmem] * (3 + 2 * len(chips)),
        out_specs=(vmem, vmem),
        scratch_shapes=[pltpu.VMEM((total, feat_width), jnp.bfloat16)],
        compiler_params=pltpu.CompilerParams(vmem_limit_bytes=12 * MIB + 6 * total * feat_width),
        name="scores",
    )(block_ids, slots, own, points, *near, *far)
    return fresh, margin.reshape(row_count)


def solution(mesh):
    return jax.shard_map(
        local,
        mesh=mesh,
        in_specs=(
            P(("groups", "shard", "sub"), None),
            P(("groups", "shard", "sub")),
            P(("groups", "shard", "sub")),
            P(("groups", "shard", "sub")),
            P(("groups", "shard"), "sub"),
        ),
        out_specs=(P(("groups", "shard"), "sub"), P(("groups", "shard", "sub"))),
        check_vma=False,
    )
```

```python
import functools
import math

import jax
import jax.numpy as jnp
from jax import lax
from jax.experimental import pallas as pl
from jax.experimental.pallas import tpu as pltpu
from jax.sharding import PartitionSpec as P

SLOT = 128
POINT_LIMIT = 6.0

prior_weight = 4.0
norm_eps = 1e-06

LOW_EXP = -32
MIB = 1 << 20


def code_rate(top_exp):
    return 32767.0 / (top_exp - LOW_EXP)


def encode(value, rate):
    size = jnp.maximum(jnp.abs(value), 2.0**LOW_EXP)
    level = jnp.floor((jnp.log2(size) - LOW_EXP) * rate + 0.5)
    return jnp.where(value < 0.0, -level, level).astype(jnp.int32).astype(jnp.int16)


def decode(code, rate):
    level = code.astype(jnp.int32).astype(jnp.float32)
    size = jnp.exp2(jnp.abs(level) * (1.0 / rate) + LOW_EXP)
    return jnp.where(level == 0.0, 0.0, jnp.where(level < 0.0, -size, size))


def bits_of(count):
    return [1 << bit for bit in range(count.bit_length() - 1)]


def near_group(subs, shards):
    group = [(0, 0)]
    for bit in bits_of(subs)[1:]:
        group = group + [(sub ^ bit, shard) for sub, shard in group]
    group = group + [(sub, shard ^ 1) for sub, shard in group]
    return group[:1] + group[:0:-1]


def late_bits(shards):
    return bits_of(shards)[1:]


def late_place(bits, over_shard):
    place = 0
    for bit in bits:
        place = place * 2 + (over_shard // bit) % 2
    return place


def add_block(sums, hot, rows_of, over_shard, *, sub, subs, shards, width, flip):
    group = near_group(subs, shards)
    late = late_place(late_bits(shards), over_shard)
    for over_sub in range(0, subs, 2):
        column = pl.multiple_of((sub ^ over_sub ^ flip) * width, width)
        part = jnp.dot(hot, rows_of(pl.ds(column, width)), preferred_element_type=jnp.float32)
        at = jnp.where(over_shard % 2 == 0, group.index((over_sub, 0)), group.index((over_sub, 1)))
        sums[at, late] += part


def hot_rows(slots, block, live):
    slot = jnp.where(block < live, slots[block : block + 1, :], -1)
    return (slot == lax.broadcasted_iota(jnp.int32, (SLOT, SLOT), 0)).astype(jnp.bfloat16)


def send_kernel(
    live_in, bids_in, slots_in, points, sums, held, live, bids, slots, small, arrived, *, blocks, group, shards, subs, width
):
    sub, shard = lax.axis_index("sub"), lax.axis_index("shard")
    firsts = [
        pltpu.make_async_copy(live_in, live, small.at[0]),
        pltpu.make_async_copy(bids_in, bids, small.at[1]),
        pltpu.make_async_copy(slots_in, slots, small.at[2]),
    ]
    for copy in firsts:
        copy.start()
    copies = []
    for first in range(0, blocks, group):
        span = pl.ds(first * SLOT, group * SLOT)
        copies.append(pltpu.make_async_copy(points.at[span], held.at[span], arrived.at[first // group]))
        copies[-1].start()
    sums[...] = jnp.zeros_like(sums)
    for copy in firsts:
        copy.wait()
    for block in range(blocks):
        if block % group == 0:
            copies[block // group].wait()
        span = slice(block * SLOT, (block + 1) * SLOT)
        add_block(
            sums,
            hot_rows(slots, block, live[0]),
            lambda column, span=span: held[span, column],
            bids[block] ^ shard,
            sub=sub,
            subs=subs,
            shards=shards,
            width=width,
            flip=1,
        )


def keep_kernel(live, bids, slots, old, points, sums, *, blocks, shards, subs, width):
    sub, shard = lax.axis_index("sub"), lax.axis_index("shard")
    sums[...] = jnp.zeros_like(sums)
    sums[0, 0] = prior_weight * old[...].astype(jnp.float32)
    for block in range(blocks):
        span = slice(block * SLOT, (block + 1) * SLOT)
        add_block(
            sums,
            hot_rows(slots, block, live[0]),
            lambda column, span=span: points[span, column],
            bids[block] ^ shard,
            sub=sub,
            subs=subs,
            shards=shards,
            width=width,
            flip=0,
        )


def turn_kernel(points, turned):
    count = points.shape[0] // 2
    for first in range(0, points.shape[0], count):
        turned[:, first : first + count] = points[first : first + count, :].T


def mix_kernel(keep, crossed, *refs, rate):
    terms, (mine, code) = refs[:-2], refs[-2:]
    total = keep[0] + crossed[0]
    for term in terms:
        total = total + decode(term[...], rate)
    mine[...] = total
    code[...] = encode(total, rate)


def finish_kernel(mine, there, own, code, *, rate):
    own[...] = mine[0] + decode(there[1], rate)
    code[0] = encode(own[...], rate)
    code[1] = encode(mine[1] + decode(there[0], rate), rate)


def score_kernel(
    bids, slots, own, turned, *refs, blocks, shards, subs, rows, width, rate, group
):
    chips = near_group(subs, shards)
    near, far, (fresh, margin, cents) = refs[: len(chips)], refs[len(chips) : 2 * len(chips)], refs[2 * len(chips) :]
    sub, shard = lax.axis_index("sub"), lax.axis_index("shard")
    bits = late_bits(shards)
    for over_shard in range(shards):
        late = late_place(bits, over_shard)
        parts = []
        for over_sub in range(0, subs, 2):
            chip = chips.index((over_sub, over_shard % 2))
            parts.append((sub ^ over_sub, decode(near[chip][late], rate)))
            parts.append((sub ^ 1 ^ over_sub, decode(far[chip][late], rate)))
        squares = sum(jnp.sum(part * part, axis=1, keepdims=True) for _, part in parts)
        scale = lax.rsqrt(squares + norm_eps)
        row = pl.ds(pl.multiple_of((shard ^ over_shard) * rows, rows), rows)
        for place, part in parts:
            cents[row, pl.ds(pl.multiple_of(place * width, width), width)] = (part * scale).astype(jnp.bfloat16)
        if over_shard == 0:
            fresh[...] = (own[...] * scale).astype(jnp.bfloat16)

    for block in range(blocks // group):
        score = jnp.dot(
            cents[...],
            turned[:, block * group * SLOT : (block + 1) * group * SLOT],
            preferred_element_type=jnp.float32,
        )
        for inner in range(group):
            at = block * group + inner
            line = slice(at, at + 1)
            part = score[:, inner * SLOT : (inner + 1) * SLOT]
            hit = lax.broadcasted_iota(jnp.int32, part.shape, 0) == bids[at] * SLOT + slots[line, :]
            mine = jnp.sum(jnp.where(hit, part, 0.0), axis=0, keepdims=True)
            rival = jnp.max(jnp.where(hit, -jnp.inf, part), axis=0, keepdims=True)
            margin[line, :] = mine - rival


def local(points, block_ids, slot_ids, live_blocks, old_centroids):
    row_count, feat_width = points.shape
    blocks = row_count // SLOT
    shards = lax.axis_size("shard")
    subs = lax.axis_size("sub")
    rows, width = old_centroids.shape
    total = rows * shards
    top = POINT_LIMIT * (row_count * shards * subs + prior_weight)
    rate = code_rate(math.ceil(math.log2(top)))
    slots = slot_ids.reshape(blocks, SLOT)
    chips = near_group(subs, shards)
    bits = late_bits(shards)
    late = 1 << len(bits)
    small_limit = 4 * MIB + 8 * total * feat_width
    smem = pl.BlockSpec(memory_space=pltpu.SMEM)
    vmem = pl.BlockSpec(memory_space=pltpu.VMEM)
    hbm = pl.BlockSpec(memory_space=pltpu.HBM)

    def swap(value, over_sub, over_shard):
        pairs = []
        for shard in range(shards):
            for sub in range(subs):
                pairs.append((shard * subs + sub, (shard ^ over_shard) * subs + (sub ^ over_sub)))
        return lax.ppermute(value, ("shard", "sub"), pairs)

    def in_hbm(value):
        return pltpu.with_memory_space_constraint(value, pltpu.HBM)

    group = 2 if blocks % 2 == 0 else 1
    shape = jax.ShapeDtypeStruct((len(chips), late, rows, width), jnp.float32)
    cost = pl.CostEstimate(flops=row_count * SLOT * feat_width, bytes_accessed=row_count * feat_width, transcendentals=0)
    sizes = dict(blocks=blocks, shards=shards, subs=subs, width=width)
    send, held = pl.pallas_call(
        functools.partial(send_kernel, group=group, **sizes),
        out_shape=(shape, jax.ShapeDtypeStruct(points.shape, points.dtype)),
        in_specs=[hbm] * 4,
        out_specs=(vmem, vmem),
        scratch_shapes=[
            pltpu.SMEM((1,), jnp.int32),
            pltpu.SMEM((blocks,), jnp.int32),
            pltpu.VMEM((blocks, SLOT), jnp.int32),
            pltpu.SemaphoreType.DMA((3,)),
            pltpu.SemaphoreType.DMA((blocks // group,)),
        ],
        compiler_params=pltpu.CompilerParams(vmem_limit_bytes=8 * MIB + 4 * total * feat_width),
        cost_estimate=cost,
        name="sums_send",
    )(live_blocks, in_hbm(block_ids), in_hbm(slots), in_hbm(points))
    crossed = swap(send, 1, 0)
    keep = pl.pallas_call(
        functools.partial(keep_kernel, **sizes),
        out_shape=shape,
        in_specs=[smem, smem, vmem, vmem, vmem],
        out_specs=vmem,
        compiler_params=pltpu.CompilerParams(vmem_limit_bytes=8 * MIB + 4 * total * feat_width),
        cost_estimate=cost,
        name="sums_keep",
    )(live_blocks, block_ids, slots, old_centroids, held)
    terms = []
    for index, (over_sub, over_shard) in list(enumerate(chips))[1:]:
        terms.append(swap(encode(keep[index] + crossed[index], rate), over_sub, over_shard))

    piece = (late, rows, width)
    mine, code = pl.pallas_call(
        functools.partial(mix_kernel, rate=rate),
        out_shape=(jax.ShapeDtypeStruct(piece, jnp.float32), jax.ShapeDtypeStruct(piece, jnp.int16)),
        compiler_params=pltpu.CompilerParams(vmem_limit_bytes=small_limit),
        name="mix",
    )(keep, crossed, *terms)
    held, code = lax.optimization_barrier((held, code))
    turned = pl.pallas_call(
        turn_kernel,
        out_shape=jax.ShapeDtypeStruct((feat_width, row_count), points.dtype),
        in_specs=[vmem],
        out_specs=vmem,
        compiler_params=pltpu.CompilerParams(vmem_limit_bytes=8 * MIB + 4 * total * feat_width),
        cost_estimate=cost,
        name="turn",
    )(held)
    for bit in bits[:-1]:
        half = mine.shape[0] // 2
        mine = mine[:half] + decode(swap(encode(mine[half:], rate), 0, bit), rate)
        code = encode(mine, rate)
    two = (2, rows, width)
    own, code = pl.pallas_call(
        functools.partial(finish_kernel, rate=rate),
        out_shape=(jax.ShapeDtypeStruct((rows, width), jnp.float32), jax.ShapeDtypeStruct(two, jnp.int16)),
        compiler_params=pltpu.CompilerParams(vmem_limit_bytes=small_limit),
        name="finish",
    )(mine, swap(code, 0, bits[-1]))
    for bit in reversed(bits[:-1]):
        code = jnp.concatenate([code, swap(code, 0, bit)])
    near = [code] + [swap(code, over_sub, over_shard) for over_sub, over_shard in chips[1:]]
    far = [swap(block, 1, 0) for block in near]

    fresh, margin = pl.pallas_call(
        functools.partial(
            score_kernel, blocks=blocks, shards=shards, subs=subs, rows=rows, width=width, rate=rate, group=group
        ),
        out_shape=(
            jax.ShapeDtypeStruct((rows, width), jnp.bfloat16),
            jax.ShapeDtypeStruct((blocks, SLOT), jnp.float32),
        ),
        in_specs=[smem] + [vmem] * (3 + 2 * len(chips)),
        out_specs=(vmem, vmem),
        scratch_shapes=[pltpu.VMEM((total, feat_width), jnp.bfloat16)],
        compiler_params=pltpu.CompilerParams(vmem_limit_bytes=12 * MIB + 6 * total * feat_width),
        name="scores",
    )(block_ids, slots, own, turned, *near, *far)
    return fresh, margin.reshape(row_count)


def solution(mesh):
    return jax.shard_map(
        local,
        mesh=mesh,
        in_specs=(
            P(("groups", "shard", "sub"), None),
            P(("groups", "shard", "sub")),
            P(("groups", "shard", "sub")),
            P(("groups", "shard", "sub")),
            P(("groups", "shard"), "sub"),
        ),
        out_specs=(P(("groups", "shard"), "sub"), P(("groups", "shard", "sub"))),
        check_vma=False,
    )
```

```python
import functools
import math

import jax
import jax.numpy as jnp
from jax import lax
from jax.experimental import pallas as pl
from jax.experimental.pallas import tpu as pltpu
from jax.sharding import PartitionSpec as P

SLOT = 128
POINT_LIMIT = 6.0

prior_weight = 4.0
norm_eps = 1e-06

LOW_EXP = -32
MIB = 1 << 20


def code_rate(top_exp):
    return 32767.0 / (top_exp - LOW_EXP)


def encode(value, rate):
    size = jnp.maximum(jnp.abs(value), 2.0**LOW_EXP)
    level = jnp.floor((jnp.log2(size) - LOW_EXP) * rate + 0.5)
    return jnp.where(value < 0.0, -level, level).astype(jnp.int32).astype(jnp.int16)


def decode(code, rate):
    level = code.astype(jnp.int32).astype(jnp.float32)
    size = jnp.exp2(jnp.abs(level) * (1.0 / rate) + LOW_EXP)
    return jnp.where(level < 0.0, -size, size)


def bits_of(count):
    return [1 << bit for bit in range(count.bit_length() - 1)]


def near_group(subs, shards):
    group = [(0, 0)]
    for bit in bits_of(subs)[1:]:
        group = group + [(sub ^ bit, shard) for sub, shard in group]
    group = group + [(sub, shard ^ 1) for sub, shard in group]
    return group[:1] + group[:0:-1]


def late_bits(shards):
    return bits_of(shards)[1:]


def late_place(bits, over_shard):
    place = 0
    for bit in bits:
        place = place * 2 + (over_shard // bit) % 2
    return place


def add_block(halves, hot, rows_of, over_shard, *, sub, subs, shards, width, flip):
    group = near_group(subs, shards)
    late = late_place(late_bits(shards), over_shard)
    for over_sub in range(0, subs, 2):
        column = pl.multiple_of((sub ^ over_sub ^ flip) * width, width)
        part = jnp.dot(hot, rows_of(pl.ds(column, width)), preferred_element_type=jnp.float32)
        at = jnp.where(over_shard % 2 == 0, group.index((over_sub, 0)), group.index((over_sub, 1)))
        half_rows = part.shape[0] // 2
        halves[0][at, late] += part[:half_rows]
        halves[1][at, late] += part[half_rows:]


def hot_rows(slots, block, live):
    slot = jnp.where(block < live, slots[block : block + 1, :], -1)
    return (slot == lax.broadcasted_iota(jnp.int32, (SLOT, SLOT), 0)).astype(jnp.bfloat16)


def send_kernel(
    live_in, bids_in, slots_in, points, first_half, second_half, held, live, bids, slots, small, arrived, *, blocks, group, shards, subs, width
):
    sub, shard = lax.axis_index("sub"), lax.axis_index("shard")
    firsts = [
        pltpu.make_async_copy(live_in, live, small.at[0]),
        pltpu.make_async_copy(bids_in, bids, small.at[1]),
        pltpu.make_async_copy(slots_in, slots, small.at[2]),
    ]
    for copy in firsts:
        copy.start()
    copies = []
    for first in range(0, blocks, group):
        span = pl.ds(first * SLOT, group * SLOT)
        copies.append(pltpu.make_async_copy(points.at[span], held.at[span], arrived.at[first // group]))
        copies[-1].start()
    for sums in (first_half, second_half):
        sums[...] = jnp.zeros_like(sums)
    for copy in firsts:
        copy.wait()
    for block in range(blocks):
        if block % group == 0:
            copies[block // group].wait()
        span = slice(block * SLOT, (block + 1) * SLOT)
        add_block(
            (first_half, second_half),
            hot_rows(slots, block, live[0]),
            lambda column, span=span: held[span, column],
            bids[block] ^ shard,
            sub=sub,
            subs=subs,
            shards=shards,
            width=width,
            flip=1,
        )


def keep_kernel(live, bids, slots, old, points, first_half, second_half, *, blocks, shards, subs, width):
    sub, shard = lax.axis_index("sub"), lax.axis_index("shard")
    prior = prior_weight * old[...].astype(jnp.float32)
    half_rows = prior.shape[0] // 2
    for half, sums in enumerate((first_half, second_half)):
        sums[...] = jnp.zeros_like(sums)
        sums[0, 0] = prior[half * half_rows : (half + 1) * half_rows]
    for block in range(blocks):
        span = slice(block * SLOT, (block + 1) * SLOT)
        add_block(
            (first_half, second_half),
            hot_rows(slots, block, live[0]),
            lambda column, span=span: points[span, column],
            bids[block] ^ shard,
            sub=sub,
            subs=subs,
            shards=shards,
            width=width,
            flip=0,
        )


def mix_kernel(keep, crossed, *refs, rate):
    terms, (mine, code) = refs[:-2], refs[-2:]
    total = keep[0] + crossed[0]
    for term in terms:
        total = total + decode(term[...], rate)
    mine[...] = total
    code[...] = encode(total, rate)


def finish_kernel(mine, there, own, code, *, rate):
    own[...] = mine[0] + decode(there[1], rate)
    code[0] = encode(own[...], rate)
    code[1] = encode(mine[1] + decode(there[0], rate), rate)


def score_kernel(
    bids, slots, own, points, near, far, *refs, half, blocks, shards, subs, rows, width, rate, group
):
    if half:
        (mine_in, rival_in, fresh_in), (fresh, margin, cents) = refs[:3], refs[3:]
    else:
        fresh, mine_out, rival_out, cents = refs
    chips = near_group(subs, shards)
    sub, shard = lax.axis_index("sub"), lax.axis_index("shard")
    bits = late_bits(shards)
    late_count = 1 << len(bits)
    half_rows = rows // 2
    for over_shard in range(shards):
        parts = []
        for over_sub in range(0, subs, 2):
            piece = chips.index((over_sub, over_shard % 2)) * late_count + late_place(bits, over_shard)
            parts.append((sub ^ over_sub, decode(near[piece], rate)))
            parts.append((sub ^ 1 ^ over_sub, decode(far[piece], rate)))
        squares = sum(jnp.sum(part * part, axis=1, keepdims=True) for _, part in parts)
        scale = lax.rsqrt(squares + norm_eps)
        row = pl.ds(pl.multiple_of((shard ^ over_shard) * half_rows, half_rows), half_rows)
        for place, part in parts:
            cents[row, pl.ds(pl.multiple_of(place * width, width), width)] = (part * scale).astype(jnp.bfloat16)
        if over_shard == 0:
            updated = (own[...] * scale).astype(jnp.bfloat16)
            if half:
                fresh[:half_rows] = fresh_in[...]
                fresh[half_rows:] = updated
            else:
                fresh[...] = updated

    lanes = 8
    row_of = lax.broadcasted_iota(jnp.int32, (half_rows, SLOT), 0)
    for block in range(blocks // group):
        score = lax.dot_general(
            cents[...],
            points[block * group * SLOT : (block + 1) * group * SLOT, :],
            (((1,), (1,)), ((), ())),
            preferred_element_type=jnp.float32,
        )
        for inner in range(group):
            at = block * group + inner
            line = slice(at, at + 1)
            part = score[:, inner * SLOT : (inner + 1) * SLOT].reshape(shards, half_rows, SLOT)
            own_part = part[0]
            for segment in range(1, shards):
                own_part = jnp.where(bids[at] == segment, part[segment], own_part)
            hit = row_of == slots[line, :] - half * half_rows
            mine = jnp.sum(jnp.where(hit, own_part, 0.0), axis=0, keepdims=True)
            rivals = jnp.where(hit, -jnp.inf, own_part).reshape(half_rows // lanes, lanes, SLOT).max(axis=0)
            for segment in range(shards):
                best = part[segment].reshape(half_rows // lanes, lanes, SLOT).max(axis=0)
                rivals = jnp.maximum(rivals, jnp.where(bids[at] == segment, -jnp.inf, best))
            rival = jnp.max(rivals, axis=0, keepdims=True)
            if half:
                margin[line, :] = (mine_in[line, :] + mine) - jnp.maximum(rival_in[line, :], rival)
            else:
                mine_out[line, :] = mine
                rival_out[line, :] = rival


def local(points, block_ids, slot_ids, live_blocks, old_centroids):
    row_count, feat_width = points.shape
    blocks = row_count // SLOT
    shards = lax.axis_size("shard")
    subs = lax.axis_size("sub")
    rows, width = old_centroids.shape
    half_rows = rows // 2
    total = rows * shards
    top = POINT_LIMIT * (row_count * shards * subs + prior_weight)
    rate = code_rate(math.ceil(math.log2(top)))
    slots = slot_ids.reshape(blocks, SLOT)
    chips = near_group(subs, shards)
    bits = late_bits(shards)
    late = 1 << len(bits)
    group = 2 if blocks % 2 == 0 else 1
    limit = pltpu.CompilerParams(vmem_limit_bytes=8 * MIB + 4 * total * feat_width)
    smem = pl.BlockSpec(memory_space=pltpu.SMEM)
    vmem = pl.BlockSpec(memory_space=pltpu.VMEM)
    hbm = pl.BlockSpec(memory_space=pltpu.HBM)

    def swap(value, over_sub, over_shard):
        pairs = []
        for shard in range(shards):
            for sub in range(subs):
                pairs.append((shard * subs + sub, (shard ^ over_shard) * subs + (sub ^ over_sub)))
        return lax.ppermute(value, ("shard", "sub"), pairs)

    def in_hbm(value):
        return pltpu.with_memory_space_constraint(value, pltpu.HBM)

    shape = jax.ShapeDtypeStruct((len(chips), late, half_rows, width), jnp.float32)
    cost = pl.CostEstimate(flops=row_count * SLOT * feat_width, bytes_accessed=row_count * feat_width, transcendentals=0)
    sizes = dict(blocks=blocks, shards=shards, subs=subs, width=width)
    *send, held = pl.pallas_call(
        functools.partial(send_kernel, group=group, **sizes),
        out_shape=(shape, shape, jax.ShapeDtypeStruct(points.shape, points.dtype)),
        in_specs=[hbm] * 4,
        out_specs=(vmem, vmem, vmem),
        scratch_shapes=[
            pltpu.SMEM((1,), jnp.int32),
            pltpu.SMEM((blocks,), jnp.int32),
            pltpu.VMEM((blocks, SLOT), jnp.int32),
            pltpu.SemaphoreType.DMA((3,)),
            pltpu.SemaphoreType.DMA((blocks // group,)),
        ],
        compiler_params=limit,
        cost_estimate=cost,
        name="sums_send",
    )(live_blocks, in_hbm(block_ids), in_hbm(slots), in_hbm(points))
    crossed = [swap(sums, 1, 0) for sums in send]
    keep = pl.pallas_call(
        functools.partial(keep_kernel, **sizes),
        out_shape=(shape, shape),
        in_specs=[smem, smem, vmem, vmem, vmem],
        out_specs=(vmem, vmem),
        compiler_params=limit,
        cost_estimate=cost,
        name="sums_keep",
    )(live_blocks, block_ids, slots, old_centroids, held)

    piece = (late, half_rows, width)
    two = (2, half_rows, width)

    def reduce_near(half):
        terms = []
        for index, (over_sub, over_shard) in list(enumerate(chips))[1:]:
            terms.append(swap(encode(keep[half][index] + crossed[half][index], rate), over_sub, over_shard))
        return terms

    def reduce_late(half, terms):
        mine, code = pl.pallas_call(
            functools.partial(mix_kernel, rate=rate),
            out_shape=(jax.ShapeDtypeStruct(piece, jnp.float32), jax.ShapeDtypeStruct(piece, jnp.int16)),
            compiler_params=limit,
            name=f"mix{half}",
        )(keep[half], crossed[half], *terms)
        for bit in bits[:-1]:
            count = mine.shape[0] // 2
            mine = mine[:count] + decode(swap(encode(mine[count:], rate), 0, bit), rate)
            code = encode(mine, rate)
        return mine, swap(code, 0, bits[-1])

    def gather(half, mine, there):
        own, code = pl.pallas_call(
            functools.partial(finish_kernel, rate=rate),
            out_shape=(
                jax.ShapeDtypeStruct((half_rows, width), jnp.float32),
                jax.ShapeDtypeStruct(two, jnp.int16),
            ),
            compiler_params=limit,
            name=f"finish{half}",
        )(mine, there)
        for bit in reversed(bits[:-1]):
            code = jnp.concatenate([code, swap(code, 0, bit)])
        near = jnp.concatenate([code] + [swap(code, over_sub, over_shard) for over_sub, over_shard in chips[1:]])
        return own, near

    def scores(half, own, near, far, *earlier):
        line = jax.ShapeDtypeStruct((blocks, SLOT), jnp.float32)
        fresh = jax.ShapeDtypeStruct((rows if half else half_rows, width), jnp.bfloat16)
        return pl.pallas_call(
            functools.partial(
                score_kernel,
                half=half,
                blocks=blocks,
                shards=shards,
                subs=subs,
                rows=rows,
                width=width,
                rate=rate,
                group=group,
            ),
            out_shape=(fresh, line) if half else (fresh, line, line),
            in_specs=[smem] + [vmem] * (5 + len(earlier)),
            out_specs=(vmem,) * (2 if half else 3),
            scratch_shapes=[pltpu.VMEM((total // 2, feat_width), jnp.bfloat16)],
            compiler_params=pltpu.CompilerParams(vmem_limit_bytes=12 * MIB + 6 * total * feat_width),
            cost_estimate=pl.CostEstimate(
                flops=row_count * total * feat_width,
                bytes_accessed=2 * row_count * feat_width,
                transcendentals=total * feat_width // 2,
            ),
            name=f"scores{half}",
        )(block_ids, slots, own, held, near, far, *earlier)

    terms = [reduce_near(half) for half in range(2)]
    pairs = [reduce_late(half, terms[half]) for half in range(2)]
    gathered = [gather(half, *pairs[half]) for half in range(2)]
    far = [swap(near, 1, 0) for _, near in gathered]
    fresh, mine, rival = scores(0, *gathered[0], far[0])
    fresh, margin = scores(1, *gathered[1], far[1], mine, rival, fresh)
    return fresh, margin.reshape(row_count)


def solution(mesh):
    return jax.shard_map(
        local,
        mesh=mesh,
        in_specs=(
            P(("groups", "shard", "sub"), None),
            P(("groups", "shard", "sub")),
            P(("groups", "shard", "sub")),
            P(("groups", "shard", "sub")),
            P(("groups", "shard"), "sub"),
        ),
        out_specs=(P(("groups", "shard"), "sub"), P(("groups", "shard", "sub"))),
        check_vma=False,
    )
```

```python
import functools
import math

import jax
import jax.numpy as jnp
from jax import lax
from jax.experimental import pallas as pl
from jax.experimental.pallas import tpu as pltpu
from jax.sharding import PartitionSpec as P

SLOT = 128
POINT_LIMIT = 6.0

prior_weight = 4.0
norm_eps = 1e-06

LOW_EXP = -32
MIB = 1 << 20


def code_rate(top_exp):
    return 32767.0 / (top_exp - LOW_EXP)


def encode(value, rate):
    size = jnp.maximum(jnp.abs(value), 2.0**LOW_EXP)
    level = jnp.floor((jnp.log2(size) - LOW_EXP) * rate + 0.5)
    return jnp.where(value < 0.0, -level, level).astype(jnp.int32).astype(jnp.int16)


def decode(code, rate):
    level = code.astype(jnp.int32).astype(jnp.float32)
    size = jnp.exp2(jnp.abs(level) * (1.0 / rate) + LOW_EXP)
    return jnp.where(level < 0.0, -size, size)


def bits_of(count):
    return [1 << bit for bit in range(count.bit_length() - 1)]


def near_group(subs, shards):
    group = [(0, 0)]
    for bit in bits_of(subs)[1:]:
        group = group + [(sub ^ bit, shard) for sub, shard in group]
    group = group + [(sub, shard ^ 1) for sub, shard in group]
    return group[:1] + group[:0:-1]


def late_bits(shards):
    return bits_of(shards)[1:]


def late_place(bits, over_shard):
    place = 0
    for bit in bits:
        place = place * 2 + (over_shard // bit) % 2
    return place


def add_block(halves, hot, rows_of, over_shard, *, sub, subs, shards, width, flip):
    group = near_group(subs, shards)
    late = late_place(late_bits(shards), over_shard)
    for over_sub in range(0, subs, 2):
        column = pl.multiple_of((sub ^ over_sub ^ flip) * width, width)
        part = jnp.dot(hot, rows_of(pl.ds(column, width)), preferred_element_type=jnp.float32)
        at = jnp.where(over_shard % 2 == 0, group.index((over_sub, 0)), group.index((over_sub, 1)))
        half_rows = part.shape[0] // 2
        halves[0][at, late] += part[:half_rows]
        halves[1][at, late] += part[half_rows:]


def hot_rows(slots, block, live):
    slot = jnp.where(block < live, slots[block : block + 1, :], -1)
    return (slot == lax.broadcasted_iota(jnp.int32, (SLOT, SLOT), 0)).astype(jnp.bfloat16)


def send_kernel(
    live_in, bids_in, slots_in, points, first_half, second_half, held, live, bids, slots, small, arrived, *, blocks, group, shards, subs, width
):
    sub, shard = lax.axis_index("sub"), lax.axis_index("shard")
    firsts = [
        pltpu.make_async_copy(live_in, live, small.at[0]),
        pltpu.make_async_copy(bids_in, bids, small.at[1]),
        pltpu.make_async_copy(slots_in, slots, small.at[2]),
    ]
    for copy in firsts:
        copy.start()
    copies = []
    for first in range(0, blocks, group):
        span = pl.ds(first * SLOT, group * SLOT)
        copies.append(pltpu.make_async_copy(points.at[span], held.at[span], arrived.at[first // group]))
        copies[-1].start()
    for sums in (first_half, second_half):
        sums[...] = jnp.zeros_like(sums)
    for copy in firsts:
        copy.wait()
    for block in range(blocks):
        if block % group == 0:
            copies[block // group].wait()
        span = slice(block * SLOT, (block + 1) * SLOT)
        add_block(
            (first_half, second_half),
            hot_rows(slots, block, live[0]),
            lambda column, span=span: held[span, column],
            bids[block] ^ shard,
            sub=sub,
            subs=subs,
            shards=shards,
            width=width,
            flip=1,
        )


def keep_kernel(live, bids, slots, old, points, first_half, second_half, *, blocks, shards, subs, width):
    sub, shard = lax.axis_index("sub"), lax.axis_index("shard")
    prior = prior_weight * old[...].astype(jnp.float32)
    half_rows = prior.shape[0] // 2
    for half, sums in enumerate((first_half, second_half)):
        sums[...] = jnp.zeros_like(sums)
        sums[0, 0] = prior[half * half_rows : (half + 1) * half_rows]
    for block in range(blocks):
        span = slice(block * SLOT, (block + 1) * SLOT)
        add_block(
            (first_half, second_half),
            hot_rows(slots, block, live[0]),
            lambda column, span=span: points[span, column],
            bids[block] ^ shard,
            sub=sub,
            subs=subs,
            shards=shards,
            width=width,
            flip=0,
        )


def mix_kernel(keep, crossed, *refs, rate):
    terms, (mine, code) = refs[:-2], refs[-2:]
    total = keep[0] + crossed[0]
    for term in terms:
        total = total + decode(term[...], rate)
    mine[...] = total
    code[...] = encode(total, rate)


def finish_kernel(mine, there, own, code, *, rate):
    own[...] = mine[0] + decode(there[1], rate)
    code[0] = encode(own[...], rate)
    code[1] = encode(mine[1] + decode(there[0], rate), rate)


def score_kernel(
    bids, slots, own, points, near, far, *refs, half, blocks, shards, subs, rows, width, rate, group
):
    if half:
        (mine_in, rival_in, fresh_in), (fresh, margin, cents) = refs[:3], refs[3:]
    else:
        fresh, mine_out, rival_out, cents = refs
    chips = near_group(subs, shards)
    sub, shard = lax.axis_index("sub"), lax.axis_index("shard")
    bits = late_bits(shards)
    late_count = 1 << len(bits)
    half_rows = rows // 2
    for over_shard in range(shards):
        parts = []
        for over_sub in range(0, subs, 2):
            piece = chips.index((over_sub, over_shard % 2)) * late_count + late_place(bits, over_shard)
            parts.append((sub ^ over_sub, decode(near[piece], rate)))
            parts.append((sub ^ 1 ^ over_sub, decode(far[piece], rate)))
        squares = sum(jnp.sum(part * part, axis=1, keepdims=True) for _, part in parts)
        scale = lax.rsqrt(squares + norm_eps)
        row = pl.ds(pl.multiple_of((shard ^ over_shard) * half_rows, half_rows), half_rows)
        for place, part in parts:
            cents[row, pl.ds(pl.multiple_of(place * width, width), width)] = (part * scale).astype(jnp.bfloat16)
        if over_shard == 0:
            updated = (own[...] * scale).astype(jnp.bfloat16)
            if half:
                fresh[:half_rows] = fresh_in[...]
                fresh[half_rows:] = updated
            else:
                fresh[...] = updated

    lanes = 8
    row_of = lax.broadcasted_iota(jnp.int32, (half_rows, SLOT), 0)
    for block in range(blocks // group):
        score = lax.dot_general(
            cents[...],
            points[block * group * SLOT : (block + 1) * group * SLOT, :],
            (((1,), (1,)), ((), ())),
            preferred_element_type=jnp.float32,
        )
        for inner in range(group):
            at = block * group + inner
            line = slice(at, at + 1)
            part = score[:, inner * SLOT : (inner + 1) * SLOT].reshape(shards, half_rows, SLOT)
            own_part = part[0]
            for segment in range(1, shards):
                own_part = jnp.where(bids[at] == segment, part[segment], own_part)
            hit = row_of == slots[line, :] - half * half_rows
            mine = jnp.sum(jnp.where(hit, own_part, 0.0), axis=0, keepdims=True)
            rivals = jnp.where(hit, -jnp.inf, own_part).reshape(half_rows // lanes, lanes, SLOT).max(axis=0)
            for segment in range(shards):
                best = part[segment].reshape(half_rows // lanes, lanes, SLOT).max(axis=0)
                rivals = jnp.maximum(rivals, jnp.where(bids[at] == segment, -jnp.inf, best))
            rival = jnp.max(rivals, axis=0, keepdims=True)
            if half:
                margin[line, :] = (mine_in[line, :] + mine) - jnp.maximum(rival_in[line, :], rival)
            else:
                mine_out[line, :] = mine
                rival_out[line, :] = rival


def local(points, block_ids, slot_ids, live_blocks, old_centroids):
    row_count, feat_width = points.shape
    blocks = row_count // SLOT
    shards = lax.axis_size("shard")
    subs = lax.axis_size("sub")
    rows, width = old_centroids.shape
    half_rows = rows // 2
    total = rows * shards
    top = POINT_LIMIT * (row_count * shards * subs + prior_weight)
    rate = code_rate(math.ceil(math.log2(top)))
    slots = slot_ids.reshape(blocks, SLOT)
    chips = near_group(subs, shards)
    bits = late_bits(shards)
    late = 1 << len(bits)
    group = 2 if blocks % 2 == 0 else 1
    limit = pltpu.CompilerParams(vmem_limit_bytes=8 * MIB + 4 * total * feat_width)
    smem = pl.BlockSpec(memory_space=pltpu.SMEM)
    vmem = pl.BlockSpec(memory_space=pltpu.VMEM)
    hbm = pl.BlockSpec(memory_space=pltpu.HBM)

    def swap(value, over_sub, over_shard):
        pairs = []
        for shard in range(shards):
            for sub in range(subs):
                pairs.append((shard * subs + sub, (shard ^ over_shard) * subs + (sub ^ over_sub)))
        return lax.ppermute(value, ("shard", "sub"), pairs)

    def in_hbm(value):
        return pltpu.with_memory_space_constraint(value, pltpu.HBM)

    shape = jax.ShapeDtypeStruct((len(chips), late, half_rows, width), jnp.float32)
    cost = pl.CostEstimate(flops=row_count * SLOT * feat_width, bytes_accessed=row_count * feat_width, transcendentals=0)
    sizes = dict(blocks=blocks, shards=shards, subs=subs, width=width)
    *send, held = pl.pallas_call(
        functools.partial(send_kernel, group=group, **sizes),
        out_shape=(shape, shape, jax.ShapeDtypeStruct(points.shape, points.dtype)),
        in_specs=[hbm] * 4,
        out_specs=(vmem, vmem, vmem),
        scratch_shapes=[
            pltpu.SMEM((1,), jnp.int32),
            pltpu.SMEM((blocks,), jnp.int32),
            pltpu.VMEM((blocks, SLOT), jnp.int32),
            pltpu.SemaphoreType.DMA((3,)),
            pltpu.SemaphoreType.DMA((blocks // group,)),
        ],
        compiler_params=limit,
        cost_estimate=cost,
        name="sums_send",
    )(live_blocks, in_hbm(block_ids), in_hbm(slots), in_hbm(points))
    crossed = [swap(sums, 1, 0) for sums in send]
    keep = pl.pallas_call(
        functools.partial(keep_kernel, **sizes),
        out_shape=(shape, shape),
        in_specs=[smem, smem, vmem, vmem, vmem],
        out_specs=(vmem, vmem),
        compiler_params=limit,
        cost_estimate=cost,
        name="sums_keep",
    )(live_blocks, block_ids, slots, old_centroids, held)

    piece = (late, half_rows, width)
    two = (2, half_rows, width)

    def after(value, *others):
        return lax.optimization_barrier((value, *others))[0] if others else value

    def reduce_near(half, *earlier):
        there = after(crossed[half], *earlier)
        codes = [encode(keep[half][index] + there[index], rate) for index in range(1, len(chips))]
        return codes, [swap(code, *chip) for code, chip in zip(codes, chips[1:])]

    def reduce_late(half, terms, *earlier):
        mine, code = pl.pallas_call(
            functools.partial(mix_kernel, rate=rate),
            out_shape=(jax.ShapeDtypeStruct(piece, jnp.float32), jax.ShapeDtypeStruct(piece, jnp.int16)),
            compiler_params=limit,
            name=f"mix{half}",
        )(after(keep[half], *earlier), crossed[half], *terms)
        for bit in bits[:-1]:
            count = mine.shape[0] // 2
            mine = mine[:count] + decode(swap(encode(mine[count:], rate), 0, bit), rate)
            code = encode(mine, rate)
        return mine, swap(code, 0, bits[-1])

    def finish(half, mine, there, *earlier):
        own, code = pl.pallas_call(
            functools.partial(finish_kernel, rate=rate),
            out_shape=(
                jax.ShapeDtypeStruct((half_rows, width), jnp.float32),
                jax.ShapeDtypeStruct(two, jnp.int16),
            ),
            compiler_params=limit,
            name=f"finish{half}",
        )(after(mine, *earlier), there)
        for bit in reversed(bits[:-1]):
            code = jnp.concatenate([code, swap(code, 0, bit)])
        return own, code

    def gather_near(codes):
        near = [[code] for code in codes]
        for half in range(2):
            for index, chip in enumerate(chips[1:]):
                code = codes[half]
                if half and index == len(chips) - 2:
                    code = after(code, near[0][1])
                near[half].append(swap(code, *chip))
        return [jnp.concatenate(blocks) for blocks in near]

    def scores(half, own, near, far, *earlier):
        line = jax.ShapeDtypeStruct((blocks, SLOT), jnp.float32)
        fresh = jax.ShapeDtypeStruct((rows if half else half_rows, width), jnp.bfloat16)
        return pl.pallas_call(
            functools.partial(
                score_kernel,
                half=half,
                blocks=blocks,
                shards=shards,
                subs=subs,
                rows=rows,
                width=width,
                rate=rate,
                group=group,
            ),
            out_shape=(fresh, line) if half else (fresh, line, line),
            in_specs=[smem] + [vmem] * (5 + len(earlier)),
            out_specs=(vmem,) * (2 if half else 3),
            scratch_shapes=[pltpu.VMEM((total // 2, feat_width), jnp.bfloat16)],
            compiler_params=pltpu.CompilerParams(vmem_limit_bytes=12 * MIB + 6 * total * feat_width),
            cost_estimate=pl.CostEstimate(
                flops=row_count * total * feat_width,
                bytes_accessed=2 * row_count * feat_width,
                transcendentals=total * feat_width // 2,
            ),
            name=f"scores{half}",
        )(block_ids, slots, own, held, near, far, *earlier)

    first_codes, first_terms = reduce_near(0)
    _, second_terms = reduce_near(1, *first_codes)
    first = reduce_late(0, first_terms)
    second = reduce_late(1, second_terms, first[0])
    first_own, first_code = finish(0, *first)
    second_own, second_code = finish(1, *second, first_code)
    own, codes = (first_own, second_own), (first_code, second_code)
    near = gather_near(codes)
    fresh, mine, rival = scores(0, own[0], near[0], swap(near[0], 1, 0))
    far = swap(near[1], 1, 0)
    fresh, margin = scores(1, own[1], near[1], far, mine, rival, fresh)
    return fresh, margin.reshape(row_count)


def solution(mesh):
    return jax.shard_map(
        local,
        mesh=mesh,
        in_specs=(
            P(("groups", "shard", "sub"), None),
            P(("groups", "shard", "sub")),
            P(("groups", "shard", "sub")),
            P(("groups", "shard", "sub")),
            P(("groups", "shard"), "sub"),
        ),
        out_specs=(P(("groups", "shard"), "sub"), P(("groups", "shard", "sub"))),
        check_vma=False,
    )
```

```python
import functools
import math

import jax
import jax.numpy as jnp
from jax import lax
from jax.experimental import pallas as pl
from jax.experimental.pallas import tpu as pltpu
from jax.sharding import PartitionSpec as P

SLOT = 128
POINT_LIMIT = 6.0

prior_weight = 4.0
norm_eps = 1e-06

LOW_EXP = -32
MIB = 1 << 20


def code_rate(top_exp):
    return 32767.0 / (top_exp - LOW_EXP)


def encode(value, rate):
    size = jnp.maximum(jnp.abs(value), 2.0**LOW_EXP)
    level = jnp.floor((jnp.log2(size) - LOW_EXP) * rate + 0.5)
    return jnp.where(value < 0.0, -level, level).astype(jnp.int32).astype(jnp.int16)


def decode(code, rate):
    level = code.astype(jnp.int32).astype(jnp.float32)
    size = jnp.exp2(jnp.abs(level) * (1.0 / rate) + LOW_EXP)
    return jnp.where(level < 0.0, -size, size)


def bits_of(count):
    return [1 << bit for bit in range(count.bit_length() - 1)]


def near_group(subs, shards):
    group = [(0, 0)]
    for bit in bits_of(subs)[1:]:
        group = group + [(sub ^ bit, shard) for sub, shard in group]
    group = group + [(sub, shard ^ 1) for sub, shard in group]
    return group


def late_bits(shards):
    return bits_of(shards)[1:]


def late_place(bits, over_shard):
    place = 0
    for bit in bits:
        place = place * 2 + (over_shard // bit) % 2
    return place


def add_block(halves, hot, rows_of, over_shard, *, sub, subs, shards, width, flip):
    group = near_group(subs, shards)
    late = late_place(late_bits(shards), over_shard)
    for over_sub in range(0, subs, 2):
        column = pl.multiple_of((sub ^ over_sub ^ flip) * width, width)
        part = jnp.dot(hot, rows_of(pl.ds(column, width)), preferred_element_type=jnp.float32)
        at = jnp.where(over_shard % 2 == 0, group.index((over_sub, 0)), group.index((over_sub, 1)))
        half_rows = part.shape[0] // 2
        halves[0][at, late] += part[:half_rows]
        halves[1][at, late] += part[half_rows:]


def hot_rows(slots, block, live):
    slot = jnp.where(block < live, slots[block : block + 1, :], -1)
    return (slot == lax.broadcasted_iota(jnp.int32, (SLOT, SLOT), 0)).astype(jnp.bfloat16)


def send_kernel(
    live_in, bids_in, slots_in, points, first_half, second_half, held, live, bids, slots, small, arrived, *, blocks, group, shards, subs, width
):
    sub, shard = lax.axis_index("sub"), lax.axis_index("shard")
    firsts = [
        pltpu.make_async_copy(live_in, live, small.at[0]),
        pltpu.make_async_copy(bids_in, bids, small.at[1]),
        pltpu.make_async_copy(slots_in, slots, small.at[2]),
    ]
    for copy in firsts:
        copy.start()
    copies = []
    for first in range(0, blocks, group):
        span = pl.ds(first * SLOT, group * SLOT)
        copies.append(pltpu.make_async_copy(points.at[span], held.at[span], arrived.at[first // group]))
        copies[-1].start(priority=(first // group) % 2)
    for sums in (first_half, second_half):
        sums[...] = jnp.zeros_like(sums)
    for copy in firsts:
        copy.wait()
    for block in range(blocks):
        if block % group == 0:
            copies[block // group].wait()
        span = slice(block * SLOT, (block + 1) * SLOT)
        add_block(
            (first_half, second_half),
            hot_rows(slots, block, live[0]),
            lambda column, span=span: held[span, column],
            bids[block] ^ shard,
            sub=sub,
            subs=subs,
            shards=shards,
            width=width,
            flip=1,
        )


def keep_kernel(live, bids, slots, old, points, first_half, second_half, *, blocks, shards, subs, width):
    sub, shard = lax.axis_index("sub"), lax.axis_index("shard")
    prior = prior_weight * old[...].astype(jnp.float32)
    half_rows = prior.shape[0] // 2
    for half, sums in enumerate((first_half, second_half)):
        sums[...] = jnp.zeros_like(sums)
        sums[0, 0] = prior[half * half_rows : (half + 1) * half_rows]
    for block in range(blocks):
        span = slice(block * SLOT, (block + 1) * SLOT)
        add_block(
            (first_half, second_half),
            hot_rows(slots, block, live[0]),
            lambda column, span=span: points[span, column],
            bids[block] ^ shard,
            sub=sub,
            subs=subs,
            shards=shards,
            width=width,
            flip=0,
        )


def mix_kernel(keep, crossed, *refs, rate):
    terms, (mine, code) = refs[:-2], refs[-2:]
    total = keep[0] + crossed[0]
    for term in terms:
        total = total + decode(term[...], rate)
    mine[...] = total
    code[...] = encode(total, rate)


def finish_kernel(mine, there, own, code, *, rate):
    own[...] = mine[0] + decode(there[1], rate)
    code[0] = encode(own[...], rate)
    code[1] = encode(mine[1] + decode(there[0], rate), rate)


def rows_kernel(own, near, far, fresh, cents, *, half, shards, subs, rows, width, rate):
    chips = near_group(subs, shards)
    sub, shard = lax.axis_index("sub"), lax.axis_index("shard")
    bits = late_bits(shards)
    late_count = 1 << len(bits)
    half_rows = rows // 2
    for over_shard in range(shards):
        parts = []
        for over_sub in range(0, subs, 2):
            piece = chips.index((over_sub, over_shard % 2)) * late_count + late_place(bits, over_shard)
            parts.append((sub ^ over_sub, decode(near[piece], rate)))
            parts.append((sub ^ 1 ^ over_sub, decode(far[piece], rate)))
        squares = sum(jnp.sum(part * part, axis=1, keepdims=True) for _, part in parts)
        scale = lax.rsqrt(squares + norm_eps)
        row = pl.ds(pl.multiple_of((shard ^ over_shard) * half_rows, half_rows), half_rows)
        for place, part in parts:
            cents[row, pl.ds(pl.multiple_of(place * width, width), width)] = (part * scale).astype(jnp.bfloat16)
        if over_shard == 0:
            fresh[...] = (own[...] * scale).astype(jnp.bfloat16)


def score_kernel(bids, slots, points, cents, *refs, half, blocks, shards, rows, group):
    if half:
        mine_in, rival_in, fresh_first, fresh_second, fresh, margin = refs
        fresh[: rows // 2] = fresh_first[...]
        fresh[rows // 2 :] = fresh_second[...]
    else:
        mine_out, rival_out = refs
    half_rows = rows // 2
    lanes = 8
    row_of = lax.broadcasted_iota(jnp.int32, (half_rows, SLOT), 0)
    for block in range(blocks // group):
        score = lax.dot_general(
            cents[...],
            points[block * group * SLOT : (block + 1) * group * SLOT, :],
            (((1,), (1,)), ((), ())),
            preferred_element_type=jnp.float32,
        )
        for inner in range(group):
            at = block * group + inner
            line = slice(at, at + 1)
            part = score[:, inner * SLOT : (inner + 1) * SLOT].reshape(shards, half_rows, SLOT)
            own_part = part[0]
            for segment in range(1, shards):
                own_part = jnp.where(bids[at] == segment, part[segment], own_part)
            hit = row_of == slots[line, :] - half * half_rows
            mine = jnp.sum(jnp.where(hit, own_part, 0.0), axis=0, keepdims=True)
            rivals = jnp.where(hit, -jnp.inf, own_part).reshape(half_rows // lanes, lanes, SLOT).max(axis=0)
            for segment in range(shards):
                best = part[segment].reshape(half_rows // lanes, lanes, SLOT).max(axis=0)
                rivals = jnp.maximum(rivals, jnp.where(bids[at] == segment, -jnp.inf, best))
            rival = jnp.max(rivals, axis=0, keepdims=True)
            if half:
                margin[line, :] = (mine_in[line, :] + mine) - jnp.maximum(rival_in[line, :], rival)
            else:
                mine_out[line, :] = mine
                rival_out[line, :] = rival


def local(points, block_ids, slot_ids, live_blocks, old_centroids):
    row_count, feat_width = points.shape
    blocks = row_count // SLOT
    shards = lax.axis_size("shard")
    subs = lax.axis_size("sub")
    rows, width = old_centroids.shape
    half_rows = rows // 2
    total = rows * shards
    top = POINT_LIMIT * (row_count * shards * subs + prior_weight)
    rate = code_rate(math.ceil(math.log2(top)))
    slots = slot_ids.reshape(blocks, SLOT)
    chips = near_group(subs, shards)
    bits = late_bits(shards)
    late = 1 << len(bits)
    group = 2 if blocks % 2 == 0 else 1
    limit = pltpu.CompilerParams(vmem_limit_bytes=8 * MIB + 4 * total * feat_width)
    smem = pl.BlockSpec(memory_space=pltpu.SMEM)
    vmem = pl.BlockSpec(memory_space=pltpu.VMEM)
    hbm = pl.BlockSpec(memory_space=pltpu.HBM)

    def swap(value, over_sub, over_shard):
        pairs = []
        for shard in range(shards):
            for sub in range(subs):
                pairs.append((shard * subs + sub, (shard ^ over_shard) * subs + (sub ^ over_sub)))
        return lax.ppermute(value, ("shard", "sub"), pairs)

    def in_hbm(value):
        return pltpu.with_memory_space_constraint(value, pltpu.HBM)

    shape = jax.ShapeDtypeStruct((len(chips), late, half_rows, width), jnp.float32)
    cost = pl.CostEstimate(flops=row_count * SLOT * feat_width, bytes_accessed=row_count * feat_width, transcendentals=0)
    sizes = dict(blocks=blocks, shards=shards, subs=subs, width=width)
    *send, held = pl.pallas_call(
        functools.partial(send_kernel, group=group, **sizes),
        out_shape=(shape, shape, jax.ShapeDtypeStruct(points.shape, points.dtype)),
        in_specs=[hbm] * 4,
        out_specs=(vmem, vmem, vmem),
        scratch_shapes=[
            pltpu.SMEM((1,), jnp.int32),
            pltpu.SMEM((blocks,), jnp.int32),
            pltpu.VMEM((blocks, SLOT), jnp.int32),
            pltpu.SemaphoreType.DMA((3,)),
            pltpu.SemaphoreType.DMA((blocks // group,)),
        ],
        compiler_params=limit,
        cost_estimate=cost,
        name="sums_send",
    )(live_blocks, in_hbm(block_ids), in_hbm(slots), in_hbm(points))
    crossed = [swap(sums, 1, 0) for sums in send]
    keep = pl.pallas_call(
        functools.partial(keep_kernel, **sizes),
        out_shape=(shape, shape),
        in_specs=[smem, smem, vmem, vmem, vmem],
        out_specs=(vmem, vmem),
        compiler_params=limit,
        cost_estimate=cost,
        name="sums_keep",
    )(live_blocks, block_ids, slots, old_centroids, held)

    piece = (late, half_rows, width)
    two = (2, half_rows, width)

    def after(value, *others):
        return lax.optimization_barrier((value, *others))[0] if others else value

    def reduce_near(half, *earlier):
        there = after(crossed[half], *earlier)
        codes = [encode(keep[half][index] + there[index], rate) for index in range(1, len(chips))]
        return codes, [swap(code, *chip) for code, chip in zip(codes, chips[1:])]

    def reduce_late(half, terms, *earlier):
        mine, code = pl.pallas_call(
            functools.partial(mix_kernel, rate=rate),
            out_shape=(jax.ShapeDtypeStruct(piece, jnp.float32), jax.ShapeDtypeStruct(piece, jnp.int16)),
            compiler_params=limit,
            name=f"mix{half}",
        )(after(keep[half], *earlier), crossed[half], *terms)
        for bit in bits[:-1]:
            count = mine.shape[0] // 2
            mine = mine[:count] + decode(swap(encode(mine[count:], rate), 0, bit), rate)
            code = encode(mine, rate)
        return mine, swap(code, 0, bits[-1])

    def finish(half, mine, there, *earlier):
        own, code = pl.pallas_call(
            functools.partial(finish_kernel, rate=rate),
            out_shape=(
                jax.ShapeDtypeStruct((half_rows, width), jnp.float32),
                jax.ShapeDtypeStruct(two, jnp.int16),
            ),
            compiler_params=limit,
            name=f"finish{half}",
        )(after(mine, *earlier), there)
        for bit in reversed(bits[:-1]):
            code = jnp.concatenate([code, swap(code, 0, bit)])
        return own, code

    def gather_near(codes):
        first = jnp.concatenate([codes[0]] + [swap(codes[0], *chip) for chip in chips[1:]])
        ready = [after(codes[1], first)] + [codes[1]] * (len(chips) - 2)
        return first, jnp.concatenate([codes[1]] + [swap(code, *chip) for code, chip in zip(ready, chips[1:])])

    def rows_of(half, own, near, far):
        return pl.pallas_call(
            functools.partial(
                rows_kernel, half=half, shards=shards, subs=subs, rows=rows, width=width, rate=rate
            ),
            out_shape=(
                jax.ShapeDtypeStruct((half_rows, width), jnp.bfloat16),
                jax.ShapeDtypeStruct((total // 2, feat_width), jnp.bfloat16),
            ),
            compiler_params=limit,
            name=f"rows{half}",
        )(own, near, far)

    def scores(half, cents, *earlier):
        line = jax.ShapeDtypeStruct((blocks, SLOT), jnp.float32)
        fresh = jax.ShapeDtypeStruct((rows, width), jnp.bfloat16)
        return pl.pallas_call(
            functools.partial(
                score_kernel, half=half, blocks=blocks, shards=shards, rows=rows, group=group
            ),
            out_shape=(fresh, line) if half else (line, line),
            in_specs=[smem] + [vmem] * (3 + len(earlier)),
            out_specs=(vmem, vmem),
            compiler_params=limit,
            cost_estimate=pl.CostEstimate(
                flops=row_count * total * feat_width,
                bytes_accessed=2 * row_count * feat_width,
                transcendentals=0,
            ),
            name=f"scores{half}",
        )(block_ids, slots, held, cents, *earlier)

    first_codes, first_terms = reduce_near(0)
    _, second_terms = reduce_near(1, *first_codes)
    first = reduce_late(0, first_terms)
    second = reduce_late(1, second_terms, first[0])
    first_own, first_code = finish(0, *first)
    second_own, second_code = finish(1, *second, first_code)
    own, codes = (first_own, second_own), (first_code, second_code)
    near = gather_near(codes)
    far = [swap(block, 1, 0) for block in near]
    first_fresh, first_rows = rows_of(0, own[0], near[0], far[0])
    mine, rival = scores(0, first_rows)
    second_fresh, second_rows = rows_of(1, own[1], near[1], far[1])
    fresh, margin = scores(1, second_rows, mine, rival, first_fresh, second_fresh)
    return fresh, margin.reshape(row_count)


def solution(mesh):
    return jax.shard_map(
        local,
        mesh=mesh,
        in_specs=(
            P(("groups", "shard", "sub"), None),
            P(("groups", "shard", "sub")),
            P(("groups", "shard", "sub")),
            P(("groups", "shard", "sub")),
            P(("groups", "shard"), "sub"),
        ),
        out_specs=(P(("groups", "shard"), "sub"), P(("groups", "shard", "sub"))),
        check_vma=False,
    )
```

```python
import functools
import math

import jax
import jax.numpy as jnp
from jax import lax
from jax.experimental import pallas as pl
from jax.experimental.pallas import tpu as pltpu
from jax.sharding import PartitionSpec as P

SLOT = 128
POINT_LIMIT = 6.0

prior_weight = 4.0
norm_eps = 1e-06

LOW_EXP = -32
MIB = 1 << 20


def code_rate(top_exp):
    return 32767.0 / (top_exp - LOW_EXP)


def encode(value, rate):
    size = jnp.maximum(jnp.abs(value), 2.0**LOW_EXP)
    level = jnp.floor((jnp.log2(size) - LOW_EXP) * rate + 0.5)
    return jnp.where(value < 0.0, -level, level).astype(jnp.int32).astype(jnp.int16)


def decode(code, rate):
    level = code.astype(jnp.int32).astype(jnp.float32)
    size = jnp.exp2(jnp.abs(level) * (1.0 / rate) + LOW_EXP)
    return jnp.where(level < 0.0, -size, size)


def bits_of(count):
    return [1 << bit for bit in range(count.bit_length() - 1)]


def late_bits(shards):
    return bits_of(shards)[1:]


def late_place(bits, over_shard):
    place = 0
    for bit in bits:
        place = place * 2 + (over_shard // bit) % 2
    return place


def add_block(sums, hot, rows_of, over_shard, *, sub, shards, width, flip):
    bits = late_bits(shards)
    late = late_place(bits, over_shard)
    count = 1 << len(bits)
    for over_sub in (0, 2):
        column = pl.multiple_of((sub ^ over_sub ^ flip) * width, width)
        part = jnp.dot(hot, rows_of(pl.ds(column, width)), preferred_element_type=jnp.float32)
        half_rows = part.shape[0] // 2
        first = (over_shard % 2 if over_sub == 0 else 1 - over_shard % 2) * 2 * count
        for half in range(2):
            rows = part[half * half_rows : (half + 1) * half_rows]
            sums[over_sub // 2][first + half * count + late] += rows


def hot_rows(slots, block, live):
    slot = jnp.where(block < live, slots[block : block + 1, :], -1)
    return (slot == lax.broadcasted_iota(jnp.int32, (SLOT, SLOT), 0)).astype(jnp.bfloat16)


def send_kernel(
    live_in, bids_in, slots_in, points, here, there, held, live, bids, slots, small, arrived, *, blocks, group, shards, width
):
    sub, shard = lax.axis_index("sub"), lax.axis_index("shard")
    firsts = [
        pltpu.make_async_copy(live_in, live, small.at[0]),
        pltpu.make_async_copy(bids_in, bids, small.at[1]),
        pltpu.make_async_copy(slots_in, slots, small.at[2]),
    ]
    for copy in firsts:
        copy.start()
    copies = []
    for first in range(0, blocks, group):
        span = pl.ds(first * SLOT, group * SLOT)
        copies.append(pltpu.make_async_copy(points.at[span], held.at[span], arrived.at[first // group]))
        copies[-1].start(priority=(first // group) % 2)
    for sums in (here, there):
        sums[...] = jnp.zeros_like(sums)
    for copy in firsts:
        copy.wait()
    for block in range(blocks):
        if block % group == 0:
            copies[block // group].wait()
        span = slice(block * SLOT, (block + 1) * SLOT)
        add_block(
            (here, there),
            hot_rows(slots, block, live[0]),
            lambda column, span=span: held[span, column],
            bids[block] ^ shard,
            sub=sub,
            shards=shards,
            width=width,
            flip=1,
        )


def keep_kernel(live, bids, slots, old, points, here, there, *, blocks, shards, width):
    sub, shard = lax.axis_index("sub"), lax.axis_index("shard")
    prior = prior_weight * old[...].astype(jnp.float32)
    half_rows = prior.shape[0] // 2
    for sums in (here, there):
        sums[...] = jnp.zeros_like(sums)
    for half in range(2):
        here[half << len(late_bits(shards))] = prior[half * half_rows : (half + 1) * half_rows]
    for block in range(blocks):
        span = slice(block * SLOT, (block + 1) * SLOT)
        add_block(
            (here, there),
            hot_rows(slots, block, live[0]),
            lambda column, span=span: points[span, column],
            bids[block] ^ shard,
            sub=sub,
            shards=shards,
            width=width,
            flip=0,
        )


def mix_kernel(keep, crossed, by_z, by_x, both, mine, code, *, half, rate):
    count = mine.shape[0]
    span = slice(half * count, (half + 1) * count)
    total = keep[span] + crossed[span]
    for term in (both[span], by_x[...], by_z[...]):
        total = total + decode(term, rate)
    mine[...] = total
    code[...] = encode(total, rate)


def finish_kernel(mine, there, own, code, *, rate):
    own[...] = mine[0] + decode(there[1], rate)
    code[0] = encode(own[...], rate)
    code[1] = encode(mine[1] + decode(there[0], rate), rate)


def rows_kernel(own, near, far, fresh, cents, *, shards, rows, width, rate):
    sub, shard = lax.axis_index("sub"), lax.axis_index("shard")
    bits = late_bits(shards)
    half_rows = rows // 2
    for over_shard in range(shards):
        parts = []
        for over_sub in (0, 2):
            chip = over_sub // 2 + 2 * (over_shard % 2)
            piece = (chip << len(bits)) + late_place(bits, over_shard)
            parts.append((sub ^ over_sub, decode(near[piece], rate)))
            parts.append((sub ^ 1 ^ over_sub, decode(far[piece], rate)))
        squares = sum(jnp.sum(part * part, axis=1, keepdims=True) for _, part in parts)
        scale = lax.rsqrt(squares + norm_eps)
        row = pl.ds(pl.multiple_of((shard ^ over_shard) * half_rows, half_rows), half_rows)
        for place, part in parts:
            cents[row, pl.ds(pl.multiple_of(place * width, width), width)] = (part * scale).astype(jnp.bfloat16)
        if over_shard == 0:
            fresh[...] = (own[...] * scale).astype(jnp.bfloat16)


def score_kernel(bids, slots, points, cents, *refs, half, blocks, rows, group):
    half_rows = rows // 2
    tile = min(256, cents.shape[0])
    lane = lax.broadcasted_iota(jnp.int32, (SLOT, SLOT), 1)
    filler = jnp.zeros((SLOT - blocks, SLOT), jnp.int32)
    turned = jnp.concatenate([slots[...], filler]).T - half * half_rows
    inside = (turned >= 0) & (turned < half_rows)
    mine_of = jnp.full((SLOT, SLOT), -jnp.inf, jnp.float32)
    rival_of = mine_of
    for block in range(0, blocks, group):
        mine = [None] * group
        rival = [None] * group
        for first in range(0, cents.shape[0], tile):
            score = lax.dot_general(
                points[block * SLOT : (block + group) * SLOT, :],
                cents[first : first + tile, :],
                (((1,), (1,)), ((), ())),
                preferred_element_type=jnp.float32,
            )
            for inner in range(group):
                at = block + inner
                row = jnp.where(inside, turned + bids[at] * half_rows, -1)[:, at : at + 1]
                for left in range(0, tile, SLOT):
                    part = score[inner * SLOT : (inner + 1) * SLOT, left : left + SLOT]
                    hit = lane + (first + left) == row
                    for best, here in ((mine, hit), (rival, ~hit)):
                        seen = jnp.where(here, part, -jnp.inf)
                        best[inner] = seen if best[inner] is None else jnp.maximum(best[inner], seen)
        for inner in range(group):
            mine_of = jnp.where(lane == block + inner, jnp.max(mine[inner], axis=1, keepdims=True), mine_of)
            rival_of = jnp.where(lane == block + inner, jnp.max(rival[inner], axis=1, keepdims=True), rival_of)
    if half:
        mine_in, rival_in, fresh_first, fresh_second, fresh, margin = refs
        fresh[:half_rows] = fresh_first[...]
        fresh[half_rows:] = fresh_second[...]
        joined = jnp.maximum(mine_in[...], mine_of) - jnp.maximum(rival_in[...], rival_of)
        margin[...] = joined.T[:blocks]
    else:
        mine_out, rival_out = refs
        mine_out[...] = mine_of
        rival_out[...] = rival_of


def local(points, block_ids, slot_ids, live_blocks, old_centroids):
    row_count, feat_width = points.shape
    blocks = row_count // SLOT
    shards = lax.axis_size("shard")
    subs = lax.axis_size("sub")
    rows, width = old_centroids.shape
    half_rows = rows // 2
    total = rows * shards
    top = POINT_LIMIT * (row_count * shards * subs + prior_weight)
    rate = code_rate(math.ceil(math.log2(top)))
    slots = slot_ids.reshape(blocks, SLOT)
    bits = late_bits(shards)
    late = 1 << len(bits)
    group = 2 if blocks % 2 == 0 else 1
    limit = pltpu.CompilerParams(vmem_limit_bytes=8 * MIB + 4 * total * feat_width)
    smem = pl.BlockSpec(memory_space=pltpu.SMEM)
    vmem = pl.BlockSpec(memory_space=pltpu.VMEM)
    hbm = pl.BlockSpec(memory_space=pltpu.HBM)

    def swap(value, over_sub, over_shard):
        pairs = []
        for shard in range(shards):
            for sub in range(subs):
                pairs.append((shard * subs + sub, (shard ^ over_shard) * subs + (sub ^ over_sub)))
        return lax.ppermute(value, ("shard", "sub"), pairs)

    def in_hbm(value):
        return pltpu.with_memory_space_constraint(value, pltpu.HBM)

    shape = jax.ShapeDtypeStruct((4 * late, half_rows, width), jnp.float32)
    cost = pl.CostEstimate(flops=row_count * SLOT * feat_width, bytes_accessed=row_count * feat_width, transcendentals=0)
    sizes = dict(blocks=blocks, shards=shards, width=width)
    *send, held = pl.pallas_call(
        functools.partial(send_kernel, group=group, **sizes),
        out_shape=(shape, shape, jax.ShapeDtypeStruct(points.shape, points.dtype)),
        in_specs=[hbm] * 4,
        out_specs=(vmem, vmem, vmem),
        scratch_shapes=[
            pltpu.SMEM((1,), jnp.int32),
            pltpu.SMEM((blocks,), jnp.int32),
            pltpu.VMEM((blocks, SLOT), jnp.int32),
            pltpu.SemaphoreType.DMA((3,)),
            pltpu.SemaphoreType.DMA((blocks // group,)),
        ],
        compiler_params=limit,
        cost_estimate=cost,
        name="sums_send",
    )(live_blocks, in_hbm(block_ids), in_hbm(slots), in_hbm(points))
    crossed = [swap(sums, 1, 0) for sums in send]
    keep = pl.pallas_call(
        functools.partial(keep_kernel, **sizes),
        out_shape=(shape, shape),
        in_specs=[smem, smem, vmem, vmem, vmem],
        out_specs=(vmem, vmem),
        compiler_params=limit,
        cost_estimate=cost,
        name="sums_keep",
    )(live_blocks, block_ids, slots, old_centroids, held)

    piece = (late, half_rows, width)
    two = (2, half_rows, width)

    def after(value, *others):
        return lax.optimization_barrier((value, *others))[0] if others else value

    def near_code(side, first, end, *earlier):
        return encode(keep[side][first:end] + after(crossed[side], *earlier)[first:end], rate)

    def reduce_late(half, by_x, by_z, *earlier):
        mine, code = pl.pallas_call(
            functools.partial(mix_kernel, half=half, rate=rate),
            out_shape=(jax.ShapeDtypeStruct(piece, jnp.float32), jax.ShapeDtypeStruct(piece, jnp.int16)),
            compiler_params=limit,
            name=f"mix{half}",
        )(after(keep[0], *earlier), crossed[0], by_z, by_x, both)
        for bit in bits[:-1]:
            count = mine.shape[0] // 2
            mine = mine[:count] + decode(swap(encode(mine[count:], rate), 0, bit), rate)
            code = encode(mine, rate)
        return mine, swap(code, 0, bits[-1])

    def finish(half, mine, there, *earlier):
        own, code = pl.pallas_call(
            functools.partial(finish_kernel, rate=rate),
            out_shape=(
                jax.ShapeDtypeStruct((half_rows, width), jnp.float32),
                jax.ShapeDtypeStruct(two, jnp.int16),
            ),
            compiler_params=limit,
            name=f"finish{half}",
        )(after(mine, *earlier), there)
        for bit in reversed(bits[:-1]):
            code = jnp.concatenate([code, swap(code, 0, bit)])
        return own, code

    def rows_of(half, own, near, far):
        return pl.pallas_call(
            functools.partial(
                rows_kernel, shards=shards, rows=rows, width=width, rate=rate
            ),
            out_shape=(
                jax.ShapeDtypeStruct((half_rows, width), jnp.bfloat16),
                jax.ShapeDtypeStruct((total // 2, feat_width), jnp.bfloat16),
            ),
            compiler_params=limit,
            name=f"rows{half}",
        )(own, near, far)

    def scores(half, cents, *earlier):
        line = jax.ShapeDtypeStruct((blocks if half else SLOT, SLOT), jnp.float32)
        fresh = jax.ShapeDtypeStruct((rows, width), jnp.bfloat16)
        return pl.pallas_call(
            functools.partial(
                score_kernel, half=half, blocks=blocks, rows=rows, group=math.gcd(blocks, 4)
            ),
            out_shape=(fresh, line) if half else (line, line),
            in_specs=[smem] + [vmem] * (3 + len(earlier)),
            out_specs=(vmem, vmem),
            compiler_params=limit,
            cost_estimate=pl.CostEstimate(
                flops=row_count * total * feat_width,
                bytes_accessed=2 * row_count * feat_width,
                transcendentals=0,
            ),
            name=f"scores{half}",
        )(block_ids, slots, held, cents, *earlier)

    both = swap(near_code(1, 0, 2 * late), 2, 1)
    first_codes = near_code(1, 2 * late, 3 * late), near_code(0, 2 * late, 3 * late)
    first_terms = swap(first_codes[0], 2, 0), swap(first_codes[1], 0, 1)
    second_terms = (
        swap(near_code(1, 3 * late, 4 * late, *first_codes), 2, 0),
        swap(near_code(0, 3 * late, 4 * late, *first_codes), 0, 1),
    )
    first = reduce_late(0, *first_terms)
    second = reduce_late(1, *second_terms, first[0])
    first_own, first_code = finish(0, *first)
    second_own, second_code = finish(1, *second, first_code)
    chips = [(2, 0), (0, 1), (2, 1)]
    near = [jnp.concatenate([first_code] + [swap(first_code, *chip) for chip in chips])]
    ready = [after(second_code, near[0]), after(second_code, near[0]), second_code]
    near.append(jnp.concatenate([second_code] + [swap(code, *chip) for code, chip in zip(ready, chips)]))
    far = [swap(block, 1, 0) for block in near]
    first_fresh, first_rows = rows_of(0, first_own, near[0], far[0])
    mine, rival = scores(0, first_rows)
    second_fresh, second_rows = rows_of(1, second_own, near[1], far[1])
    fresh, margin = scores(1, second_rows, mine, rival, first_fresh, second_fresh)
    return fresh, margin.reshape(row_count)


def solution(mesh):
    return jax.shard_map(
        local,
        mesh=mesh,
        in_specs=(
            P(("groups", "shard", "sub"), None),
            P(("groups", "shard", "sub")),
            P(("groups", "shard", "sub")),
            P(("groups", "shard", "sub")),
            P(("groups", "shard"), "sub"),
        ),
        out_specs=(P(("groups", "shard"), "sub"), P(("groups", "shard", "sub"))),
        check_vma=False,
    )
```

```python
import functools
import math

import jax
import jax.numpy as jnp
from jax import lax
from jax.experimental import pallas as pl
from jax.experimental.pallas import tpu as pltpu
from jax.sharding import PartitionSpec as P

SLOT = 128
POINT_LIMIT = 6.0

prior_weight = 4.0
norm_eps = 1e-06

LOW_EXP = -32
MIB = 1 << 20


def code_rate(top_exp):
    return 32767.0 / (top_exp - LOW_EXP)


def encode(value, rate):
    size = jnp.maximum(jnp.abs(value), 2.0**LOW_EXP)
    level = jnp.floor((jnp.log2(size) - LOW_EXP) * rate + 0.5)
    return jnp.where(value < 0.0, -level, level).astype(jnp.int32).astype(jnp.int16)


def decode(code, rate):
    level = code.astype(jnp.int32).astype(jnp.float32)
    size = jnp.exp2(jnp.abs(level) * (1.0 / rate) + LOW_EXP)
    return jnp.where(level < 0.0, -size, size)


def bits_of(count):
    return [1 << bit for bit in range(count.bit_length() - 1)]


def near_group(subs, shards):
    group = [(0, 0)]
    for bit in bits_of(subs)[1:]:
        group = group + [(sub ^ bit, shard) for sub, shard in group]
    group = group + [(sub, shard ^ 1) for sub, shard in group]
    return group


def late_bits(shards):
    return bits_of(shards)[1:]


def late_place(bits, over_shard):
    place = 0
    for bit in bits:
        place = place * 2 + (over_shard // bit) % 2
    return place


def add_block(halves, hot, rows_of, over_shard, *, sub, subs, shards, width, flip):
    group = near_group(subs, shards)
    late = late_place(late_bits(shards), over_shard)
    for over_sub in range(0, subs, 2):
        column = pl.multiple_of((sub ^ over_sub ^ flip) * width, width)
        part = jnp.dot(hot, rows_of(pl.ds(column, width)), preferred_element_type=jnp.float32)
        at = jnp.where(over_shard % 2 == 0, group.index((over_sub, 0)), group.index((over_sub, 1)))
        half_rows = part.shape[0] // 2
        halves[0][at, late] += part[:half_rows]
        halves[1][at, late] += part[half_rows:]


def hot_rows(slots, block, live):
    slot = jnp.where(block < live, slots[block : block + 1, :], -1)
    return (slot == lax.broadcasted_iota(jnp.int32, (SLOT, SLOT), 0)).astype(jnp.bfloat16)


def send_kernel(
    live_in, bids_in, slots_in, points, first_half, second_half, held, live, bids, slots, small, arrived, *, blocks, group, shards, subs, width
):
    sub, shard = lax.axis_index("sub"), lax.axis_index("shard")
    firsts = [
        pltpu.make_async_copy(live_in, live, small.at[0]),
        pltpu.make_async_copy(bids_in, bids, small.at[1]),
        pltpu.make_async_copy(slots_in, slots, small.at[2]),
    ]
    for copy in firsts:
        copy.start()
    copies = []
    for first in range(0, blocks, group):
        span = pl.ds(first * SLOT, group * SLOT)
        copies.append(pltpu.make_async_copy(points.at[span], held.at[span], arrived.at[first // group]))
        copies[-1].start(priority=(first // group) % 2)
    for sums in (first_half, second_half):
        sums[...] = jnp.zeros_like(sums)
    for copy in firsts:
        copy.wait()
    for block in range(blocks):
        if block % group == 0:
            copies[block // group].wait()
        span = slice(block * SLOT, (block + 1) * SLOT)
        add_block(
            (first_half, second_half),
            hot_rows(slots, block, live[0]),
            lambda column, span=span: held[span, column],
            bids[block] ^ shard,
            sub=sub,
            subs=subs,
            shards=shards,
            width=width,
            flip=1,
        )


def keep_kernel(live, bids, slots, old, points, first_half, second_half, *, blocks, shards, subs, width):
    sub, shard = lax.axis_index("sub"), lax.axis_index("shard")
    prior = prior_weight * old[...].astype(jnp.float32)
    half_rows = prior.shape[0] // 2
    for half, sums in enumerate((first_half, second_half)):
        sums[...] = jnp.zeros_like(sums)
        sums[0, 0] = prior[half * half_rows : (half + 1) * half_rows]
    for block in range(blocks):
        span = slice(block * SLOT, (block + 1) * SLOT)
        add_block(
            (first_half, second_half),
            hot_rows(slots, block, live[0]),
            lambda column, span=span: points[span, column],
            bids[block] ^ shard,
            sub=sub,
            subs=subs,
            shards=shards,
            width=width,
            flip=0,
        )


def mix_kernel(keep, crossed, *refs, rate):
    terms, (mine, code) = refs[:-2], refs[-2:]
    total = keep[0] + crossed[0]
    for term in terms:
        total = total + decode(term[...], rate)
    mine[...] = total
    code[...] = encode(total, rate)


def finish_kernel(mine, there, own, code, *, rate):
    own[...] = mine[0] + decode(there[1], rate)
    code[0] = encode(own[...], rate)
    code[1] = encode(mine[1] + decode(there[0], rate), rate)


def rows_kernel(own, near, far, fresh, cents, *, half, shards, subs, rows, width, rate):
    chips = near_group(subs, shards)
    sub, shard = lax.axis_index("sub"), lax.axis_index("shard")
    bits = late_bits(shards)
    late_count = 1 << len(bits)
    half_rows = rows // 2
    for over_shard in range(shards):
        parts = []
        for over_sub in range(0, subs, 2):
            piece = chips.index((over_sub, over_shard % 2)) * late_count + late_place(bits, over_shard)
            parts.append((sub ^ over_sub, decode(near[piece], rate)))
            parts.append((sub ^ 1 ^ over_sub, decode(far[piece], rate)))
        squares = sum(jnp.sum(part * part, axis=1, keepdims=True) for _, part in parts)
        scale = lax.rsqrt(squares + norm_eps)
        row = pl.ds(pl.multiple_of((shard ^ over_shard) * half_rows, half_rows), half_rows)
        for place, part in parts:
            cents[row, pl.ds(pl.multiple_of(place * width, width), width)] = (part * scale).astype(jnp.bfloat16)
        if over_shard == 0:
            fresh[...] = (own[...] * scale).astype(jnp.bfloat16)


def score_kernel(bids, slots, points, cents, *refs, half, last, blocks, shards, rows, group):
    if last:
        mine_in, rival_in, fresh_first, fresh_second, fresh, margin = refs
        fresh[: rows // 2] = fresh_first[...]
        fresh[rows // 2 :] = fresh_second[...]
    else:
        mine_out, rival_out = refs
    half_rows = rows // 2
    lanes = 8
    row_of = lax.broadcasted_iota(jnp.int32, (half_rows, SLOT), 0)
    for block in range(blocks // group):
        score = lax.dot_general(
            cents[...],
            points[block * group * SLOT : (block + 1) * group * SLOT, :],
            (((1,), (1,)), ((), ())),
            preferred_element_type=jnp.float32,
        )
        for inner in range(group):
            at = block * group + inner
            line = slice(at, at + 1)
            part = score[:, inner * SLOT : (inner + 1) * SLOT].reshape(shards, half_rows, SLOT)
            own_part = part[0]
            for segment in range(1, shards):
                own_part = jnp.where(bids[at] == segment, part[segment], own_part)
            hit = row_of == slots[line, :] - half * half_rows
            mine = jnp.sum(jnp.where(hit, own_part, 0.0), axis=0, keepdims=True)
            rivals = jnp.where(hit, -jnp.inf, own_part).reshape(half_rows // lanes, lanes, SLOT).max(axis=0)
            for segment in range(shards):
                best = part[segment].reshape(half_rows // lanes, lanes, SLOT).max(axis=0)
                rivals = jnp.maximum(rivals, jnp.where(bids[at] == segment, -jnp.inf, best))
            rival = jnp.max(rivals, axis=0, keepdims=True)
            if last:
                margin[line, :] = (mine_in[line, :] + mine) - jnp.maximum(rival_in[line, :], rival)
            else:
                mine_out[line, :] = mine
                rival_out[line, :] = rival


def local(points, block_ids, slot_ids, live_blocks, old_centroids):
    row_count, feat_width = points.shape
    blocks = row_count // SLOT
    shards = lax.axis_size("shard")
    subs = lax.axis_size("sub")
    rows, width = old_centroids.shape
    half_rows = rows // 2
    total = rows * shards
    top = POINT_LIMIT * (row_count * shards * subs + prior_weight)
    rate = code_rate(math.ceil(math.log2(top)))
    slots = slot_ids.reshape(blocks, SLOT)
    chips = near_group(subs, shards)
    bits = late_bits(shards)
    late = 1 << len(bits)
    group = 2 if blocks % 2 == 0 else 1
    limit = pltpu.CompilerParams(vmem_limit_bytes=8 * MIB + 4 * total * feat_width)
    smem = pl.BlockSpec(memory_space=pltpu.SMEM)
    vmem = pl.BlockSpec(memory_space=pltpu.VMEM)
    hbm = pl.BlockSpec(memory_space=pltpu.HBM)

    def swap(value, over_sub, over_shard):
        pairs = []
        for shard in range(shards):
            for sub in range(subs):
                pairs.append((shard * subs + sub, (shard ^ over_shard) * subs + (sub ^ over_sub)))
        return lax.ppermute(value, ("shard", "sub"), pairs)

    def in_hbm(value):
        return pltpu.with_memory_space_constraint(value, pltpu.HBM)

    shape = jax.ShapeDtypeStruct((len(chips), late, half_rows, width), jnp.float32)
    cost = pl.CostEstimate(flops=row_count * SLOT * feat_width, bytes_accessed=row_count * feat_width, transcendentals=0)
    sizes = dict(blocks=blocks, shards=shards, subs=subs, width=width)
    *send, held = pl.pallas_call(
        functools.partial(send_kernel, group=group, **sizes),
        out_shape=(shape, shape, jax.ShapeDtypeStruct(points.shape, points.dtype)),
        in_specs=[hbm] * 4,
        out_specs=(vmem, vmem, vmem),
        scratch_shapes=[
            pltpu.SMEM((1,), jnp.int32),
            pltpu.SMEM((blocks,), jnp.int32),
            pltpu.VMEM((blocks, SLOT), jnp.int32),
            pltpu.SemaphoreType.DMA((3,)),
            pltpu.SemaphoreType.DMA((blocks // group,)),
        ],
        compiler_params=limit,
        cost_estimate=cost,
        name="sums_send",
    )(live_blocks, in_hbm(block_ids), in_hbm(slots), in_hbm(points))
    crossed = [swap(sums, 1, 0) for sums in send]
    keep = pl.pallas_call(
        functools.partial(keep_kernel, **sizes),
        out_shape=(shape, shape),
        in_specs=[smem, smem, vmem, vmem, vmem],
        out_specs=(vmem, vmem),
        compiler_params=limit,
        cost_estimate=cost,
        name="sums_keep",
    )(live_blocks, block_ids, slots, old_centroids, held)

    piece = (late, half_rows, width)
    two = (2, half_rows, width)

    def after(value, *others):
        return lax.optimization_barrier((value, *others))[0] if others else value

    def reduce_near(half, *earlier):
        there = after(crossed[half], *earlier)
        codes = [encode(keep[half][index] + there[index], rate) for index in range(1, len(chips))]
        return codes, [swap(code, *chip) for code, chip in zip(codes, chips[1:])]

    def reduce_late(half, terms, *earlier):
        mine, code = pl.pallas_call(
            functools.partial(mix_kernel, rate=rate),
            out_shape=(jax.ShapeDtypeStruct(piece, jnp.float32), jax.ShapeDtypeStruct(piece, jnp.int16)),
            compiler_params=limit,
            name=f"mix{half}",
        )(after(keep[half], *earlier), crossed[half], *terms)
        for bit in bits[:-1]:
            count = mine.shape[0] // 2
            mine = mine[:count] + decode(swap(encode(mine[count:], rate), 0, bit), rate)
            code = encode(mine, rate)
        return mine, swap(code, 0, bits[-1])

    def finish(half, mine, there, *earlier):
        own, code = pl.pallas_call(
            functools.partial(finish_kernel, rate=rate),
            out_shape=(
                jax.ShapeDtypeStruct((half_rows, width), jnp.float32),
                jax.ShapeDtypeStruct(two, jnp.int16),
            ),
            compiler_params=limit,
            name=f"finish{half}",
        )(after(mine, *earlier), there)
        for bit in reversed(bits[:-1]):
            code = jnp.concatenate([code, swap(code, 0, bit)])
        return own, code

    def rows_of(half, own, near, far):
        return pl.pallas_call(
            functools.partial(
                rows_kernel, half=half, shards=shards, subs=subs, rows=rows, width=width, rate=rate
            ),
            out_shape=(
                jax.ShapeDtypeStruct((half_rows, width), jnp.bfloat16),
                jax.ShapeDtypeStruct((total // 2, feat_width), jnp.bfloat16),
            ),
            compiler_params=limit,
            name=f"rows{half}",
        )(own, near, far)

    def scores(half, last, cents, *earlier):
        line = jax.ShapeDtypeStruct((blocks, SLOT), jnp.float32)
        fresh = jax.ShapeDtypeStruct((rows, width), jnp.bfloat16)
        return pl.pallas_call(
            functools.partial(
                score_kernel, half=half, last=last, blocks=blocks, shards=shards, rows=rows, group=group
            ),
            out_shape=(fresh, line) if last else (line, line),
            in_specs=[smem] + [vmem] * (3 + len(earlier)),
            out_specs=(vmem, vmem),
            compiler_params=limit,
            cost_estimate=pl.CostEstimate(
                flops=row_count * total * feat_width,
                bytes_accessed=2 * row_count * feat_width,
                transcendentals=0,
            ),
            name=f"scores{half}",
        )(block_ids, slots, held, cents, *earlier)

    first_codes, first_terms = reduce_near(0)
    _, second_terms = reduce_near(1, *first_codes)
    first = reduce_late(0, first_terms)
    second = reduce_late(1, second_terms, first[0])
    first_own, first_code = finish(0, *first)
    second_own, second_code = finish(1, *second, first_code)
    own, codes = (first_own, second_own), (first_code, second_code)
    near = jnp.concatenate([codes[0], swap(codes[0], 2, 0)])
    near = [jnp.concatenate([near, swap(near, 0, 1)])]
    near.append(jnp.concatenate([codes[1]] + [swap(codes[1], *chip) for chip in chips[1:]]))
    far = [swap(block, 1, 0) for block in near]
    second_fresh, second_rows = rows_of(1, own[1], near[1], far[1])
    mine, rival = scores(1, False, second_rows)
    first_fresh, first_rows = rows_of(0, own[0], near[0], far[0])
    fresh, margin = scores(0, True, first_rows, mine, rival, first_fresh, second_fresh)
    return fresh, margin.reshape(row_count)


def solution(mesh):
    return jax.shard_map(
        local,
        mesh=mesh,
        in_specs=(
            P(("groups", "shard", "sub"), None),
            P(("groups", "shard", "sub")),
            P(("groups", "shard", "sub")),
            P(("groups", "shard", "sub")),
            P(("groups", "shard"), "sub"),
        ),
        out_specs=(P(("groups", "shard"), "sub"), P(("groups", "shard", "sub"))),
        check_vma=False,
    )
```

```python
import functools
import math

import jax
import jax.numpy as jnp
from jax import lax
from jax.experimental import pallas as pl
from jax.experimental.pallas import tpu as pltpu
from jax.sharding import PartitionSpec as P

SLOT = 128
POINT_LIMIT = 6.0

prior_weight = 4.0
norm_eps = 1e-06

LOW_EXP = -32
MIB = 1 << 20


def code_rate(top_exp):
    return 32767.0 / (top_exp - LOW_EXP)


def encode(value, rate):
    size = jnp.maximum(jnp.abs(value), 2.0**LOW_EXP)
    level = jnp.floor((jnp.log2(size) - LOW_EXP) * rate + 0.5)
    return jnp.where(value < 0.0, -level, level).astype(jnp.int32).astype(jnp.int16)


def decode(code, rate):
    level = code.astype(jnp.int32).astype(jnp.float32)
    size = jnp.exp2(jnp.abs(level) * (1.0 / rate) + LOW_EXP)
    return jnp.where(level < 0.0, -size, size)


def bits_of(count):
    return [1 << bit for bit in range(count.bit_length() - 1)]


def near_group(subs, shards):
    group = [(0, 0)]
    for bit in bits_of(subs)[1:]:
        group = group + [(sub ^ bit, shard) for sub, shard in group]
    group = group + [(sub, shard ^ 1) for sub, shard in group]
    return group


def late_bits(shards):
    return bits_of(shards)[1:]


def late_place(bits, over_shard):
    place = 0
    for bit in bits:
        place = place * 2 + (over_shard // bit) % 2
    return place


def add_block(sums, hot, rows_of, over_shard, *, sub, shards, width, flip):
    bits = late_bits(shards)
    late = late_place(bits, over_shard)
    count = 1 << len(bits)
    for over_sub in (0, 2):
        column = pl.multiple_of((sub ^ over_sub ^ flip) * width, width)
        part = jnp.dot(hot, rows_of(pl.ds(column, width)), preferred_element_type=jnp.float32)
        half_rows = part.shape[0] // 2
        first = (over_shard % 2 if over_sub == 0 else 1 - over_shard % 2) * 2 * count
        for half in range(2):
            rows = part[half * half_rows : (half + 1) * half_rows]
            sums[over_sub // 2][first + half * count + late] += rows


def hot_rows(slots, block, live):
    slot = jnp.where(block < live, slots[block : block + 1, :], -1)
    return (slot == lax.broadcasted_iota(jnp.int32, (SLOT, SLOT), 0)).astype(jnp.bfloat16)


def send_kernel(
    live_in, bids_in, slots_in, points, here, there, held, live, bids, slots, small, arrived, *, blocks, group, shards, width
):
    sub, shard = lax.axis_index("sub"), lax.axis_index("shard")
    firsts = [
        pltpu.make_async_copy(live_in, live, small.at[0]),
        pltpu.make_async_copy(bids_in, bids, small.at[1]),
        pltpu.make_async_copy(slots_in, slots, small.at[2]),
    ]
    for copy in firsts:
        copy.start()
    copies = []
    for first in range(0, blocks, group):
        span = pl.ds(first * SLOT, group * SLOT)
        copies.append(pltpu.make_async_copy(points.at[span], held.at[span], arrived.at[first // group]))
        copies[-1].start(priority=(first // group) % 2)
    for sums in (here, there):
        sums[...] = jnp.zeros_like(sums)
    for copy in firsts:
        copy.wait()
    for block in range(blocks):
        if block % group == 0:
            copies[block // group].wait()
        span = slice(block * SLOT, (block + 1) * SLOT)
        add_block(
            (here, there),
            hot_rows(slots, block, live[0]),
            lambda column, span=span: held[span, column],
            bids[block] ^ shard,
            sub=sub,
            shards=shards,
            width=width,
            flip=1,
        )


def keep_kernel(live, bids, slots, old, points, here, there, *, blocks, shards, width):
    sub, shard = lax.axis_index("sub"), lax.axis_index("shard")
    prior = prior_weight * old[...].astype(jnp.float32)
    half_rows = prior.shape[0] // 2
    for sums in (here, there):
        sums[...] = jnp.zeros_like(sums)
    for half in range(2):
        here[half << len(late_bits(shards))] = prior[half * half_rows : (half + 1) * half_rows]
    for block in range(blocks):
        span = slice(block * SLOT, (block + 1) * SLOT)
        add_block(
            (here, there),
            hot_rows(slots, block, live[0]),
            lambda column, span=span: points[span, column],
            bids[block] ^ shard,
            sub=sub,
            shards=shards,
            width=width,
            flip=0,
        )


def mix_kernel(keep, crossed, by_z, by_x, both, mine, code, *, half, rate):
    count = mine.shape[0]
    span = slice(half * count, (half + 1) * count)
    total = keep[span] + crossed[span]
    for term in (both[span], by_x[...], by_z[...]):
        total = total + decode(term, rate)
    mine[...] = total
    code[...] = encode(total, rate)


def finish_kernel(mine, there, own, code, *, rate):
    own[...] = mine[0] + decode(there[1], rate)
    code[0] = encode(own[...], rate)
    code[1] = encode(mine[1] + decode(there[0], rate), rate)


def rows_kernel(own, near, far, fresh, cents, *, half, shards, subs, rows, width, rate):
    chips = near_group(subs, shards)
    sub, shard = lax.axis_index("sub"), lax.axis_index("shard")
    bits = late_bits(shards)
    late_count = 1 << len(bits)
    half_rows = rows // 2
    for over_shard in range(shards):
        parts = []
        for over_sub in range(0, subs, 2):
            piece = chips.index((over_sub, over_shard % 2)) * late_count + late_place(bits, over_shard)
            parts.append((sub ^ over_sub, decode(near[piece], rate)))
            parts.append((sub ^ 1 ^ over_sub, decode(far[piece], rate)))
        squares = sum(jnp.sum(part * part, axis=1, keepdims=True) for _, part in parts)
        scale = lax.rsqrt(squares + norm_eps)
        row = pl.ds(pl.multiple_of((shard ^ over_shard) * half_rows, half_rows), half_rows)
        for place, part in parts:
            cents[row, pl.ds(pl.multiple_of(place * width, width), width)] = (part * scale).astype(jnp.bfloat16)
        if over_shard == 0:
            fresh[...] = (own[...] * scale).astype(jnp.bfloat16)


def score_kernel(bids, slots, points, cents, *refs, half, last, blocks, shards, rows, group):
    if last:
        mine_in, rival_in, fresh_first, fresh_second, fresh, margin = refs
        fresh[: rows // 2] = fresh_first[...]
        fresh[rows // 2 :] = fresh_second[...]
    else:
        mine_out, rival_out = refs
    half_rows = rows // 2
    lanes = 8
    row_of = lax.broadcasted_iota(jnp.int32, (half_rows, SLOT), 0)
    for block in range(blocks // group):
        score = lax.dot_general(
            cents[...],
            points[block * group * SLOT : (block + 1) * group * SLOT, :],
            (((1,), (1,)), ((), ())),
            preferred_element_type=jnp.float32,
        )
        for inner in range(group):
            at = block * group + inner
            line = slice(at, at + 1)
            part = score[:, inner * SLOT : (inner + 1) * SLOT].reshape(shards, half_rows, SLOT)
            own_part = part[0]
            for segment in range(1, shards):
                own_part = jnp.where(bids[at] == segment, part[segment], own_part)
            hit = row_of == slots[line, :] - half * half_rows
            mine = jnp.sum(jnp.where(hit, own_part, 0.0), axis=0, keepdims=True)
            rivals = jnp.where(hit, -jnp.inf, own_part).reshape(half_rows // lanes, lanes, SLOT).max(axis=0)
            for segment in range(shards):
                best = part[segment].reshape(half_rows // lanes, lanes, SLOT).max(axis=0)
                rivals = jnp.maximum(rivals, jnp.where(bids[at] == segment, -jnp.inf, best))
            rival = jnp.max(rivals, axis=0, keepdims=True)
            if last:
                margin[line, :] = (mine_in[line, :] + mine) - jnp.maximum(rival_in[line, :], rival)
            else:
                mine_out[line, :] = mine
                rival_out[line, :] = rival


def local(points, block_ids, slot_ids, live_blocks, old_centroids):
    row_count, feat_width = points.shape
    blocks = row_count // SLOT
    shards = lax.axis_size("shard")
    subs = lax.axis_size("sub")
    rows, width = old_centroids.shape
    half_rows = rows // 2
    total = rows * shards
    top = POINT_LIMIT * (row_count * shards * subs + prior_weight)
    rate = code_rate(math.ceil(math.log2(top)))
    slots = slot_ids.reshape(blocks, SLOT)
    chips = near_group(subs, shards)
    bits = late_bits(shards)
    late = 1 << len(bits)
    group = 2 if blocks % 2 == 0 else 1
    limit = pltpu.CompilerParams(vmem_limit_bytes=8 * MIB + 4 * total * feat_width)
    smem = pl.BlockSpec(memory_space=pltpu.SMEM)
    vmem = pl.BlockSpec(memory_space=pltpu.VMEM)
    hbm = pl.BlockSpec(memory_space=pltpu.HBM)

    def swap(value, over_sub, over_shard):
        pairs = []
        for shard in range(shards):
            for sub in range(subs):
                pairs.append((shard * subs + sub, (shard ^ over_shard) * subs + (sub ^ over_sub)))
        return lax.ppermute(value, ("shard", "sub"), pairs)

    def after(value, *others):
        return lax.optimization_barrier((value, *others))[0] if others else value

    def in_hbm(value):
        return pltpu.with_memory_space_constraint(value, pltpu.HBM)

    shape = jax.ShapeDtypeStruct((4 * late, half_rows, width), jnp.float32)
    cost = pl.CostEstimate(flops=row_count * SLOT * feat_width, bytes_accessed=row_count * feat_width, transcendentals=0)
    sizes = dict(blocks=blocks, shards=shards, width=width)
    *send, held = pl.pallas_call(
        functools.partial(send_kernel, group=group, **sizes),
        out_shape=(shape, shape, jax.ShapeDtypeStruct(points.shape, points.dtype)),
        in_specs=[hbm] * 4,
        out_specs=(vmem, vmem, vmem),
        scratch_shapes=[
            pltpu.SMEM((1,), jnp.int32),
            pltpu.SMEM((blocks,), jnp.int32),
            pltpu.VMEM((blocks, SLOT), jnp.int32),
            pltpu.SemaphoreType.DMA((3,)),
            pltpu.SemaphoreType.DMA((blocks // group,)),
        ],
        compiler_params=limit,
        cost_estimate=cost,
        name="sums_send",
    )(live_blocks, in_hbm(block_ids), in_hbm(slots), in_hbm(points))
    crossed = [swap(sums, 1, 0) for sums in send]
    keep = pl.pallas_call(
        functools.partial(keep_kernel, **sizes),
        out_shape=(shape, shape),
        in_specs=[smem, smem, vmem, vmem, vmem],
        out_specs=(vmem, vmem),
        compiler_params=limit,
        cost_estimate=cost,
        name="sums_keep",
    )(live_blocks, block_ids, slots, old_centroids, held)

    piece = (late, half_rows, width)
    two = (2, half_rows, width)

    def near_code(side, first, end, *earlier):
        return encode(keep[side][first:end] + after(crossed[side], *earlier)[first:end], rate)

    def reduce_late(half, by_x, by_z, *earlier):
        mine, code = pl.pallas_call(
            functools.partial(mix_kernel, half=half, rate=rate),
            out_shape=(jax.ShapeDtypeStruct(piece, jnp.float32), jax.ShapeDtypeStruct(piece, jnp.int16)),
            compiler_params=limit,
            name=f"mix{half}",
        )(after(keep[0], *earlier), crossed[0], by_z, by_x, both)
        for bit in bits[:-1]:
            count = mine.shape[0] // 2
            mine = mine[:count] + decode(swap(encode(mine[count:], rate), 0, bit), rate)
            code = encode(mine, rate)
        return mine, swap(code, 0, bits[-1])

    def finish(half, mine, there, *earlier):
        own, code = pl.pallas_call(
            functools.partial(finish_kernel, rate=rate),
            out_shape=(
                jax.ShapeDtypeStruct((half_rows, width), jnp.float32),
                jax.ShapeDtypeStruct(two, jnp.int16),
            ),
            compiler_params=limit,
            name=f"finish{half}",
        )(after(mine, *earlier), there)
        for bit in reversed(bits[:-1]):
            code = jnp.concatenate([code, swap(code, 0, bit)])
        return own, code

    def rows_of(half, own, near, far):
        return pl.pallas_call(
            functools.partial(
                rows_kernel, half=half, shards=shards, subs=subs, rows=rows, width=width, rate=rate
            ),
            out_shape=(
                jax.ShapeDtypeStruct((half_rows, width), jnp.bfloat16),
                jax.ShapeDtypeStruct((total // 2, feat_width), jnp.bfloat16),
            ),
            compiler_params=limit,
            name=f"rows{half}",
        )(own, near, far)

    def scores(half, last, cents, *earlier):
        line = jax.ShapeDtypeStruct((blocks, SLOT), jnp.float32)
        fresh = jax.ShapeDtypeStruct((rows, width), jnp.bfloat16)
        return pl.pallas_call(
            functools.partial(
                score_kernel, half=half, last=last, blocks=blocks, shards=shards, rows=rows, group=group
            ),
            out_shape=(fresh, line) if last else (line, line),
            in_specs=[smem] + [vmem] * (3 + len(earlier)),
            out_specs=(vmem, vmem),
            compiler_params=limit,
            cost_estimate=pl.CostEstimate(
                flops=row_count * total * feat_width,
                bytes_accessed=2 * row_count * feat_width,
                transcendentals=0,
            ),
            name=f"scores{half}",
        )(block_ids, slots, held, cents, *earlier)

    diagonal = near_code(1, 0, 2 * late)
    both = swap(diagonal, 2, 1)
    by_x = near_code(1, 2 * late, 3 * late, diagonal)
    by_z = near_code(0, 2 * late, 3 * late, diagonal)
    first_terms = swap(by_x, 2, 0), swap(by_z, 0, 1)
    second_terms = (
        swap(near_code(1, 3 * late, 4 * late, by_x, by_z), 2, 0),
        swap(near_code(0, 3 * late, 4 * late, by_x, by_z), 0, 1),
    )
    first = reduce_late(0, *first_terms)
    second = reduce_late(1, *second_terms, first[0])
    first_own, first_code = finish(0, *first)
    second_own, second_code = finish(1, *second, first_code)
    own, codes = (first_own, second_own), (first_code, second_code)
    near = jnp.concatenate([codes[0], swap(codes[0], 2, 0)])
    ready = [after(codes[1], near), after(codes[1], near), codes[1]]
    near = [jnp.concatenate([near, swap(near, 0, 1)])]
    near.append(jnp.concatenate([codes[1]] + [swap(code, *chip) for code, chip in zip(ready, chips[1:])]))
    far = [swap(block, 1, 0) for block in near]
    second_fresh, second_rows = rows_of(1, own[1], near[1], far[1])
    mine, rival = scores(1, False, second_rows)
    first_fresh, first_rows = rows_of(0, own[0], near[0], far[0])
    fresh, margin = scores(0, True, first_rows, mine, rival, first_fresh, second_fresh)
    return fresh, margin.reshape(row_count)


def solution(mesh):
    return jax.shard_map(
        local,
        mesh=mesh,
        in_specs=(
            P(("groups", "shard", "sub"), None),
            P(("groups", "shard", "sub")),
            P(("groups", "shard", "sub")),
            P(("groups", "shard", "sub")),
            P(("groups", "shard"), "sub"),
        ),
        out_specs=(P(("groups", "shard"), "sub"), P(("groups", "shard", "sub"))),
        check_vma=False,
    )
```

```python
import functools
import math

import jax
import jax.numpy as jnp
from jax import lax
from jax.experimental import pallas as pl
from jax.experimental.pallas import tpu as pltpu
from jax.sharding import PartitionSpec as P

SLOT = 128
POINT_LIMIT = 6.0

prior_weight = 4.0
norm_eps = 1e-06

LOW_EXP = -32
MIB = 1 << 20


def code_rate(top_exp):
    return 32767.0 / (top_exp - LOW_EXP)


def encode(value, rate):
    size = jnp.maximum(jnp.abs(value), 2.0**LOW_EXP)
    level = jnp.floor((jnp.log2(size) - LOW_EXP) * rate + 0.5)
    return jnp.where(value < 0.0, -level, level).astype(jnp.int32).astype(jnp.int16)


def decode(code, rate):
    level = code.astype(jnp.int32).astype(jnp.float32)
    size = jnp.exp2(jnp.abs(level) * (1.0 / rate) + LOW_EXP)
    return jnp.where(level < 0.0, -size, size)


def bits_of(count):
    return [1 << bit for bit in range(count.bit_length() - 1)]


def near_group(subs, shards):
    group = [(0, 0)]
    for bit in bits_of(subs)[1:]:
        group = group + [(sub ^ bit, shard) for sub, shard in group]
    group = group + [(sub, shard ^ 1) for sub, shard in group]
    return group


def late_bits(shards):
    return bits_of(shards)[1:]


def late_place(bits, over_shard):
    place = 0
    for bit in bits:
        place = place * 2 + (over_shard // bit) % 2
    return place


def add_block(halves, hot, rows_of, over_shard, *, sub, subs, shards, width, flip):
    group = near_group(subs, shards)
    late = late_place(late_bits(shards), over_shard)
    for over_sub in range(0, subs, 2):
        column = pl.multiple_of((sub ^ over_sub ^ flip) * width, width)
        part = jnp.dot(hot, rows_of(pl.ds(column, width)), preferred_element_type=jnp.float32)
        at = jnp.where(over_shard % 2 == 0, group.index((over_sub, 0)), group.index((over_sub, 1)))
        half_rows = part.shape[0] // 2
        halves[0][at, late] += part[:half_rows]
        halves[1][at, late] += part[half_rows:]


def hot_rows(slots, block, live):
    slot = jnp.where(block < live, slots[block : block + 1, :], -1)
    return (slot == lax.broadcasted_iota(jnp.int32, (SLOT, SLOT), 0)).astype(jnp.bfloat16)


def send_kernel(
    live_in, bids_in, slots_in, points, first_half, second_half, held, live, bids, slots, small, arrived, *, blocks, group, shards, subs, width
):
    sub, shard = lax.axis_index("sub"), lax.axis_index("shard")
    firsts = [
        pltpu.make_async_copy(live_in, live, small.at[0]),
        pltpu.make_async_copy(bids_in, bids, small.at[1]),
        pltpu.make_async_copy(slots_in, slots, small.at[2]),
    ]
    for copy in firsts:
        copy.start()
    copies = []
    for first in range(0, blocks, group):
        span = pl.ds(first * SLOT, group * SLOT)
        copies.append(pltpu.make_async_copy(points.at[span], held.at[span], arrived.at[first // group]))
        copies[-1].start(priority=(first // group) % 2)
    for sums in (first_half, second_half):
        sums[...] = jnp.zeros_like(sums)
    for copy in firsts:
        copy.wait()
    for block in range(blocks):
        if block % group == 0:
            copies[block // group].wait()
        span = slice(block * SLOT, (block + 1) * SLOT)
        add_block(
            (first_half, second_half),
            hot_rows(slots, block, live[0]),
            lambda column, span=span: held[span, column],
            bids[block] ^ shard,
            sub=sub,
            subs=subs,
            shards=shards,
            width=width,
            flip=1,
        )


def keep_kernel(live, bids, slots, old, points, first_half, second_half, *, blocks, shards, subs, width):
    sub, shard = lax.axis_index("sub"), lax.axis_index("shard")
    prior = prior_weight * old[...].astype(jnp.float32)
    half_rows = prior.shape[0] // 2
    for half, sums in enumerate((first_half, second_half)):
        sums[...] = jnp.zeros_like(sums)
        sums[0, 0] = prior[half * half_rows : (half + 1) * half_rows]
    for block in range(blocks):
        span = slice(block * SLOT, (block + 1) * SLOT)
        add_block(
            (first_half, second_half),
            hot_rows(slots, block, live[0]),
            lambda column, span=span: points[span, column],
            bids[block] ^ shard,
            sub=sub,
            subs=subs,
            shards=shards,
            width=width,
            flip=0,
        )


def mix_kernel(keep, crossed, *refs, rate):
    terms, (mine, code) = refs[:-2], refs[-2:]
    total = keep[0] + crossed[0]
    for term in terms:
        total = total + decode(term[...], rate)
    mine[...] = total
    code[...] = encode(total, rate)


def finish_kernel(mine, there, own, code, *, rate):
    own[...] = mine[0] + decode(there[1], rate)
    code[0] = encode(own[...], rate)
    code[1] = encode(mine[1] + decode(there[0], rate), rate)


def rows_kernel(own, near, far, fresh, cents, *, half, shards, subs, rows, width, rate):
    chips = near_group(subs, shards)
    sub, shard = lax.axis_index("sub"), lax.axis_index("shard")
    bits = late_bits(shards)
    late_count = 1 << len(bits)
    half_rows = rows // 2
    for over_shard in range(shards):
        parts = []
        for over_sub in range(0, subs, 2):
            piece = chips.index((over_sub, over_shard % 2)) * late_count + late_place(bits, over_shard)
            parts.append((sub ^ over_sub, decode(near[piece], rate)))
            parts.append((sub ^ 1 ^ over_sub, decode(far[piece], rate)))
        squares = sum(jnp.sum(part * part, axis=1, keepdims=True) for _, part in parts)
        scale = lax.rsqrt(squares + norm_eps)
        row = pl.ds(pl.multiple_of((shard ^ over_shard) * half_rows, half_rows), half_rows)
        for place, part in parts:
            cents[row, pl.ds(pl.multiple_of(place * width, width), width)] = (part * scale).astype(jnp.bfloat16)
        if over_shard == 0:
            fresh[...] = (own[...] * scale).astype(jnp.bfloat16)


def score_kernel(bids, slots, points, cents, *refs, half, last, blocks, shards, rows, group):
    if last:
        mine_in, rival_in, fresh_first, fresh_second, fresh, margin = refs
        fresh[: rows // 2] = fresh_first[...]
        fresh[rows // 2 :] = fresh_second[...]
    else:
        mine_out, rival_out = refs
    half_rows = rows // 2
    lanes = 8
    row_of = lax.broadcasted_iota(jnp.int32, (half_rows, SLOT), 0)
    for block in range(blocks // group):
        score = lax.dot_general(
            cents[...],
            points[block * group * SLOT : (block + 1) * group * SLOT, :],
            (((1,), (1,)), ((), ())),
            preferred_element_type=jnp.float32,
        )
        for inner in range(group):
            at = block * group + inner
            line = slice(at, at + 1)
            part = score[:, inner * SLOT : (inner + 1) * SLOT].reshape(shards, half_rows, SLOT)
            own_part = part[0]
            for segment in range(1, shards):
                own_part = jnp.where(bids[at] == segment, part[segment], own_part)
            hit = row_of == slots[line, :] - half * half_rows
            mine = jnp.sum(jnp.where(hit, own_part, 0.0), axis=0, keepdims=True)
            rivals = jnp.where(hit, -jnp.inf, own_part).reshape(half_rows // lanes, lanes, SLOT).max(axis=0)
            for segment in range(shards):
                best = part[segment].reshape(half_rows // lanes, lanes, SLOT).max(axis=0)
                rivals = jnp.maximum(rivals, jnp.where(bids[at] == segment, -jnp.inf, best))
            rival = jnp.max(rivals, axis=0, keepdims=True)
            if last:
                margin[line, :] = (mine_in[line, :] + mine) - jnp.maximum(rival_in[line, :], rival)
            else:
                mine_out[line, :] = mine
                rival_out[line, :] = rival


def local(points, block_ids, slot_ids, live_blocks, old_centroids):
    row_count, feat_width = points.shape
    blocks = row_count // SLOT
    shards = lax.axis_size("shard")
    subs = lax.axis_size("sub")
    rows, width = old_centroids.shape
    half_rows = rows // 2
    total = rows * shards
    top = POINT_LIMIT * (row_count * shards * subs + prior_weight)
    rate = code_rate(math.ceil(math.log2(top)))
    slots = slot_ids.reshape(blocks, SLOT)
    chips = near_group(subs, shards)
    bits = late_bits(shards)
    late = 1 << len(bits)
    limit = pltpu.CompilerParams(vmem_limit_bytes=8 * MIB + 4 * total * feat_width)
    smem = pl.BlockSpec(memory_space=pltpu.SMEM)
    vmem = pl.BlockSpec(memory_space=pltpu.VMEM)
    hbm = pl.BlockSpec(memory_space=pltpu.HBM)

    def swap(value, over_sub, over_shard):
        pairs = []
        for shard in range(shards):
            for sub in range(subs):
                pairs.append((shard * subs + sub, (shard ^ over_shard) * subs + (sub ^ over_sub)))
        return lax.ppermute(value, ("shard", "sub"), pairs)

    def in_hbm(value):
        return pltpu.with_memory_space_constraint(value, pltpu.HBM)

    shape = jax.ShapeDtypeStruct((len(chips), late, half_rows, width), jnp.float32)
    cost = pl.CostEstimate(flops=row_count * SLOT * feat_width, bytes_accessed=row_count * feat_width, transcendentals=0)
    sizes = dict(blocks=blocks, shards=shards, subs=subs, width=width)
    *send, held = pl.pallas_call(
        functools.partial(send_kernel, group=1, **sizes),
        out_shape=(shape, shape, jax.ShapeDtypeStruct(points.shape, points.dtype)),
        in_specs=[hbm] * 4,
        out_specs=(vmem, vmem, vmem),
        scratch_shapes=[
            pltpu.SMEM((1,), jnp.int32),
            pltpu.SMEM((blocks,), jnp.int32),
            pltpu.VMEM((blocks, SLOT), jnp.int32),
            pltpu.SemaphoreType.DMA((3,)),
            pltpu.SemaphoreType.DMA((blocks,)),
        ],
        compiler_params=limit,
        cost_estimate=cost,
        name="sums_send",
    )(live_blocks, in_hbm(block_ids), in_hbm(slots), in_hbm(points))
    crossed = [swap(sums, 1, 0) for sums in send]
    keep = pl.pallas_call(
        functools.partial(keep_kernel, **sizes),
        out_shape=(shape, shape),
        in_specs=[smem, smem, vmem, vmem, vmem],
        out_specs=(vmem, vmem),
        compiler_params=limit,
        cost_estimate=cost,
        name="sums_keep",
    )(live_blocks, block_ids, slots, old_centroids, held)

    piece = (late, half_rows, width)
    two = (2, half_rows, width)

    def after(value, *others):
        return lax.optimization_barrier((value, *others))[0] if others else value

    def reduce_near(half, *earlier):
        there = after(crossed[half], *earlier)
        codes = [encode(keep[half][index] + there[index], rate) for index in range(1, len(chips))]
        return codes, [swap(code, *chip) for code, chip in zip(codes, chips[1:])]

    def reduce_late(half, terms, *earlier):
        mine, code = pl.pallas_call(
            functools.partial(mix_kernel, rate=rate),
            out_shape=(jax.ShapeDtypeStruct(piece, jnp.float32), jax.ShapeDtypeStruct(piece, jnp.int16)),
            compiler_params=limit,
            name=f"mix{half}",
        )(after(keep[half], *earlier), crossed[half], *terms)
        for bit in bits[:-1]:
            count = mine.shape[0] // 2
            mine = mine[:count] + decode(swap(encode(mine[count:], rate), 0, bit), rate)
            code = encode(mine, rate)
        return mine, swap(code, 0, bits[-1])

    def finish(half, mine, there, *earlier):
        own, code = pl.pallas_call(
            functools.partial(finish_kernel, rate=rate),
            out_shape=(
                jax.ShapeDtypeStruct((half_rows, width), jnp.float32),
                jax.ShapeDtypeStruct(two, jnp.int16),
            ),
            compiler_params=limit,
            name=f"finish{half}",
        )(after(mine, *earlier), there)
        for bit in reversed(bits[:-1]):
            code = jnp.concatenate([code, swap(code, 0, bit)])
        return own, code

    def rows_of(half, own, near, far):
        return pl.pallas_call(
            functools.partial(
                rows_kernel, half=half, shards=shards, subs=subs, rows=rows, width=width, rate=rate
            ),
            out_shape=(
                jax.ShapeDtypeStruct((half_rows, width), jnp.bfloat16),
                jax.ShapeDtypeStruct((total // 2, feat_width), jnp.bfloat16),
            ),
            compiler_params=limit,
            name=f"rows{half}",
        )(own, near, far)

    def scores(half, last, cents, *earlier):
        line = jax.ShapeDtypeStruct((blocks, SLOT), jnp.float32)
        fresh = jax.ShapeDtypeStruct((rows, width), jnp.bfloat16)
        return pl.pallas_call(
            functools.partial(
                score_kernel, half=half, last=last, blocks=blocks, shards=shards, rows=rows, group=math.gcd(blocks, 4)
            ),
            out_shape=(fresh, line) if last else (line, line),
            in_specs=[smem] + [vmem] * (3 + len(earlier)),
            out_specs=(vmem, vmem),
            compiler_params=limit,
            cost_estimate=pl.CostEstimate(
                flops=row_count * total * feat_width,
                bytes_accessed=2 * row_count * feat_width,
                transcendentals=0,
            ),
            name=f"scores{half}",
        )(block_ids, slots, held, cents, *earlier)

    first_codes, first_terms = reduce_near(0)
    _, second_terms = reduce_near(1, *first_codes)
    first = reduce_late(0, first_terms)
    second = reduce_late(1, second_terms, first[0])
    first_own, first_code = finish(0, *first)
    second_own, second_code = finish(1, *second, first_code)
    own, codes = (first_own, second_own), (first_code, second_code)
    near = jnp.concatenate([codes[0], swap(codes[0], 2, 0)])
    near = [jnp.concatenate([near, swap(near, 0, 1)])]
    near.append(jnp.concatenate([codes[1]] + [swap(codes[1], *chip) for chip in chips[1:]]))
    far = [swap(block, 1, 0) for block in near]
    second_fresh, second_rows = rows_of(1, own[1], near[1], far[1])
    mine, rival = scores(1, False, second_rows)
    first_fresh, first_rows = rows_of(0, own[0], near[0], far[0])
    fresh, margin = scores(0, True, first_rows, mine, rival, first_fresh, second_fresh)
    return fresh, margin.reshape(row_count)


def solution(mesh):
    return jax.shard_map(
        local,
        mesh=mesh,
        in_specs=(
            P(("groups", "shard", "sub"), None),
            P(("groups", "shard", "sub")),
            P(("groups", "shard", "sub")),
            P(("groups", "shard", "sub")),
            P(("groups", "shard"), "sub"),
        ),
        out_specs=(P(("groups", "shard"), "sub"), P(("groups", "shard", "sub"))),
        check_vma=False,
    )
```

```python
import functools
import math

import jax
import jax.numpy as jnp
from jax import lax
from jax.experimental import pallas as pl
from jax.experimental.pallas import tpu as pltpu
from jax.sharding import PartitionSpec as P

SLOT = 128
POINT_LIMIT = 6.0

prior_weight = 4.0
norm_eps = 1e-06

LOW_EXP = -32
MIB = 1 << 20


def code_rate(top_exp):
    return 32767.0 / (top_exp - LOW_EXP)


def encode(value, rate):
    size = jnp.maximum(jnp.abs(value), 2.0**LOW_EXP)
    level = jnp.floor((jnp.log2(size) - LOW_EXP) * rate + 0.5)
    return jnp.where(value < 0.0, -level, level).astype(jnp.int32).astype(jnp.int16)


def decode(code, rate):
    level = code.astype(jnp.int32).astype(jnp.float32)
    size = jnp.exp2(jnp.abs(level) * (1.0 / rate) + LOW_EXP)
    return jnp.where(level < 0.0, -size, size)


def bits_of(count):
    return [1 << bit for bit in range(count.bit_length() - 1)]


def near_group(subs, shards):
    group = [(0, 0)]
    for bit in bits_of(subs)[1:]:
        group = group + [(sub ^ bit, shard) for sub, shard in group]
    group = group + [(sub, shard ^ 1) for sub, shard in group]
    return group


def late_bits(shards):
    return bits_of(shards)[1:]


def late_place(bits, over_shard):
    place = 0
    for bit in bits:
        place = place * 2 + (over_shard // bit) % 2
    return place


def add_block(halves, hot, rows_of, over_shard, *, sub, subs, shards, width, flip):
    group = near_group(subs, shards)
    late = late_place(late_bits(shards), over_shard)
    for over_sub in range(0, subs, 2):
        column = pl.multiple_of((sub ^ over_sub ^ flip) * width, width)
        part = jnp.dot(hot, rows_of(pl.ds(column, width)), preferred_element_type=jnp.float32)
        at = jnp.where(over_shard % 2 == 0, group.index((over_sub, 0)), group.index((over_sub, 1)))
        half_rows = part.shape[0] // 2
        halves[0][at, late] += part[:half_rows]
        halves[1][at, late] += part[half_rows:]


def hot_rows(slots, block, live):
    slot = jnp.where(block < live, slots[block : block + 1, :], -1)
    return (slot == lax.broadcasted_iota(jnp.int32, (SLOT, SLOT), 0)).astype(jnp.bfloat16)


def send_kernel(
    live_in, bids_in, slots_in, points, first_half, second_half, held, live, bids, slots, small, arrived, *, blocks, parts, shards, subs, width
):
    sub, shard = lax.axis_index("sub"), lax.axis_index("shard")
    firsts = [
        pltpu.make_async_copy(live_in, live, small.at[0]),
        pltpu.make_async_copy(bids_in, bids, small.at[1]),
        pltpu.make_async_copy(slots_in, slots, small.at[2]),
    ]
    for copy in firsts:
        copy.start()
    copies = {}
    first = 0
    for part, count in enumerate(parts):
        span = pl.ds(first * SLOT, count * SLOT)
        copies[first] = pltpu.make_async_copy(points.at[span], held.at[span], arrived.at[part])
        copies[first].start(priority=part % 2)
        first += count
    for sums in (first_half, second_half):
        sums[...] = jnp.zeros_like(sums)
    for copy in firsts:
        copy.wait()
    for block in range(blocks):
        if block in copies:
            copies[block].wait()
        span = slice(block * SLOT, (block + 1) * SLOT)
        add_block(
            (first_half, second_half),
            hot_rows(slots, block, live[0]),
            lambda column, span=span: held[span, column],
            bids[block] ^ shard,
            sub=sub,
            subs=subs,
            shards=shards,
            width=width,
            flip=1,
        )


def keep_kernel(live, bids, slots, old, points, first_half, second_half, *, blocks, shards, subs, width):
    sub, shard = lax.axis_index("sub"), lax.axis_index("shard")
    prior = prior_weight * old[...].astype(jnp.float32)
    half_rows = prior.shape[0] // 2
    for half, sums in enumerate((first_half, second_half)):
        sums[...] = jnp.zeros_like(sums)
        sums[0, 0] = prior[half * half_rows : (half + 1) * half_rows]
    for block in range(blocks):
        span = slice(block * SLOT, (block + 1) * SLOT)
        add_block(
            (first_half, second_half),
            hot_rows(slots, block, live[0]),
            lambda column, span=span: points[span, column],
            bids[block] ^ shard,
            sub=sub,
            subs=subs,
            shards=shards,
            width=width,
            flip=0,
        )


def mix_kernel(keep, crossed, *refs, rate):
    terms, (mine, code) = refs[:-2], refs[-2:]
    total = keep[0] + crossed[0]
    for term in terms:
        total = total + decode(term[...], rate)
    mine[...] = total
    code[...] = encode(total, rate)


def finish_kernel(mine, there, own, code, *, rate):
    own[...] = mine[0] + decode(there[1], rate)
    code[0] = encode(own[...], rate)
    code[1] = encode(mine[1] + decode(there[0], rate), rate)


def rows_kernel(own, *refs, shards, subs, rows, width, rate):
    chips = near_group(subs, shards)
    sub, shard = lax.axis_index("sub"), lax.axis_index("shard")
    bits = late_bits(shards)
    late_count = 1 << len(bits)
    half_rows = rows // 2
    fresh, cents = refs[-2:]
    count = (len(refs) - 2) // 2
    near, far = refs[:count], refs[count : 2 * count]

    def piece_of(blocks, piece):
        each = blocks[0].shape[0]
        return decode(blocks[piece // each][piece % each], rate)

    for over_shard in range(shards):
        parts = []
        for over_sub in range(0, subs, 2):
            piece = chips.index((over_sub, over_shard % 2)) * late_count + late_place(bits, over_shard)
            parts.append((sub ^ over_sub, piece_of(near, piece)))
            parts.append((sub ^ 1 ^ over_sub, piece_of(far, piece)))
        squares = sum(jnp.sum(part * part, axis=1, keepdims=True) for _, part in parts)
        scale = lax.rsqrt(squares + norm_eps)
        row = pl.ds(pl.multiple_of((shard ^ over_shard) * half_rows, half_rows), half_rows)
        for place, part in parts:
            cents[row, pl.ds(pl.multiple_of(place * width, width), width)] = (part * scale).astype(jnp.bfloat16)
        if over_shard == 0:
            fresh[...] = (own[...] * scale).astype(jnp.bfloat16)


def score_kernel(bids, slots, points, cents, *refs, half, last, blocks, shards, rows, group):
    if last:
        mine_in, rival_in, fresh_first, fresh_second, fresh, margin = refs
        fresh[: rows // 2] = fresh_first[...]
        fresh[rows // 2 :] = fresh_second[...]
    else:
        mine_out, rival_out = refs
    half_rows = rows // 2
    lanes = 8
    row_of = lax.broadcasted_iota(jnp.int32, (half_rows, SLOT), 0)
    for block in range(blocks // group):
        score = lax.dot_general(
            cents[...],
            points[block * group * SLOT : (block + 1) * group * SLOT, :],
            (((1,), (1,)), ((), ())),
            preferred_element_type=jnp.float32,
        )
        for inner in range(group):
            at = block * group + inner
            line = slice(at, at + 1)
            part = score[:, inner * SLOT : (inner + 1) * SLOT].reshape(shards, half_rows, SLOT)
            own_part = part[0]
            for segment in range(1, shards):
                own_part = jnp.where(bids[at] == segment, part[segment], own_part)
            hit = row_of == slots[line, :] - half * half_rows
            mine = jnp.sum(jnp.where(hit, own_part, 0.0), axis=0, keepdims=True)
            rivals = jnp.where(hit, -jnp.inf, own_part).reshape(half_rows // lanes, lanes, SLOT).max(axis=0)
            for segment in range(shards):
                best = part[segment].reshape(half_rows // lanes, lanes, SLOT).max(axis=0)
                rivals = jnp.maximum(rivals, jnp.where(bids[at] == segment, -jnp.inf, best))
            rival = jnp.max(rivals, axis=0, keepdims=True)
            if last:
                margin[line, :] = (mine_in[line, :] + mine) - jnp.maximum(rival_in[line, :], rival)
            else:
                mine_out[line, :] = mine
                rival_out[line, :] = rival


def local(points, block_ids, slot_ids, live_blocks, old_centroids):
    row_count, feat_width = points.shape
    blocks = row_count // SLOT
    shards = lax.axis_size("shard")
    subs = lax.axis_size("sub")
    rows, width = old_centroids.shape
    half_rows = rows // 2
    total = rows * shards
    top = POINT_LIMIT * (row_count * shards * subs + prior_weight)
    rate = code_rate(math.ceil(math.log2(top)))
    slots = slot_ids.reshape(blocks, SLOT)
    chips = near_group(subs, shards)
    bits = late_bits(shards)
    late = 1 << len(bits)
    group = 2 if blocks % 2 == 0 else 1
    parts = [count for count in (blocks // 2, blocks // 3, blocks - blocks // 2 - blocks // 3) if count]
    limit = pltpu.CompilerParams(vmem_limit_bytes=8 * MIB + 4 * total * feat_width)
    smem = pl.BlockSpec(memory_space=pltpu.SMEM)
    vmem = pl.BlockSpec(memory_space=pltpu.VMEM)
    hbm = pl.BlockSpec(memory_space=pltpu.HBM)

    def swap(value, over_sub, over_shard):
        pairs = []
        for shard in range(shards):
            for sub in range(subs):
                pairs.append((shard * subs + sub, (shard ^ over_shard) * subs + (sub ^ over_sub)))
        return lax.ppermute(value, ("shard", "sub"), pairs)

    def in_hbm(value):
        return pltpu.with_memory_space_constraint(value, pltpu.HBM)

    shape = jax.ShapeDtypeStruct((len(chips), late, half_rows, width), jnp.float32)
    cost = pl.CostEstimate(flops=row_count * SLOT * feat_width, bytes_accessed=row_count * feat_width, transcendentals=0)
    sizes = dict(blocks=blocks, shards=shards, subs=subs, width=width)
    *send, held = pl.pallas_call(
        functools.partial(send_kernel, parts=parts, **sizes),
        out_shape=(shape, shape, jax.ShapeDtypeStruct(points.shape, points.dtype)),
        in_specs=[hbm] * 4,
        out_specs=(vmem, vmem, vmem),
        scratch_shapes=[
            pltpu.SMEM((1,), jnp.int32),
            pltpu.SMEM((blocks,), jnp.int32),
            pltpu.VMEM((blocks, SLOT), jnp.int32),
            pltpu.SemaphoreType.DMA((3,)),
            pltpu.SemaphoreType.DMA((len(parts),)),
        ],
        compiler_params=limit,
        cost_estimate=cost,
        name="sums_send",
    )(live_blocks, in_hbm(block_ids), in_hbm(slots), in_hbm(points))
    crossed = [swap(sums, 1, 0) for sums in send]
    keep = pl.pallas_call(
        functools.partial(keep_kernel, **sizes),
        out_shape=(shape, shape),
        in_specs=[smem, smem, vmem, vmem, vmem],
        out_specs=(vmem, vmem),
        compiler_params=limit,
        cost_estimate=cost,
        name="sums_keep",
    )(live_blocks, block_ids, slots, old_centroids, held)

    piece = (late, half_rows, width)
    two = (2, half_rows, width)

    def after(value, *others):
        return lax.optimization_barrier((value, *others))[0] if others else value

    def reduce_near(half, *earlier):
        there = after(crossed[half], *earlier)
        codes = [encode(keep[half][index] + there[index], rate) for index in range(1, len(chips))]
        return codes, [swap(code, *chip) for code, chip in zip(codes, chips[1:])]

    def reduce_late(half, terms, *earlier):
        mine, code = pl.pallas_call(
            functools.partial(mix_kernel, rate=rate),
            out_shape=(jax.ShapeDtypeStruct(piece, jnp.float32), jax.ShapeDtypeStruct(piece, jnp.int16)),
            compiler_params=limit,
            name=f"mix{half}",
        )(after(keep[half], *earlier), crossed[half], *terms)
        for bit in bits[:-1]:
            count = mine.shape[0] // 2
            mine = mine[:count] + decode(swap(encode(mine[count:], rate), 0, bit), rate)
            code = encode(mine, rate)
        return mine, swap(code, 0, bits[-1])

    def finish(half, mine, there, *earlier):
        own, code = pl.pallas_call(
            functools.partial(finish_kernel, rate=rate),
            out_shape=(
                jax.ShapeDtypeStruct((half_rows, width), jnp.float32),
                jax.ShapeDtypeStruct(two, jnp.int16),
            ),
            compiler_params=limit,
            name=f"finish{half}",
        )(after(mine, *earlier), there)
        for bit in reversed(bits[:-1]):
            code = jnp.concatenate([code, swap(code, 0, bit)])
        return own, code

    def rows_of(half, own, near, far):
        return pl.pallas_call(
            functools.partial(
                rows_kernel, shards=shards, subs=subs, rows=rows, width=width, rate=rate
            ),
            out_shape=(
                jax.ShapeDtypeStruct((half_rows, width), jnp.bfloat16),
                jax.ShapeDtypeStruct((total // 2, feat_width), jnp.bfloat16),
            ),
            compiler_params=limit,
            name=f"rows{half}",
        )(own, *near, *far)

    def scores(half, last, cents, *earlier):
        line = jax.ShapeDtypeStruct((blocks, SLOT), jnp.float32)
        fresh = jax.ShapeDtypeStruct((rows, width), jnp.bfloat16)
        return pl.pallas_call(
            functools.partial(
                score_kernel, half=half, last=last, blocks=blocks, shards=shards, rows=rows, group=group
            ),
            out_shape=(fresh, line) if last else (line, line),
            in_specs=[smem] + [vmem] * (3 + len(earlier)),
            out_specs=(vmem, vmem),
            compiler_params=limit,
            cost_estimate=pl.CostEstimate(
                flops=row_count * total * feat_width,
                bytes_accessed=2 * row_count * feat_width,
                transcendentals=0,
            ),
            name=f"scores{half}",
        )(block_ids, slots, held, cents, *earlier)

    first_codes, first_terms = reduce_near(0)
    _, second_terms = reduce_near(1, *first_codes)
    first = reduce_late(0, first_terms)
    second = reduce_late(1, second_terms, first[0])
    first_own, first_code = finish(0, *first)
    second_own, second_code = finish(1, *second, first_code)
    own, codes = (first_own, second_own), (first_code, second_code)
    near = jnp.concatenate([codes[0], swap(codes[0], 2, 0)])
    near = [jnp.concatenate([near, swap(near, 0, 1)])]
    blocks_near = [codes[1]] + [swap(codes[1], *chip) for chip in chips[1:]]
    second_fresh, second_rows = rows_of(1, own[1], blocks_near, [swap(block, 1, 0) for block in blocks_near])
    mine, rival = scores(1, False, second_rows)
    first_near = after(near[0], second_fresh)
    first_fresh, first_rows = rows_of(0, own[0], [first_near], [swap(first_near, 1, 0)])
    fresh, margin = scores(0, True, first_rows, mine, rival, first_fresh, second_fresh)
    return fresh, margin.reshape(row_count)


def solution(mesh):
    return jax.shard_map(
        local,
        mesh=mesh,
        in_specs=(
            P(("groups", "shard", "sub"), None),
            P(("groups", "shard", "sub")),
            P(("groups", "shard", "sub")),
            P(("groups", "shard", "sub")),
            P(("groups", "shard"), "sub"),
        ),
        out_specs=(P(("groups", "shard"), "sub"), P(("groups", "shard", "sub"))),
        check_vma=False,
    )
```

```python
import functools
import math

import jax
import jax.numpy as jnp
from jax import lax
from jax.experimental import pallas as pl
from jax.experimental.pallas import tpu as pltpu
from jax.sharding import PartitionSpec as P

SLOT = 128
POINT_LIMIT = 6.0

prior_weight = 4.0
norm_eps = 1e-06

LOW_EXP = -32
MIB = 1 << 20


def code_rate(top_exp):
    return 32767.0 / (top_exp - LOW_EXP)


def encode(value, rate):
    size = jnp.maximum(jnp.abs(value), 2.0**LOW_EXP)
    level = jnp.floor((jnp.log2(size) - LOW_EXP) * rate + 0.5)
    return jnp.where(value < 0.0, -level, level).astype(jnp.int32).astype(jnp.int16)


def decode(code, rate):
    level = code.astype(jnp.int32).astype(jnp.float32)
    size = jnp.exp2(jnp.abs(level) * (1.0 / rate) + LOW_EXP)
    return jnp.where(level < 0.0, -size, size)


def bits_of(count):
    return [1 << bit for bit in range(count.bit_length() - 1)]


def near_group(subs, shards):
    group = [(0, 0)]
    for bit in bits_of(subs)[1:]:
        group = group + [(sub ^ bit, shard) for sub, shard in group]
    group = group + [(sub, shard ^ 1) for sub, shard in group]
    return group


def late_bits(shards):
    return bits_of(shards)[1:]


def late_place(bits, over_shard):
    place = 0
    for bit in bits:
        place = place * 2 + (over_shard // bit) % 2
    return place


def add_block(halves, hot, rows_of, over_shard, *, sub, subs, shards, width, flip):
    group = near_group(subs, shards)
    late = late_place(late_bits(shards), over_shard)
    for over_sub in range(0, subs, 2):
        column = pl.multiple_of((sub ^ over_sub ^ flip) * width, width)
        part = jnp.dot(hot, rows_of(pl.ds(column, width)), preferred_element_type=jnp.float32)
        at = jnp.where(over_shard % 2 == 0, group.index((over_sub, 0)), group.index((over_sub, 1)))
        half_rows = part.shape[0] // 2
        halves[0][at, late] += part[:half_rows]
        halves[1][at, late] += part[half_rows:]


def hot_rows(slots, block, live):
    slot = jnp.where(block < live, slots[block : block + 1, :], -1)
    return (slot == lax.broadcasted_iota(jnp.int32, (SLOT, SLOT), 0)).astype(jnp.bfloat16)


def send_kernel(
    live_in, bids_in, slots_in, points, first_half, second_half, held, live, bids, slots, small, arrived, *, blocks, parts, shards, subs, width
):
    sub, shard = lax.axis_index("sub"), lax.axis_index("shard")
    firsts = [
        pltpu.make_async_copy(live_in, live, small.at[0]),
        pltpu.make_async_copy(bids_in, bids, small.at[1]),
        pltpu.make_async_copy(slots_in, slots, small.at[2]),
    ]
    for copy in firsts:
        copy.start()
    copies = {}
    first = 0
    for part, count in enumerate(parts):
        span = pl.ds(first * SLOT, count * SLOT)
        copies[first] = pltpu.make_async_copy(points.at[span], held.at[span], arrived.at[part])
        copies[first].start(priority=part % 2)
        first += count
    for sums in (first_half, second_half):
        sums[...] = jnp.zeros_like(sums)
    for copy in firsts:
        copy.wait()
    for block in range(blocks):
        if block in copies:
            copies[block].wait()
        span = slice(block * SLOT, (block + 1) * SLOT)
        add_block(
            (first_half, second_half),
            hot_rows(slots, block, live[0]),
            lambda column, span=span: held[span, column],
            bids[block] ^ shard,
            sub=sub,
            subs=subs,
            shards=shards,
            width=width,
            flip=1,
        )


def keep_kernel(live, bids, slots, old, points, first_half, second_half, *, blocks, shards, subs, width):
    sub, shard = lax.axis_index("sub"), lax.axis_index("shard")
    prior = prior_weight * old[...].astype(jnp.float32)
    half_rows = prior.shape[0] // 2
    for half, sums in enumerate((first_half, second_half)):
        sums[...] = jnp.zeros_like(sums)
        sums[0, 0] = prior[half * half_rows : (half + 1) * half_rows]
    for block in range(blocks):
        span = slice(block * SLOT, (block + 1) * SLOT)
        add_block(
            (first_half, second_half),
            hot_rows(slots, block, live[0]),
            lambda column, span=span: points[span, column],
            bids[block] ^ shard,
            sub=sub,
            subs=subs,
            shards=shards,
            width=width,
            flip=0,
        )


def mix_kernel(keep, crossed, *refs, rate):
    terms, (mine, code) = refs[:-2], refs[-2:]
    total = keep[0] + crossed[0]
    for term in terms:
        total = total + decode(term[...], rate)
    mine[...] = total
    code[...] = encode(total, rate)


def finish_kernel(mine, there, own, code, *, rate):
    own[...] = mine[0] + decode(there[1], rate)
    code[0] = encode(own[...], rate)
    code[1] = encode(mine[1] + decode(there[0], rate), rate)


def rows_kernel(own, *refs, shards, subs, rows, width, rate):
    chips = near_group(subs, shards)
    sub, shard = lax.axis_index("sub"), lax.axis_index("shard")
    bits = late_bits(shards)
    late_count = 1 << len(bits)
    half_rows = rows // 2
    fresh, cents = refs[-2:]
    count = (len(refs) - 2) // 2
    near, far = refs[:count], refs[count : 2 * count]

    def piece_of(blocks, piece):
        each = blocks[0].shape[0]
        return decode(blocks[piece // each][piece % each], rate)

    for over_shard in range(shards):
        parts = []
        for over_sub in range(0, subs, 2):
            piece = chips.index((over_sub, over_shard % 2)) * late_count + late_place(bits, over_shard)
            parts.append((sub ^ over_sub, piece_of(near, piece)))
            parts.append((sub ^ 1 ^ over_sub, piece_of(far, piece)))
        squares = sum(jnp.sum(part * part, axis=1, keepdims=True) for _, part in parts)
        scale = lax.rsqrt(squares + norm_eps)
        row = pl.ds(pl.multiple_of((shard ^ over_shard) * half_rows, half_rows), half_rows)
        for place, part in parts:
            cents[row, pl.ds(pl.multiple_of(place * width, width), width)] = (part * scale).astype(jnp.bfloat16)
        if over_shard == 0:
            fresh[...] = (own[...] * scale).astype(jnp.bfloat16)


def score_kernel(bids, slots, points, cents, *refs, half, last, blocks, shards, rows, group):
    if last:
        mine_in, rival_in, fresh_first, fresh_second, fresh_out, margin_out, fresh, margin, written = refs
        fresh[: rows // 2] = fresh_first[...]
        fresh[rows // 2 :] = fresh_second[...]
        cut = (blocks - 1) // 8 * 8
        spans = [slice(0, cut), slice(cut, blocks)] if cut else [slice(0, blocks)]
        writes = [pltpu.make_async_copy(fresh, fresh_out, written.at[0])]
        for index, span in enumerate(spans):
            writes.append(pltpu.make_async_copy(margin.at[span], margin_out.at[span], written.at[index + 1]))
        writes[0].start()
    else:
        mine_out, rival_out = refs
    half_rows = rows // 2
    lanes = 8
    row_of = lax.broadcasted_iota(jnp.int32, (half_rows, SLOT), 0)
    for block in range(blocks // group):
        score = lax.dot_general(
            cents[...],
            points[block * group * SLOT : (block + 1) * group * SLOT, :],
            (((1,), (1,)), ((), ())),
            preferred_element_type=jnp.float32,
        )
        for inner in range(group):
            at = block * group + inner
            line = slice(at, at + 1)
            part = score[:, inner * SLOT : (inner + 1) * SLOT].reshape(shards, half_rows, SLOT)
            own_part = part[0]
            for segment in range(1, shards):
                own_part = jnp.where(bids[at] == segment, part[segment], own_part)
            hit = row_of == slots[line, :] - half * half_rows
            mine = jnp.sum(jnp.where(hit, own_part, 0.0), axis=0, keepdims=True)
            rivals = jnp.where(hit, -jnp.inf, own_part).reshape(half_rows // lanes, lanes, SLOT).max(axis=0)
            for segment in range(shards):
                best = part[segment].reshape(half_rows // lanes, lanes, SLOT).max(axis=0)
                rivals = jnp.maximum(rivals, jnp.where(bids[at] == segment, -jnp.inf, best))
            rival = jnp.max(rivals, axis=0, keepdims=True)
            if last:
                margin[line, :] = (mine_in[line, :] + mine) - jnp.maximum(rival_in[line, :], rival)
                for span, write in zip(spans, writes[1:]):
                    if at + 1 == span.stop:
                        write.start()
            else:
                mine_out[line, :] = mine
                rival_out[line, :] = rival
    if last:
        for write in writes:
            write.wait()


def local(points, block_ids, slot_ids, live_blocks, old_centroids):
    row_count, feat_width = points.shape
    blocks = row_count // SLOT
    shards = lax.axis_size("shard")
    subs = lax.axis_size("sub")
    rows, width = old_centroids.shape
    half_rows = rows // 2
    total = rows * shards
    top = POINT_LIMIT * (row_count * shards * subs + prior_weight)
    rate = code_rate(math.ceil(math.log2(top)))
    slots = slot_ids.reshape(blocks, SLOT)
    chips = near_group(subs, shards)
    bits = late_bits(shards)
    late = 1 << len(bits)
    group = 2 if blocks % 2 == 0 else 1
    parts = [count for count in (blocks // 2, blocks // 3, blocks - blocks // 2 - blocks // 3) if count]
    limit = pltpu.CompilerParams(vmem_limit_bytes=8 * MIB + 4 * total * feat_width)
    smem = pl.BlockSpec(memory_space=pltpu.SMEM)
    vmem = pl.BlockSpec(memory_space=pltpu.VMEM)
    hbm = pl.BlockSpec(memory_space=pltpu.HBM)

    def swap(value, over_sub, over_shard):
        pairs = []
        for shard in range(shards):
            for sub in range(subs):
                pairs.append((shard * subs + sub, (shard ^ over_shard) * subs + (sub ^ over_sub)))
        return lax.ppermute(value, ("shard", "sub"), pairs)

    def in_hbm(value):
        return pltpu.with_memory_space_constraint(value, pltpu.HBM)

    shape = jax.ShapeDtypeStruct((len(chips), late, half_rows, width), jnp.float32)
    cost = pl.CostEstimate(flops=row_count * SLOT * feat_width, bytes_accessed=row_count * feat_width, transcendentals=0)
    sizes = dict(blocks=blocks, shards=shards, subs=subs, width=width)
    *send, held = pl.pallas_call(
        functools.partial(send_kernel, parts=parts, **sizes),
        out_shape=(shape, shape, jax.ShapeDtypeStruct(points.shape, points.dtype)),
        in_specs=[hbm] * 4,
        out_specs=(vmem, vmem, vmem),
        scratch_shapes=[
            pltpu.SMEM((1,), jnp.int32),
            pltpu.SMEM((blocks,), jnp.int32),
            pltpu.VMEM((blocks, SLOT), jnp.int32),
            pltpu.SemaphoreType.DMA((3,)),
            pltpu.SemaphoreType.DMA((len(parts),)),
        ],
        compiler_params=limit,
        cost_estimate=cost,
        name="sums_send",
    )(live_blocks, in_hbm(block_ids), in_hbm(slots), in_hbm(points))
    crossed = [swap(sums, 1, 0) for sums in send]
    keep = pl.pallas_call(
        functools.partial(keep_kernel, **sizes),
        out_shape=(shape, shape),
        in_specs=[smem, smem, vmem, vmem, vmem],
        out_specs=(vmem, vmem),
        compiler_params=limit,
        cost_estimate=cost,
        name="sums_keep",
    )(live_blocks, block_ids, slots, old_centroids, held)

    piece = (late, half_rows, width)
    two = (2, half_rows, width)

    def after(value, *others):
        return lax.optimization_barrier((value, *others))[0] if others else value

    def reduce_near(half, *earlier):
        there = after(crossed[half], *earlier)
        codes = [encode(keep[half][index] + there[index], rate) for index in range(1, len(chips))]
        return codes, [swap(code, *chip) for code, chip in zip(codes, chips[1:])]

    def reduce_late(half, terms, *earlier):
        mine, code = pl.pallas_call(
            functools.partial(mix_kernel, rate=rate),
            out_shape=(jax.ShapeDtypeStruct(piece, jnp.float32), jax.ShapeDtypeStruct(piece, jnp.int16)),
            compiler_params=limit,
            name=f"mix{half}",
        )(after(keep[half], *earlier), crossed[half], *terms)
        for bit in bits[:-1]:
            count = mine.shape[0] // 2
            mine = mine[:count] + decode(swap(encode(mine[count:], rate), 0, bit), rate)
            code = encode(mine, rate)
        return mine, swap(code, 0, bits[-1])

    def finish(half, mine, there, *earlier):
        own, code = pl.pallas_call(
            functools.partial(finish_kernel, rate=rate),
            out_shape=(
                jax.ShapeDtypeStruct((half_rows, width), jnp.float32),
                jax.ShapeDtypeStruct(two, jnp.int16),
            ),
            compiler_params=limit,
            name=f"finish{half}",
        )(after(mine, *earlier), there)
        for bit in reversed(bits[:-1]):
            code = jnp.concatenate([code, swap(code, 0, bit)])
        return own, code

    def rows_of(half, own, near, far):
        return pl.pallas_call(
            functools.partial(
                rows_kernel, shards=shards, subs=subs, rows=rows, width=width, rate=rate
            ),
            out_shape=(
                jax.ShapeDtypeStruct((half_rows, width), jnp.bfloat16),
                jax.ShapeDtypeStruct((total // 2, feat_width), jnp.bfloat16),
            ),
            compiler_params=limit,
            name=f"rows{half}",
        )(own, *near, *far)

    def scores(half, last, cents, *earlier):
        line = jax.ShapeDtypeStruct((blocks, SLOT), jnp.float32)
        fresh = jax.ShapeDtypeStruct((rows, width), jnp.bfloat16)
        return pl.pallas_call(
            functools.partial(
                score_kernel, half=half, last=last, blocks=blocks, shards=shards, rows=rows, group=group
            ),
            out_shape=(fresh, line) if last else (line, line),
            in_specs=[smem] + [vmem] * (3 + len(earlier)),
            out_specs=(hbm, hbm) if last else (vmem, vmem),
            scratch_shapes=[
                pltpu.VMEM((rows, width), jnp.bfloat16),
                pltpu.VMEM((blocks, SLOT), jnp.float32),
                pltpu.SemaphoreType.DMA((3,)),
            ]
            if last
            else [],
            compiler_params=limit,
            cost_estimate=pl.CostEstimate(
                flops=row_count * total * feat_width,
                bytes_accessed=2 * row_count * feat_width,
                transcendentals=0,
            ),
            name=f"scores{half}",
        )(block_ids, slots, held, cents, *earlier)

    first_codes, first_terms = reduce_near(0)
    _, second_terms = reduce_near(1, *first_codes)
    first = reduce_late(0, first_terms)
    second = reduce_late(1, second_terms, first[0])
    first_own, first_code = finish(0, *first)
    second_own, second_code = finish(1, *second, first_code)
    own, codes = (first_own, second_own), (first_code, second_code)
    near = jnp.concatenate([codes[0], swap(codes[0], 2, 0)])
    near = [jnp.concatenate([near, swap(near, 0, 1)])]
    blocks_near = [codes[1]] + [swap(codes[1], *chip) for chip in chips[1:]]
    second_fresh, second_rows = rows_of(1, own[1], blocks_near, [swap(block, 1, 0) for block in blocks_near])
    mine, rival = scores(1, False, second_rows)
    first_near = after(near[0], second_fresh)
    first_fresh, first_rows = rows_of(0, own[0], [first_near], [swap(first_near, 1, 0)])
    fresh, margin = scores(0, True, first_rows, mine, rival, first_fresh, second_fresh)
    return fresh, margin.reshape(row_count)


def solution(mesh):
    return jax.shard_map(
        local,
        mesh=mesh,
        in_specs=(
            P(("groups", "shard", "sub"), None),
            P(("groups", "shard", "sub")),
            P(("groups", "shard", "sub")),
            P(("groups", "shard", "sub")),
            P(("groups", "shard"), "sub"),
        ),
        out_specs=(P(("groups", "shard"), "sub"), P(("groups", "shard", "sub"))),
        check_vma=False,
    )
```

```python
import functools
import math

import jax
import jax.numpy as jnp
from jax import lax
from jax.experimental import pallas as pl
from jax.experimental.pallas import tpu as pltpu
from jax.sharding import PartitionSpec as P

SLOT = 128
POINT_LIMIT = 6.0

prior_weight = 4.0
norm_eps = 1e-06

LOW_EXP = -32
MIB = 1 << 20


def code_rate(top_exp):
    return 32767.0 / (top_exp - LOW_EXP)


def encode(value, rate):
    size = jnp.maximum(jnp.abs(value), 2.0**LOW_EXP)
    level = jnp.floor((jnp.log2(size) - LOW_EXP) * rate + 0.5)
    return jnp.where(value < 0.0, -level, level).astype(jnp.int32).astype(jnp.int16)


def decode(code, rate):
    level = code.astype(jnp.int32).astype(jnp.float32)
    size = jnp.exp2(jnp.abs(level) * (1.0 / rate) + LOW_EXP)
    return jnp.where(level < 0.0, -size, size)


def bits_of(count):
    return [1 << bit for bit in range(count.bit_length() - 1)]


def near_group(subs, shards):
    group = [(0, 0)]
    for bit in bits_of(subs)[1:]:
        group = group + [(sub ^ bit, shard) for sub, shard in group]
    group = group + [(sub, shard ^ 1) for sub, shard in group]
    return group


def late_bits(shards):
    return bits_of(shards)[1:]


def late_place(bits, over_shard):
    place = 0
    for bit in bits:
        place = place * 2 + (over_shard // bit) % 2
    return place


def add_block(halves, hot, rows_of, over_shard, *, sub, subs, shards, width, flip):
    group = near_group(subs, shards)
    late = late_place(late_bits(shards), over_shard)
    for over_sub in range(0, subs, 2):
        column = pl.multiple_of((sub ^ over_sub ^ flip) * width, width)
        part = jnp.dot(hot, rows_of(pl.ds(column, width)), preferred_element_type=jnp.float32)
        at = jnp.where(over_shard % 2 == 0, group.index((over_sub, 0)), group.index((over_sub, 1)))
        half_rows = part.shape[0] // 2
        halves[0][at, late] += part[:half_rows]
        halves[1][at, late] += part[half_rows:]


def hot_rows(slots, block, live):
    slot = jnp.where(block < live, slots[block : block + 1, :], -1)
    return (slot == lax.broadcasted_iota(jnp.int32, (SLOT, SLOT), 0)).astype(jnp.bfloat16)


def send_kernel(
    live_in, bids_in, slots_in, points, first_half, second_half, held, live, bids, slots, small, arrived, *, blocks, parts, shards, subs, width
):
    sub, shard = lax.axis_index("sub"), lax.axis_index("shard")
    firsts = [
        pltpu.make_async_copy(live_in, live, small.at[0]),
        pltpu.make_async_copy(bids_in, bids, small.at[1]),
        pltpu.make_async_copy(slots_in, slots, small.at[2]),
    ]
    for copy in firsts:
        copy.start()
    copies = {}
    first = 0
    for part, count in enumerate(parts):
        span = pl.ds(first * SLOT, count * SLOT)
        copies[first] = pltpu.make_async_copy(points.at[span], held.at[span], arrived.at[part])
        copies[first].start(priority=part % 2)
        first += count
    for sums in (first_half, second_half):
        sums[...] = jnp.zeros_like(sums)
    for copy in firsts:
        copy.wait()
    for block in range(blocks):
        if block in copies:
            copies[block].wait()
        span = slice(block * SLOT, (block + 1) * SLOT)
        add_block(
            (first_half, second_half),
            hot_rows(slots, block, live[0]),
            lambda column, span=span: held[span, column],
            bids[block] ^ shard,
            sub=sub,
            subs=subs,
            shards=shards,
            width=width,
            flip=1,
        )


def keep_kernel(live, bids, slots, old, points, first_half, second_half, *, blocks, shards, subs, width):
    sub, shard = lax.axis_index("sub"), lax.axis_index("shard")
    prior = prior_weight * old[...].astype(jnp.float32)
    half_rows = prior.shape[0] // 2
    for half, sums in enumerate((first_half, second_half)):
        sums[...] = jnp.zeros_like(sums)
        sums[0, 0] = prior[half * half_rows : (half + 1) * half_rows]
    for block in range(blocks):
        span = slice(block * SLOT, (block + 1) * SLOT)
        add_block(
            (first_half, second_half),
            hot_rows(slots, block, live[0]),
            lambda column, span=span: points[span, column],
            bids[block] ^ shard,
            sub=sub,
            subs=subs,
            shards=shards,
            width=width,
            flip=0,
        )


def mix_kernel(keep, crossed, *refs, rate):
    terms, (mine, code) = refs[:-2], refs[-2:]
    total = keep[0] + crossed[0]
    for term in terms:
        total = total + decode(term[...], rate)
    mine[...] = total
    code[...] = encode(total, rate)


def finish_kernel(mine, there, own, code, *, rate):
    own[...] = mine[0] + decode(there[1], rate)
    code[0] = encode(own[...], rate)
    code[1] = encode(mine[1] + decode(there[0], rate), rate)


def rows_kernel(own, *refs, shards, subs, rows, width, rate):
    chips = near_group(subs, shards)
    sub, shard = lax.axis_index("sub"), lax.axis_index("shard")
    bits = late_bits(shards)
    late_count = 1 << len(bits)
    half_rows = rows // 2
    fresh, cents = refs[-2:]
    count = (len(refs) - 2) // 2
    near, far = refs[:count], refs[count : 2 * count]

    def piece_of(blocks, piece):
        each = blocks[0].shape[0]
        return decode(blocks[piece // each][piece % each], rate)

    for over_shard in range(shards):
        parts = []
        for over_sub in range(0, subs, 2):
            piece = chips.index((over_sub, over_shard % 2)) * late_count + late_place(bits, over_shard)
            parts.append((sub ^ over_sub, piece_of(near, piece)))
            parts.append((sub ^ 1 ^ over_sub, piece_of(far, piece)))
        squares = sum(jnp.sum(part * part, axis=1, keepdims=True) for _, part in parts)
        scale = lax.rsqrt(squares + norm_eps)
        row = pl.ds(pl.multiple_of((shard ^ over_shard) * half_rows, half_rows), half_rows)
        for place, part in parts:
            cents[row, pl.ds(pl.multiple_of(place * width, width), width)] = (part * scale).astype(jnp.bfloat16)
        if over_shard == 0:
            fresh[...] = (own[...] * scale).astype(jnp.bfloat16)


def score_kernel(bids, slots, points, cents, *refs, half, last, blocks, shards, rows, group):
    if last:
        mine_in, rival_in, fresh_first, fresh_second, fresh, margin = refs
        fresh[: rows // 2] = fresh_first[...]
        fresh[rows // 2 :] = fresh_second[...]
    else:
        mine_out, rival_out = refs
    half_rows = rows // 2
    lanes = 8
    row_of = lax.broadcasted_iota(jnp.int32, (half_rows, SLOT), 0)
    for block in range(blocks // group):
        score = lax.dot_general(
            cents[...],
            points[block * group * SLOT : (block + 1) * group * SLOT, :],
            (((1,), (1,)), ((), ())),
            preferred_element_type=jnp.float32,
        )
        for inner in range(group):
            at = block * group + inner
            line = slice(at, at + 1)
            part = score[:, inner * SLOT : (inner + 1) * SLOT].reshape(shards, half_rows, SLOT)
            own_part = part[0]
            for segment in range(1, shards):
                own_part = jnp.where(bids[at] == segment, part[segment], own_part)
            hit = row_of == slots[line, :] - half * half_rows
            mine = jnp.sum(jnp.where(hit, own_part, 0.0), axis=0, keepdims=True)
            rivals = jnp.where(hit, -jnp.inf, own_part).reshape(half_rows // lanes, lanes, SLOT).max(axis=0)
            for segment in range(shards):
                best = part[segment].reshape(half_rows // lanes, lanes, SLOT).max(axis=0)
                rivals = jnp.maximum(rivals, jnp.where(bids[at] == segment, -jnp.inf, best))
            rival = jnp.max(rivals, axis=0, keepdims=True)
            if last:
                margin[line, :] = (mine_in[line, :] + mine) - jnp.maximum(rival_in[line, :], rival)
            else:
                mine_out[line, :] = mine
                rival_out[line, :] = rival


def local(points, block_ids, slot_ids, live_blocks, old_centroids):
    row_count, feat_width = points.shape
    blocks = row_count // SLOT
    shards = lax.axis_size("shard")
    subs = lax.axis_size("sub")
    rows, width = old_centroids.shape
    half_rows = rows // 2
    total = rows * shards
    top = POINT_LIMIT * (row_count * shards * subs + prior_weight)
    rate = code_rate(math.ceil(math.log2(top)))
    slots = slot_ids.reshape(blocks, SLOT)
    chips = near_group(subs, shards)
    bits = late_bits(shards)
    late = 1 << len(bits)
    group = 2 if blocks % 2 == 0 else 1
    parts = [count for count in (blocks // 2, blocks // 3, blocks - blocks // 2 - blocks // 3) if count]
    limit = pltpu.CompilerParams(vmem_limit_bytes=8 * MIB + 4 * total * feat_width)
    smem = pl.BlockSpec(memory_space=pltpu.SMEM)
    vmem = pl.BlockSpec(memory_space=pltpu.VMEM)
    hbm = pl.BlockSpec(memory_space=pltpu.HBM)

    def swap(value, over_sub, over_shard):
        pairs = []
        for shard in range(shards):
            for sub in range(subs):
                pairs.append((shard * subs + sub, (shard ^ over_shard) * subs + (sub ^ over_sub)))
        return lax.ppermute(value, ("shard", "sub"), pairs)

    def in_hbm(value):
        return pltpu.with_memory_space_constraint(value, pltpu.HBM)

    shape = jax.ShapeDtypeStruct((len(chips), late, half_rows, width), jnp.float32)
    cost = pl.CostEstimate(flops=row_count * SLOT * feat_width, bytes_accessed=row_count * feat_width, transcendentals=0)
    sizes = dict(blocks=blocks, shards=shards, subs=subs, width=width)
    *send, held = pl.pallas_call(
        functools.partial(send_kernel, parts=parts, **sizes),
        out_shape=(shape, shape, jax.ShapeDtypeStruct(points.shape, points.dtype)),
        in_specs=[hbm] * 4,
        out_specs=(vmem, vmem, vmem),
        scratch_shapes=[
            pltpu.SMEM((1,), jnp.int32),
            pltpu.SMEM((blocks,), jnp.int32),
            pltpu.VMEM((blocks, SLOT), jnp.int32),
            pltpu.SemaphoreType.DMA((3,)),
            pltpu.SemaphoreType.DMA((len(parts),)),
        ],
        compiler_params=limit,
        cost_estimate=cost,
        name="sums_send",
    )(live_blocks, in_hbm(block_ids), in_hbm(slots), in_hbm(points))
    crossed = [swap(sums, 1, 0) for sums in send]
    keep = pl.pallas_call(
        functools.partial(keep_kernel, **sizes),
        out_shape=(shape, shape),
        in_specs=[smem, smem, vmem, vmem, vmem],
        out_specs=(vmem, vmem),
        compiler_params=limit,
        cost_estimate=cost,
        name="sums_keep",
    )(live_blocks, block_ids, slots, old_centroids, held)

    piece = (late, half_rows, width)
    two = (2, half_rows, width)

    def after(value, *others):
        return lax.optimization_barrier((value, *others))[0] if others else value

    def reduce_near(half, *earlier):
        there = after(crossed[half], *earlier)
        codes = [encode(keep[half][index] + there[index], rate) for index in range(1, len(chips))]
        return codes, [swap(code, *chip) for code, chip in zip(codes, chips[1:])]

    def reduce_late(half, terms, *earlier):
        mine, code = pl.pallas_call(
            functools.partial(mix_kernel, rate=rate),
            out_shape=(jax.ShapeDtypeStruct(piece, jnp.float32), jax.ShapeDtypeStruct(piece, jnp.int16)),
            compiler_params=limit,
            name=f"mix{half}",
        )(after(keep[half], *earlier), crossed[half], *terms)
        for bit in bits[:-1]:
            count = mine.shape[0] // 2
            mine = mine[:count] + decode(swap(encode(mine[count:], rate), 0, bit), rate)
            code = encode(mine, rate)
        return mine, swap(code, 0, bits[-1])

    def finish(half, mine, there, *earlier):
        own, code = pl.pallas_call(
            functools.partial(finish_kernel, rate=rate),
            out_shape=(
                jax.ShapeDtypeStruct((half_rows, width), jnp.float32),
                jax.ShapeDtypeStruct(two, jnp.int16),
            ),
            compiler_params=limit,
            name=f"finish{half}",
        )(after(mine, *earlier), there)
        for bit in reversed(bits[:-1]):
            code = jnp.concatenate([code, swap(code, 0, bit)])
        return own, code

    def rows_of(half, own, near, far):
        return pl.pallas_call(
            functools.partial(
                rows_kernel, shards=shards, subs=subs, rows=rows, width=width, rate=rate
            ),
            out_shape=(
                jax.ShapeDtypeStruct((half_rows, width), jnp.bfloat16),
                jax.ShapeDtypeStruct((total // 2, feat_width), jnp.bfloat16),
            ),
            compiler_params=limit,
            name=f"rows{half}",
        )(own, *near, *far)

    def scores(half, last, cents, *earlier):
        line = jax.ShapeDtypeStruct((blocks, SLOT), jnp.float32)
        fresh = jax.ShapeDtypeStruct((rows, width), jnp.bfloat16)
        return pl.pallas_call(
            functools.partial(
                score_kernel, half=half, last=last, blocks=blocks, shards=shards, rows=rows, group=group
            ),
            out_shape=(fresh, line) if last else (line, line),
            in_specs=[smem] + [vmem] * (3 + len(earlier)),
            out_specs=(vmem, vmem),
            compiler_params=limit,
            cost_estimate=pl.CostEstimate(
                flops=row_count * total * feat_width,
                bytes_accessed=2 * row_count * feat_width,
                transcendentals=0,
            ),
            name=f"scores{half}",
        )(block_ids, slots, held, cents, *earlier)

    first_codes, first_terms = reduce_near(0)
    _, second_terms = reduce_near(1, *first_codes)
    first = reduce_late(0, first_terms)
    second = reduce_late(1, second_terms, first[0])
    first_own, first_code = finish(0, *first)
    second_own, second_code = finish(1, *second, first_code)
    own, codes = (first_own, second_own), (first_code, second_code)
    by_x = swap(codes[0], 2, 0)
    by_z = swap(codes[0], 0, 1)
    near = [jnp.concatenate([codes[0], by_x, by_z, swap(by_x, 0, 1)])]
    ready = [codes[1], codes[1], codes[1]]
    blocks_near = [codes[1]] + [swap(code, *chip) for code, chip in zip(ready, chips[1:])]
    second_fresh, second_rows = rows_of(1, own[1], blocks_near, [swap(block, 1, 0) for block in blocks_near])
    mine, rival = scores(1, False, second_rows)
    first_near = after(near[0], second_fresh)
    first_fresh, first_rows = rows_of(0, own[0], [first_near], [swap(first_near, 1, 0)])
    fresh, margin = scores(0, True, first_rows, mine, rival, first_fresh, second_fresh)
    return fresh, margin.reshape(row_count)


def solution(mesh):
    return jax.shard_map(
        local,
        mesh=mesh,
        in_specs=(
            P(("groups", "shard", "sub"), None),
            P(("groups", "shard", "sub")),
            P(("groups", "shard", "sub")),
            P(("groups", "shard", "sub")),
            P(("groups", "shard"), "sub"),
        ),
        out_specs=(P(("groups", "shard"), "sub"), P(("groups", "shard", "sub"))),
        check_vma=False,
    )
```

```python
import functools
import math

import jax
import jax.numpy as jnp
from jax import lax
from jax.experimental import pallas as pl
from jax.experimental.pallas import tpu as pltpu
from jax.sharding import PartitionSpec as P

SLOT = 128
POINT_LIMIT = 6.0

prior_weight = 4.0
norm_eps = 1e-06

LOW_EXP = -32
MIB = 1 << 20


def code_rate(top_exp):
    return 32767.0 / (top_exp - LOW_EXP)


def encode(value, rate):
    size = jnp.maximum(jnp.abs(value), 2.0**LOW_EXP)
    level = jnp.floor((jnp.log2(size) - LOW_EXP) * rate + 0.5)
    return jnp.where(value < 0.0, -level, level).astype(jnp.int32).astype(jnp.int16)


def decode(code, rate):
    level = code.astype(jnp.int32).astype(jnp.float32)
    size = jnp.exp2(jnp.abs(level) * (1.0 / rate) + LOW_EXP)
    return jnp.where(level < 0.0, -size, size)


def bits_of(count):
    return [1 << bit for bit in range(count.bit_length() - 1)]


def near_group(subs, shards):
    group = [(0, 0)]
    for bit in bits_of(subs)[1:]:
        group = group + [(sub ^ bit, shard) for sub, shard in group]
    group = group + [(sub, shard ^ 1) for sub, shard in group]
    return group


def late_bits(shards):
    return bits_of(shards)[1:]


def late_place(bits, over_shard):
    place = 0
    for bit in bits:
        place = place * 2 + (over_shard // bit) % 2
    return place


def add_block(halves, hot, rows_of, over_shard, *, sub, subs, shards, width, flip):
    group = near_group(subs, shards)
    late = late_place(late_bits(shards), over_shard)
    for over_sub in range(0, subs, 2):
        column = pl.multiple_of((sub ^ over_sub ^ flip) * width, width)
        part = jnp.dot(hot, rows_of(pl.ds(column, width)), preferred_element_type=jnp.float32)
        at = jnp.where(over_shard % 2 == 0, group.index((over_sub, 0)), group.index((over_sub, 1)))
        half_rows = part.shape[0] // 2
        halves[0][at, late] += part[:half_rows]
        halves[1][at, late] += part[half_rows:]


def hot_rows(slots, block, live):
    slot = jnp.where(block < live, slots[block : block + 1, :], -1)
    return (slot == lax.broadcasted_iota(jnp.int32, (SLOT, SLOT), 0)).astype(jnp.bfloat16)


def send_kernel(
    live_in, bids_in, slots_in, points, first_half, second_half, held, live, bids, slots, small, arrived, *, blocks, parts, shards, subs, width
):
    sub, shard = lax.axis_index("sub"), lax.axis_index("shard")
    firsts = [
        pltpu.make_async_copy(live_in, live, small.at[0]),
        pltpu.make_async_copy(bids_in, bids, small.at[1]),
        pltpu.make_async_copy(slots_in, slots, small.at[2]),
    ]
    for copy in firsts:
        copy.start()
    copies = {}
    first = 0
    for part, count in enumerate(parts):
        copies[first] = []
        half = count * SLOT // 2
        for side in range(2):
            span = pl.ds(first * SLOT + side * half, half)
            copy = pltpu.make_async_copy(points.at[span], held.at[span], arrived.at[2 * part + side])
            copy.start(priority=side)
            copies[first].append(copy)
        first += count
    for sums in (first_half, second_half):
        sums[...] = jnp.zeros_like(sums)
    for copy in firsts:
        copy.wait()
    for block in range(blocks):
        for copy in copies.get(block, ()):
            copy.wait()
        span = slice(block * SLOT, (block + 1) * SLOT)
        add_block(
            (first_half, second_half),
            hot_rows(slots, block, live[0]),
            lambda column, span=span: held[span, column],
            bids[block] ^ shard,
            sub=sub,
            subs=subs,
            shards=shards,
            width=width,
            flip=1,
        )


def keep_kernel(live, bids, slots, old, points, first_half, second_half, *, blocks, shards, subs, width):
    sub, shard = lax.axis_index("sub"), lax.axis_index("shard")
    prior = prior_weight * old[...].astype(jnp.float32)
    half_rows = prior.shape[0] // 2
    for half, sums in enumerate((first_half, second_half)):
        sums[...] = jnp.zeros_like(sums)
        sums[0, 0] = prior[half * half_rows : (half + 1) * half_rows]
    for block in range(blocks):
        span = slice(block * SLOT, (block + 1) * SLOT)
        add_block(
            (first_half, second_half),
            hot_rows(slots, block, live[0]),
            lambda column, span=span: points[span, column],
            bids[block] ^ shard,
            sub=sub,
            subs=subs,
            shards=shards,
            width=width,
            flip=0,
        )


def mix_kernel(keep, crossed, *refs, rate):
    terms, (mine, code) = refs[:-2], refs[-2:]
    total = keep[0] + crossed[0]
    for term in terms:
        total = total + decode(term[...], rate)
    mine[...] = total
    code[...] = encode(total, rate)


def finish_kernel(mine, there, own, code, *, rate):
    own[...] = mine[0] + decode(there[1], rate)
    code[0] = encode(own[...], rate)
    code[1] = encode(mine[1] + decode(there[0], rate), rate)


def rows_kernel(own, *refs, shards, subs, rows, width, rate):
    chips = near_group(subs, shards)
    sub, shard = lax.axis_index("sub"), lax.axis_index("shard")
    bits = late_bits(shards)
    late_count = 1 << len(bits)
    half_rows = rows // 2
    fresh, cents = refs[-2:]
    count = (len(refs) - 2) // 2
    near, far = refs[:count], refs[count : 2 * count]

    def piece_of(blocks, piece):
        each = blocks[0].shape[0]
        return decode(blocks[piece // each][piece % each], rate)

    for over_shard in range(shards):
        parts = []
        for over_sub in range(0, subs, 2):
            piece = chips.index((over_sub, over_shard % 2)) * late_count + late_place(bits, over_shard)
            parts.append((sub ^ over_sub, piece_of(near, piece)))
            parts.append((sub ^ 1 ^ over_sub, piece_of(far, piece)))
        squares = sum(jnp.sum(part * part, axis=1, keepdims=True) for _, part in parts)
        scale = lax.rsqrt(squares + norm_eps)
        row = pl.ds(pl.multiple_of((shard ^ over_shard) * half_rows, half_rows), half_rows)
        for place, part in parts:
            cents[row, pl.ds(pl.multiple_of(place * width, width), width)] = (part * scale).astype(jnp.bfloat16)
        if over_shard == 0:
            fresh[...] = (own[...] * scale).astype(jnp.bfloat16)


def score_kernel(bids, slots, points, cents, *refs, half, last, blocks, shards, rows, group):
    if last:
        mine_in, rival_in, fresh_first, fresh_second, fresh, margin = refs
        fresh[: rows // 2] = fresh_first[...]
        fresh[rows // 2 :] = fresh_second[...]
    else:
        mine_out, rival_out = refs
    half_rows = rows // 2
    lanes = 8
    row_of = lax.broadcasted_iota(jnp.int32, (half_rows, SLOT), 0)
    for block in range(blocks // group):
        score = lax.dot_general(
            cents[...],
            points[block * group * SLOT : (block + 1) * group * SLOT, :],
            (((1,), (1,)), ((), ())),
            preferred_element_type=jnp.float32,
        )
        for inner in range(group):
            at = block * group + inner
            line = slice(at, at + 1)
            part = score[:, inner * SLOT : (inner + 1) * SLOT].reshape(shards, half_rows, SLOT)
            own_part = part[0]
            for segment in range(1, shards):
                own_part = jnp.where(bids[at] == segment, part[segment], own_part)
            hit = row_of == slots[line, :] - half * half_rows
            mine = jnp.sum(jnp.where(hit, own_part, 0.0), axis=0, keepdims=True)
            rivals = jnp.where(hit, -jnp.inf, own_part).reshape(half_rows // lanes, lanes, SLOT).max(axis=0)
            for segment in range(shards):
                best = part[segment].reshape(half_rows // lanes, lanes, SLOT).max(axis=0)
                rivals = jnp.maximum(rivals, jnp.where(bids[at] == segment, -jnp.inf, best))
            rival = jnp.max(rivals, axis=0, keepdims=True)
            if last:
                margin[line, :] = (mine_in[line, :] + mine) - jnp.maximum(rival_in[line, :], rival)
            else:
                mine_out[line, :] = mine
                rival_out[line, :] = rival


def local(points, block_ids, slot_ids, live_blocks, old_centroids):
    row_count, feat_width = points.shape
    blocks = row_count // SLOT
    shards = lax.axis_size("shard")
    subs = lax.axis_size("sub")
    rows, width = old_centroids.shape
    half_rows = rows // 2
    total = rows * shards
    top = POINT_LIMIT * (row_count * shards * subs + prior_weight)
    rate = code_rate(math.ceil(math.log2(top)))
    slots = slot_ids.reshape(blocks, SLOT)
    chips = near_group(subs, shards)
    bits = late_bits(shards)
    late = 1 << len(bits)
    group = 2 if blocks % 2 == 0 else 1
    third = blocks // 3
    parts = [count for count in (third, blocks - 2 * third + 1, third - 1) if count > 0]
    limit = pltpu.CompilerParams(vmem_limit_bytes=8 * MIB + 4 * total * feat_width)
    smem = pl.BlockSpec(memory_space=pltpu.SMEM)
    vmem = pl.BlockSpec(memory_space=pltpu.VMEM)
    hbm = pl.BlockSpec(memory_space=pltpu.HBM)

    def swap(value, over_sub, over_shard):
        pairs = []
        for shard in range(shards):
            for sub in range(subs):
                pairs.append((shard * subs + sub, (shard ^ over_shard) * subs + (sub ^ over_sub)))
        return lax.ppermute(value, ("shard", "sub"), pairs)

    def in_hbm(value):
        return pltpu.with_memory_space_constraint(value, pltpu.HBM)

    shape = jax.ShapeDtypeStruct((len(chips), late, half_rows, width), jnp.float32)
    cost = pl.CostEstimate(flops=row_count * SLOT * feat_width, bytes_accessed=row_count * feat_width, transcendentals=0)
    sizes = dict(blocks=blocks, shards=shards, subs=subs, width=width)
    *send, held = pl.pallas_call(
        functools.partial(send_kernel, parts=parts, **sizes),
        out_shape=(shape, shape, jax.ShapeDtypeStruct(points.shape, points.dtype)),
        in_specs=[hbm] * 4,
        out_specs=(vmem, vmem, vmem),
        scratch_shapes=[
            pltpu.SMEM((1,), jnp.int32),
            pltpu.SMEM((blocks,), jnp.int32),
            pltpu.VMEM((blocks, SLOT), jnp.int32),
            pltpu.SemaphoreType.DMA((3,)),
            pltpu.SemaphoreType.DMA((2 * len(parts),)),
        ],
        compiler_params=limit,
        cost_estimate=cost,
        name="sums_send",
    )(live_blocks, in_hbm(block_ids), in_hbm(slots), in_hbm(points))
    crossed = [swap(sums, 1, 0) for sums in send]
    keep = pl.pallas_call(
        functools.partial(keep_kernel, **sizes),
        out_shape=(shape, shape),
        in_specs=[smem, smem, vmem, vmem, vmem],
        out_specs=(vmem, vmem),
        compiler_params=limit,
        cost_estimate=cost,
        name="sums_keep",
    )(live_blocks, block_ids, slots, old_centroids, held)

    piece = (late, half_rows, width)
    two = (2, half_rows, width)

    def after(value, *others):
        return lax.optimization_barrier((value, *others))[0] if others else value

    def reduce_near(half, *earlier):
        there = after(crossed[half], *earlier)
        codes = [encode(keep[half][index] + there[index], rate) for index in range(1, len(chips))]
        return codes, [swap(code, *chip) for code, chip in zip(codes, chips[1:])]

    def reduce_late(half, terms, *earlier):
        mine, code = pl.pallas_call(
            functools.partial(mix_kernel, rate=rate),
            out_shape=(jax.ShapeDtypeStruct(piece, jnp.float32), jax.ShapeDtypeStruct(piece, jnp.int16)),
            compiler_params=limit,
            name=f"mix{half}",
        )(after(keep[half], *earlier), crossed[half], *terms)
        for bit in bits[:-1]:
            count = mine.shape[0] // 2
            mine = mine[:count] + decode(swap(encode(mine[count:], rate), 0, bit), rate)
            code = encode(mine, rate)
        return mine, swap(code, 0, bits[-1])

    def finish(half, mine, there, *earlier):
        own, code = pl.pallas_call(
            functools.partial(finish_kernel, rate=rate),
            out_shape=(
                jax.ShapeDtypeStruct((half_rows, width), jnp.float32),
                jax.ShapeDtypeStruct(two, jnp.int16),
            ),
            compiler_params=limit,
            name=f"finish{half}",
        )(after(mine, *earlier), there)
        for bit in reversed(bits[:-1]):
            code = jnp.concatenate([code, swap(code, 0, bit)])
        return own, code

    def rows_of(half, own, near, far):
        return pl.pallas_call(
            functools.partial(
                rows_kernel, shards=shards, subs=subs, rows=rows, width=width, rate=rate
            ),
            out_shape=(
                jax.ShapeDtypeStruct((half_rows, width), jnp.bfloat16),
                jax.ShapeDtypeStruct((total // 2, feat_width), jnp.bfloat16),
            ),
            compiler_params=limit,
            name=f"rows{half}",
        )(own, *near, *far)

    def scores(half, last, cents, *earlier):
        line = jax.ShapeDtypeStruct((blocks, SLOT), jnp.float32)
        fresh = jax.ShapeDtypeStruct((rows, width), jnp.bfloat16)
        return pl.pallas_call(
            functools.partial(
                score_kernel, half=half, last=last, blocks=blocks, shards=shards, rows=rows, group=group
            ),
            out_shape=(fresh, line) if last else (line, line),
            in_specs=[smem] + [vmem] * (3 + len(earlier)),
            out_specs=(vmem, vmem),
            compiler_params=limit,
            cost_estimate=pl.CostEstimate(
                flops=row_count * total * feat_width,
                bytes_accessed=2 * row_count * feat_width,
                transcendentals=0,
            ),
            name=f"scores{half}",
        )(block_ids, slots, held, cents, *earlier)

    first_codes, first_terms = reduce_near(0)
    _, second_terms = reduce_near(1, *first_codes)
    first = reduce_late(0, first_terms)
    second = reduce_late(1, second_terms, first[0])
    first_own, first_code = finish(0, *first)
    second_own, second_code = finish(1, *second, first_code)
    own, codes = (first_own, second_own), (first_code, second_code)
    near = jnp.concatenate([codes[0], swap(codes[0], 2, 0)])
    near = [jnp.concatenate([near, swap(near, 0, 1)])]
    blocks_near = [codes[1]] + [swap(codes[1], *chip) for chip in chips[1:]]
    second_fresh, second_rows = rows_of(1, own[1], blocks_near, [swap(block, 1, 0) for block in blocks_near])
    mine, rival = scores(1, False, second_rows)
    first_near = after(near[0], second_fresh)
    first_fresh, first_rows = rows_of(0, own[0], [first_near], [swap(first_near, 1, 0)])
    fresh, margin = scores(0, True, first_rows, mine, rival, first_fresh, second_fresh)
    return fresh, margin.reshape(row_count)


def solution(mesh):
    return jax.shard_map(
        local,
        mesh=mesh,
        in_specs=(
            P(("groups", "shard", "sub"), None),
            P(("groups", "shard", "sub")),
            P(("groups", "shard", "sub")),
            P(("groups", "shard", "sub")),
            P(("groups", "shard"), "sub"),
        ),
        out_specs=(P(("groups", "shard"), "sub"), P(("groups", "shard", "sub"))),
        check_vma=False,
    )
```

```python
import functools
import math

import jax
import jax.numpy as jnp
from jax import lax
from jax.experimental import pallas as pl
from jax.experimental.pallas import tpu as pltpu
from jax.sharding import PartitionSpec as P

SLOT = 128
POINT_LIMIT = 6.0

prior_weight = 4.0
norm_eps = 1e-06

LOW_EXP = -32
MIB = 1 << 20


def code_rate(top_exp):
    return 32767.0 / (top_exp - LOW_EXP)


def encode(value, rate):
    size = jnp.maximum(jnp.abs(value), 2.0**LOW_EXP)
    level = jnp.floor((jnp.log2(size) - LOW_EXP) * rate + 0.5)
    return jnp.where(value < 0.0, -level, level).astype(jnp.int32).astype(jnp.int16)


def decode(code, rate):
    level = code.astype(jnp.int32).astype(jnp.float32)
    size = jnp.exp2(jnp.abs(level) * (1.0 / rate) + LOW_EXP)
    return jnp.where(level < 0.0, -size, size)


def bits_of(count):
    return [1 << bit for bit in range(count.bit_length() - 1)]


def near_group(subs, shards):
    group = [(0, 0), (0, 1)]
    for bit in bits_of(subs)[1:]:
        group = group + [(sub ^ bit, shard) for sub, shard in group]
    return group


def late_bits(shards):
    return bits_of(shards)[1:]


def late_place(bits, over_shard):
    place = 0
    for bit in bits:
        place = place * 2 + (over_shard // bit) % 2
    return place


def add_block(halves, hot, rows_of, over_shard, *, sub, subs, shards, width, flip):
    group = near_group(subs, shards)
    late = late_place(late_bits(shards), over_shard)
    for over_sub in range(0, subs, 2):
        column = pl.multiple_of((sub ^ over_sub ^ flip) * width, width)
        part = jnp.dot(hot, rows_of(pl.ds(column, width)), preferred_element_type=jnp.float32)
        at = jnp.where(over_shard % 2 == 0, group.index((over_sub, 0)), group.index((over_sub, 1)))
        half_rows = part.shape[0] // 2
        halves[0][at, late] += part[:half_rows]
        halves[1][at, late] += part[half_rows:]


def hot_rows(slots, block, live):
    slot = jnp.where(block < live, slots[block : block + 1, :], -1)
    return (slot == lax.broadcasted_iota(jnp.int32, (SLOT, SLOT), 0)).astype(jnp.bfloat16)


def send_kernel(
    live_in, bids_in, slots_in, points, first_half, second_half, held, live, bids, slots, small, arrived, *, blocks, parts, shards, subs, width
):
    sub, shard = lax.axis_index("sub"), lax.axis_index("shard")
    firsts = [
        pltpu.make_async_copy(live_in, live, small.at[0]),
        pltpu.make_async_copy(bids_in, bids, small.at[1]),
        pltpu.make_async_copy(slots_in, slots, small.at[2]),
    ]
    for copy in firsts:
        copy.start()
    copies = {}
    first = 0
    for part, count in enumerate(parts):
        span = pl.ds(first * SLOT, count * SLOT)
        copies[first] = pltpu.make_async_copy(points.at[span], held.at[span], arrived.at[part])
        copies[first].start(priority=part % 2)
        first += count
    for sums in (first_half, second_half):
        sums[...] = jnp.zeros_like(sums)
    for copy in firsts:
        copy.wait()
    for block in range(blocks):
        if block in copies:
            copies[block].wait()
        span = slice(block * SLOT, (block + 1) * SLOT)
        add_block(
            (first_half, second_half),
            hot_rows(slots, block, live[0]),
            lambda column, span=span: held[span, column],
            bids[block] ^ shard,
            sub=sub,
            subs=subs,
            shards=shards,
            width=width,
            flip=1,
        )


def keep_kernel(live, bids, slots, old, points, first_half, second_half, *, blocks, shards, subs, width):
    sub, shard = lax.axis_index("sub"), lax.axis_index("shard")
    prior = prior_weight * old[...].astype(jnp.float32)
    half_rows = prior.shape[0] // 2
    for half, sums in enumerate((first_half, second_half)):
        sums[...] = jnp.zeros_like(sums)
        sums[0, 0] = prior[half * half_rows : (half + 1) * half_rows]
    for block in range(blocks):
        span = slice(block * SLOT, (block + 1) * SLOT)
        add_block(
            (first_half, second_half),
            hot_rows(slots, block, live[0]),
            lambda column, span=span: points[span, column],
            bids[block] ^ shard,
            sub=sub,
            subs=subs,
            shards=shards,
            width=width,
            flip=0,
        )


def mix_kernel(keep, crossed, *refs, rate):
    terms, (mine, code) = refs[:-2], refs[-2:]
    total = keep[0] + crossed[0]
    for term in terms:
        total = total + decode(term[...], rate)
    mine[...] = total
    code[...] = encode(total, rate)


def finish_kernel(mine, there, own, code, *, rate):
    own[...] = mine[0] + decode(there[1], rate)
    code[0] = encode(own[...], rate)
    code[1] = encode(mine[1] + decode(there[0], rate), rate)


def rows_kernel(own, *refs, shards, subs, rows, width, rate):
    chips = near_group(subs, shards)
    sub, shard = lax.axis_index("sub"), lax.axis_index("shard")
    bits = late_bits(shards)
    late_count = 1 << len(bits)
    half_rows = rows // 2
    fresh, cents = refs[-2:]
    count = (len(refs) - 2) // 2
    near, far = refs[:count], refs[count : 2 * count]

    def piece_of(blocks, piece):
        each = blocks[0].shape[0]
        return decode(blocks[piece // each][piece % each], rate)

    for over_shard in range(shards):
        parts = []
        for over_sub in range(0, subs, 2):
            piece = chips.index((over_sub, over_shard % 2)) * late_count + late_place(bits, over_shard)
            parts.append((sub ^ over_sub, piece_of(near, piece)))
            parts.append((sub ^ 1 ^ over_sub, piece_of(far, piece)))
        squares = sum(jnp.sum(part * part, axis=1, keepdims=True) for _, part in parts)
        scale = lax.rsqrt(squares + norm_eps)
        row = pl.ds(pl.multiple_of((shard ^ over_shard) * half_rows, half_rows), half_rows)
        for place, part in parts:
            cents[row, pl.ds(pl.multiple_of(place * width, width), width)] = (part * scale).astype(jnp.bfloat16)
        if over_shard == 0:
            fresh[...] = (own[...] * scale).astype(jnp.bfloat16)


def score_kernel(bids, slots, points, cents, *refs, half, last, blocks, shards, rows, group):
    if last:
        mine_in, rival_in, fresh_first, fresh_second, fresh, margin = refs
        fresh[: rows // 2] = fresh_first[...]
        fresh[rows // 2 :] = fresh_second[...]
    else:
        mine_out, rival_out = refs
    half_rows = rows // 2
    lanes = 8
    row_of = lax.broadcasted_iota(jnp.int32, (half_rows, SLOT), 0)
    for block in range(blocks // group):
        score = lax.dot_general(
            cents[...],
            points[block * group * SLOT : (block + 1) * group * SLOT, :],
            (((1,), (1,)), ((), ())),
            preferred_element_type=jnp.float32,
        )
        for inner in range(group):
            at = block * group + inner
            line = slice(at, at + 1)
            part = score[:, inner * SLOT : (inner + 1) * SLOT].reshape(shards, half_rows, SLOT)
            own_part = part[0]
            for segment in range(1, shards):
                own_part = jnp.where(bids[at] == segment, part[segment], own_part)
            hit = row_of == slots[line, :] - half * half_rows
            mine = jnp.sum(jnp.where(hit, own_part, 0.0), axis=0, keepdims=True)
            rivals = jnp.where(hit, -jnp.inf, own_part).reshape(half_rows // lanes, lanes, SLOT).max(axis=0)
            for segment in range(shards):
                best = part[segment].reshape(half_rows // lanes, lanes, SLOT).max(axis=0)
                rivals = jnp.maximum(rivals, jnp.where(bids[at] == segment, -jnp.inf, best))
            rival = jnp.max(rivals, axis=0, keepdims=True)
            if last:
                margin[line, :] = (mine_in[line, :] + mine) - jnp.maximum(rival_in[line, :], rival)
            else:
                mine_out[line, :] = mine
                rival_out[line, :] = rival


def local(points, block_ids, slot_ids, live_blocks, old_centroids):
    row_count, feat_width = points.shape
    blocks = row_count // SLOT
    shards = lax.axis_size("shard")
    subs = lax.axis_size("sub")
    rows, width = old_centroids.shape
    half_rows = rows // 2
    total = rows * shards
    top = POINT_LIMIT * (row_count * shards * subs + prior_weight)
    rate = code_rate(math.ceil(math.log2(top)))
    slots = slot_ids.reshape(blocks, SLOT)
    chips = near_group(subs, shards)
    bits = late_bits(shards)
    late = 1 << len(bits)
    group = 2 if blocks % 2 == 0 else 1
    parts = [count for count in (blocks // 2, blocks // 3, blocks - blocks // 2 - blocks // 3) if count]
    limit = pltpu.CompilerParams(vmem_limit_bytes=8 * MIB + 4 * total * feat_width)
    smem = pl.BlockSpec(memory_space=pltpu.SMEM)
    vmem = pl.BlockSpec(memory_space=pltpu.VMEM)
    hbm = pl.BlockSpec(memory_space=pltpu.HBM)

    def swap(value, over_sub, over_shard):
        pairs = []
        for shard in range(shards):
            for sub in range(subs):
                pairs.append((shard * subs + sub, (shard ^ over_shard) * subs + (sub ^ over_sub)))
        return lax.ppermute(value, ("shard", "sub"), pairs)

    def in_hbm(value):
        return pltpu.with_memory_space_constraint(value, pltpu.HBM)

    shape = jax.ShapeDtypeStruct((len(chips), late, half_rows, width), jnp.float32)
    cost = pl.CostEstimate(flops=row_count * SLOT * feat_width, bytes_accessed=row_count * feat_width, transcendentals=0)
    sizes = dict(blocks=blocks, shards=shards, subs=subs, width=width)
    *send, held = pl.pallas_call(
        functools.partial(send_kernel, parts=parts, **sizes),
        out_shape=(shape, shape, jax.ShapeDtypeStruct(points.shape, points.dtype)),
        in_specs=[hbm] * 4,
        out_specs=(vmem, vmem, vmem),
        scratch_shapes=[
            pltpu.SMEM((1,), jnp.int32),
            pltpu.SMEM((blocks,), jnp.int32),
            pltpu.VMEM((blocks, SLOT), jnp.int32),
            pltpu.SemaphoreType.DMA((3,)),
            pltpu.SemaphoreType.DMA((len(parts),)),
        ],
        compiler_params=limit,
        cost_estimate=cost,
        name="sums_send",
    )(live_blocks, in_hbm(block_ids), in_hbm(slots), in_hbm(points))
    crossed = [swap(sums, 1, 0) for sums in send]
    keep = pl.pallas_call(
        functools.partial(keep_kernel, **sizes),
        out_shape=(shape, shape),
        in_specs=[smem, smem, vmem, vmem, vmem],
        out_specs=(vmem, vmem),
        compiler_params=limit,
        cost_estimate=cost,
        name="sums_keep",
    )(live_blocks, block_ids, slots, old_centroids, held)

    piece = (late, half_rows, width)
    two = (2, half_rows, width)

    def after(value, *others):
        return lax.optimization_barrier((value, *others))[0] if others else value

    def reduce_near(half, *earlier):
        there = after(crossed[half], *earlier)
        codes = [encode(keep[half][index] + there[index], rate) for index in range(1, len(chips))]
        return codes, [swap(code, *chip) for code, chip in zip(codes, chips[1:])]

    def reduce_late(half, terms, *earlier):
        mine, code = pl.pallas_call(
            functools.partial(mix_kernel, rate=rate),
            out_shape=(jax.ShapeDtypeStruct(piece, jnp.float32), jax.ShapeDtypeStruct(piece, jnp.int16)),
            compiler_params=limit,
            name=f"mix{half}",
        )(after(keep[half], *earlier), crossed[half], *terms)
        for bit in bits[:-1]:
            count = mine.shape[0] // 2
            mine = mine[:count] + decode(swap(encode(mine[count:], rate), 0, bit), rate)
            code = encode(mine, rate)
        return mine, swap(code, 0, bits[-1])

    def finish(half, mine, there, *earlier):
        own, code = pl.pallas_call(
            functools.partial(finish_kernel, rate=rate),
            out_shape=(
                jax.ShapeDtypeStruct((half_rows, width), jnp.float32),
                jax.ShapeDtypeStruct(two, jnp.int16),
            ),
            compiler_params=limit,
            name=f"finish{half}",
        )(after(mine, *earlier), there)
        for bit in reversed(bits[:-1]):
            code = jnp.concatenate([code, swap(code, 0, bit)])
        return own, code

    def rows_of(half, own, near, far):
        return pl.pallas_call(
            functools.partial(
                rows_kernel, shards=shards, subs=subs, rows=rows, width=width, rate=rate
            ),
            out_shape=(
                jax.ShapeDtypeStruct((half_rows, width), jnp.bfloat16),
                jax.ShapeDtypeStruct((total // 2, feat_width), jnp.bfloat16),
            ),
            compiler_params=limit,
            name=f"rows{half}",
        )(own, *near, *far)

    def scores(half, last, cents, *earlier):
        line = jax.ShapeDtypeStruct((blocks, SLOT), jnp.float32)
        fresh = jax.ShapeDtypeStruct((rows, width), jnp.bfloat16)
        return pl.pallas_call(
            functools.partial(
                score_kernel, half=half, last=last, blocks=blocks, shards=shards, rows=rows, group=group
            ),
            out_shape=(fresh, line) if last else (line, line),
            in_specs=[smem] + [vmem] * (3 + len(earlier)),
            out_specs=(vmem, vmem),
            compiler_params=limit,
            cost_estimate=pl.CostEstimate(
                flops=row_count * total * feat_width,
                bytes_accessed=2 * row_count * feat_width,
                transcendentals=0,
            ),
            name=f"scores{half}",
        )(block_ids, slots, held, cents, *earlier)

    first_codes, first_terms = reduce_near(0)
    _, second_terms = reduce_near(1, *first_codes)
    first = reduce_late(0, first_terms)
    second = reduce_late(1, second_terms, first[0])
    first_own, first_code = finish(0, *first)
    second_own, second_code = finish(1, *second, first_code)
    own, codes = (first_own, second_own), (first_code, second_code)
    near = jnp.concatenate([codes[0], swap(codes[0], 0, 1)])
    near = [jnp.concatenate([near, swap(near, 2, 0)])]
    blocks_near = [codes[1]] + [swap(codes[1], *chip) for chip in chips[1:]]
    second_fresh, second_rows = rows_of(1, own[1], blocks_near, [swap(block, 1, 0) for block in blocks_near])
    mine, rival = scores(1, False, second_rows)
    first_near = after(near[0], second_fresh)
    first_fresh, first_rows = rows_of(0, own[0], [first_near], [swap(first_near, 1, 0)])
    fresh, margin = scores(0, True, first_rows, mine, rival, first_fresh, second_fresh)
    return fresh, margin.reshape(row_count)


def solution(mesh):
    return jax.shard_map(
        local,
        mesh=mesh,
        in_specs=(
            P(("groups", "shard", "sub"), None),
            P(("groups", "shard", "sub")),
            P(("groups", "shard", "sub")),
            P(("groups", "shard", "sub")),
            P(("groups", "shard"), "sub"),
        ),
        out_specs=(P(("groups", "shard"), "sub"), P(("groups", "shard", "sub"))),
        check_vma=False,
    )
```
